512 devices in a mesh: row: 32 (over z, x), rep: 16 (over y, core).
Axes of the slice: x: 4, y: 8, z: 8, core: 2. Of those that a mesh axis runs over, the one named last changes fastest.
Arguments:
- features: bfloat16 [65536, 512], P(('row', 'rep')), may hold values from -24 to 24
- edge_weights: bfloat16 [65536, 16], P(('row', 'rep')), may hold values from 0.25 to 2
- neighbours: int32 [65536, 16], P(('row', 'rep')), may hold values from 0 to 4095, as said below
- send_list: int32 [32, 16, 16, 2], P('row', 'rep'), may hold values from 0 to 31, as said below
- send_count: int32 [32, 16, 16], P('row', 'rep'), may hold values from 0 to 2, as said below
- w_agg: bfloat16 [512, 512], replicated, may hold values from -0.25 to 0.25
- w_self: bfloat16 [512, 512], replicated, may hold values from -0.25 to 0.25
- cotangent: bfloat16 [65536, 512], P(('row', 'rep')), may hold values from -6 to 6
Outputs:
- hidden: bfloat16 [65536, 512], P(('row', 'rep'))
- grad_agg: float32 [512, 512], P('row')
- grad_self: float32 [512, 512], P('row')
The draws below stay inside these ranges and needn't reach their ends.
Inputs may be any that keep to these rules, and one draw needn't show every extreme that they name: The 16 codes of a node name 16 distinct neighbours, none the node itself. Codes of slots below 12 are below 4096; a code c of a later slot has c // 128 below the sum of send_count[o, s, g] over s for the node's owner index o and group g. `send_list`: entries of one (o, s, g) below its count are distinct positions of blocks in group s; entries at or past the count are unused. send_count[o, g, g] is 0. In every draw some device receives 2 blocks from every other group, and every device receives 2 from some group.
All inputs are finite; a program needn't handle non-finite values.
Results may differ from the reference program's by a relative error of at most 0.0051.
Values may be sent and summed in bfloat16 or wider, within the bound.
No kernel may reach another device: no remote copies, remote signals or barrier semaphores. Data moves between devices by JAX's collectives and lax.ppermute only.
A program may use at most 64 MiB of HBM per device.

```python
import math
import jax
import jax.numpy as jnp

F = 512
TILE = 128
K = 16
K_LOC = 12
CAP = 2
BD = 1
OWNERS = 32
GROUPS = 16
GBLK = 32
NODES = 65536


def counts_table(key):
    first, second, third = jax.random.split(key, 3)
    table = jax.random.randint(first, (OWNERS, GROUPS, GROUPS), 0, CAP + 1)
    source = jnp.arange(GROUPS)[None, :, None]
    target = jnp.arange(GROUPS)[None, None, :]
    chosen = (target + jax.random.randint(second, (OWNERS, 1, GROUPS), 1, GROUPS)) % GROUPS
    table = jnp.where(source == chosen, CAP, table)
    loaded = jax.random.randint(third, (), 0, OWNERS * GROUPS)
    receiver = jnp.arange(OWNERS)[:, None, None] * GROUPS + target
    table = jnp.where(receiver == loaded, CAP, table)
    table = jnp.where(source == target, 0, table)
    return table.astype(jnp.int32)


def draw_send_count(key, part):
    return counts_table(key)


def draw_send_list(key, part):
    key = jax.random.fold_in(key, 2)
    start = jax.random.randint(key, (OWNERS, GROUPS, GROUPS, 1), 0, GBLK)
    return ((start + jnp.arange(CAP)[None, None, None, :]) % GBLK).astype(jnp.int32)


def draw_neighbours(key, part):
    table = counts_table(key)
    key = jax.random.fold_in(key, 3)
    totals = jnp.sum(table, axis=1)
    first, second, third = jax.random.split(key, 3)
    shape_all = (OWNERS, GROUPS, BD * TILE, K)
    local_pick = jax.random.randint(first, shape_all, 0, GBLK)
    remote_pick = jax.random.randint(second, shape_all, 0, 1048576) % totals[:, :, None, None]
    spacing = (TILE - 1) // K
    offsets = 1 + jnp.arange(K)[None, None, None, :] * spacing + jax.random.randint(third, shape_all, 0, spacing)
    within = jnp.arange(BD * TILE)[None, None, :, None] % TILE
    rows_in = (within + offsets) % TILE
    is_local = jnp.arange(K)[None, None, None, :] < K_LOC
    codes = jnp.where(is_local, local_pick, remote_pick) * TILE + rows_in
    return codes.reshape(NODES, K).astype(jnp.int32)


def spiked(array, rng, source, target, shards_of, factor):
    def block_of(dim):
        return (jnp.arange(array.shape[dim]) // (array.shape[dim] // shards_of)).reshape((-1,) + (1,) * (array.ndim - 1 - dim))

    one_side = jax.random.permutation(rng, shards_of)[block_of(target)]
    other_side = (block_of(target) + shards_of // 2) % shards_of
    return jnp.where((block_of(source) == one_side) | (block_of(source) == other_side), factor * array, array)


def shard_levels(rng, shape, cuts, smallest, largest):
    def one(dim, parts):
        heights = jax.random.uniform(jax.random.fold_in(jax.random.fold_in(rng, 6), dim), (parts,), jnp.float32, smallest / len(cuts), largest / len(cuts))
        return jnp.repeat(jnp.exp(heights), shape[dim] // parts).reshape((-1,) + (1,) * (len(shape) - dim - 1))

    loudness = one(*cuts[0])
    for cut in cuts[1:]:
        loudness = loudness * one(*cut)
    return loudness


def gaussian(key, extent, deviation, most, cuts=(), held_as=jnp.bfloat16):
    array = jax.random.normal(key, extent, jnp.float32) * deviation
    if len(cuts) > 0:
        array = shard_levels(key, extent, cuts, -0.22, 0.18) * array
    return jnp.clip(array, min=-most, max=most).astype(held_as)


def noise_with(rng, extent, scale, reach, cuts, heavy, kind=jnp.bfloat16):
    values = scale * jax.random.normal(rng, extent, jnp.float32)
    if cuts:
        values = values * shard_levels(rng, extent, cuts, -0.22, 0.18)
    return jnp.clip(spiked(values, jax.random.fold_in(rng, 3), *heavy), -reach, reach).astype(kind)


def setup_inputs(seed: int = 0) -> dict:
    keys = jax.random.split(jax.random.key(seed), 9)
    features = noise_with(keys[0], (NODES, F), 1.0, 24.0, ((0, 512),), (0, 1, 512, 6.0))
    edge_weights = jnp.clip(jnp.exp(math.log(2.0) - 2.0794415 * jax.random.uniform(keys[1], (NODES, K), jnp.float32) ** shard_levels(keys[1], (NODES, K), ((0, 512),), -0.2, 0.2)), 0.25, 2.0).astype(jnp.bfloat16)
    neighbours = draw_neighbours(jax.random.fold_in(keys[8], 71), 0)
    send_list = draw_send_list(jax.random.fold_in(keys[8], 71), 0)
    send_count = draw_send_count(jax.random.fold_in(keys[8], 71), 0)
    w_agg = gaussian(keys[5], (F, F), F ** -0.5, 0.25)
    w_self = gaussian(keys[6], (F, F), F ** -0.5, 0.25)
    cotangent = gaussian(keys[7], (NODES, F), 1.0, 6.0, ((0, 512),))
    return dict(features=features, edge_weights=edge_weights, neighbours=neighbours, send_list=send_list, send_count=send_count, w_agg=w_agg, w_self=w_self, cotangent=cotangent)


def block_of(group_ids, position):
    return ((position // BD) * GROUPS + group_ids) * BD + position % BD


def reference(features, edge_weights, neighbours, send_list, send_count, w_agg, w_self, cotangent):
    codes = neighbours.reshape(OWNERS, GROUPS, BD * TILE, K)
    group_ids = jnp.arange(GROUPS, dtype=jnp.int32)[None, :, None, None]
    local_codes = codes[..., :K_LOC]
    local_nodes = block_of(group_ids, local_codes // TILE) * TILE + local_codes % TILE
    remote_codes = codes[..., K_LOC:]
    slot_index = remote_codes // TILE
    counts = jnp.transpose(send_count, (0, 2, 1))
    inclusive = jnp.cumsum(counts, axis=2).astype(jnp.int32)
    exclusive = (inclusive - counts).astype(jnp.int32)
    source = jnp.sum((inclusive[:, :, None, None, :] <= slot_index[..., None]).astype(jnp.int32), axis=-1).astype(jnp.int32)
    shape_rem = source.shape
    start_of = jnp.take_along_axis(exclusive, source.reshape(OWNERS, GROUPS, -1), axis=2).reshape(shape_rem)
    entry = slot_index - start_of
    lists = jnp.transpose(send_list, (0, 2, 1, 3)).reshape(OWNERS, GROUPS, GROUPS * CAP)
    position = jnp.take_along_axis(lists, (source * CAP + entry).reshape(OWNERS, GROUPS, -1).astype(jnp.int32), axis=2).reshape(shape_rem)
    remote_nodes = block_of(source, position) * TILE + remote_codes % TILE
    global_ids = jnp.concatenate([local_nodes, remote_nodes], axis=-1).reshape(NODES, K).astype(jnp.int32)
    dense = features.astype(jnp.float32)
    weights = edge_weights.astype(jnp.float32)
    summed = dense
    for slot in range(K):
        summed = summed + weights[:, slot:slot + 1] * jnp.take(dense, global_ids[:, slot], axis=0)
    degree = 1.0 + jnp.sum(weights, axis=1)
    aggregate = (summed / degree[:, None]).astype(jnp.bfloat16)
    preact = jnp.dot(aggregate, w_agg, preferred_element_type=jnp.float32) + jnp.dot(features, w_self, preferred_element_type=jnp.float32)
    hidden = jax.nn.silu(preact).astype(jnp.bfloat16)
    sigma = jax.nn.sigmoid(preact)
    grad_pre = (cotangent.astype(jnp.float32) * sigma * (1.0 + preact * (1.0 - sigma))).astype(jnp.bfloat16)
    grad_agg = jnp.dot(aggregate.T, grad_pre, preferred_element_type=jnp.float32)
    grad_self = jnp.dot(features.T, grad_pre, preferred_element_type=jnp.float32)
    return hidden, grad_agg, grad_self
```

```python
import jax
import jax.numpy as jnp
from jax import lax
from jax.experimental import pallas as pl
from jax.experimental.pallas import tpu as pltpu
from jax.sharding import Mesh, PartitionSpec as P

NZ, NX, NY, NC = 8, 4, 8, 2
OWNERS = NZ * NX
GROUPS = NY * NC
T = 128
K_LOC = 12
K_REM = 4
CAP = 2
F32 = jnp.float32
BF16 = jnp.bfloat16
VMEM_LIMIT = 48 * 1024 * 1024


def build_kernel(scalars, local_ref, remote_ref, remote_hot, local_hot):
    g = pl.program_id(0)
    own_z = scalars[2 * NX * GROUPS]
    rows = lax.broadcasted_iota(jnp.int32, (T, T), 0).astype(F32)
    lanes = lax.broadcasted_iota(jnp.int32, (1, T), 1).astype(F32)
    for x in range(NX):
        start = scalars[x * GROUPS + g]
        count = scalars[NX * GROUPS + x * GROUPS + g]
        relative = remote_ref[0, x, 0:K_REM, :] - (start * T).astype(F32)
        relative = jnp.where(relative < (count * T).astype(F32), relative, -1.0)
        weight = remote_ref[0, x, K_REM : 2 * K_REM, :]
        for m in range(CAP):
            hot = jnp.zeros((T, T), F32)
            for k in range(K_REM):
                hot = jnp.where(rows == relative[k : k + 1] - float(m * T), weight[k : k + 1], hot)
            remote_hot[0, x, m * T : (m + 1) * T, :] = hot.astype(BF16)
    for q in range(2):
        p = 2 * g + q
        for x in range(NX):
            code = local_ref[x, 0:K_LOC, :] - (p * T).astype(F32)
            weight = local_ref[x, K_LOC : 2 * K_LOC, :]
            own = lanes - jnp.where(p == own_z * NX + x, 0.0, 1024.0)
            hot = jnp.where(rows == own, 1.0, 0.0)
            for k in range(K_LOC):
                hot = jnp.where(rows == code[k : k + 1], weight[k : k + 1], hot)
            local_hot[q * T : (q + 1) * T, x * T : (x + 1) * T] = hot.astype(BF16)


def build(scalars, local_data, remote_data):
    return pl.pallas_call(
        build_kernel,
        grid_spec=pltpu.PrefetchScalarGridSpec(
            num_scalar_prefetch=1,
            grid=(GROUPS,),
            in_specs=[
                pl.BlockSpec((NX, 40, T), lambda g, s: (0, 0, 0)),
                pl.BlockSpec((1, NX, 16, T), lambda g, s: (g, 0, 0, 0)),
            ],
            out_specs=[
                pl.BlockSpec((1, NX, CAP * T, T), lambda g, s: (g, 0, 0, 0)),
                pl.BlockSpec((2 * T, NX * T), lambda g, s: (g, 0)),
            ],
        ),
        out_shape=[
            jax.ShapeDtypeStruct((GROUPS, NX, CAP * T, T), BF16),
            jax.ShapeDtypeStruct((OWNERS * T, NX * T), BF16),
        ],
        compiler_params=pltpu.CompilerParams(vmem_limit_bytes=VMEM_LIMIT),
        cost_estimate=pl.CostEstimate(flops=200_000_000, bytes_accessed=10_000_000, transcendentals=0),
        name="build_hot",
    )(scalars, local_data, remote_data)


def partial_kernel(scalars, blocks_ref, remote_hot, local_hot, send_ref, keep_ref, total):
    i = pl.program_id(0)
    own_y = scalars[0]
    own_c = scalars[1]
    y = lax.rem(own_y + 1 + i, NY)

    @pl.when(i == 0)
    def _():
        total[...] = jnp.zeros_like(total)

    part = total[...]
    for j in range(2):
        pair = jnp.concatenate([blocks_ref[4 * i + 2 * j], blocks_ref[4 * i + 2 * j + 1]], axis=1)
        part = part + jnp.dot(pair, local_hot[2 * T * j : 2 * T * (j + 1), :], preferred_element_type=F32)
    total[...] = part

    def product(core, x):
        at = 2 + ((x * NY + y) * NC + core) * CAP
        first = jnp.clip(scalars[at], 0, OWNERS - 1)
        second = jnp.clip(scalars[at + 1], 0, OWNERS - 1)
        pair = jnp.concatenate([blocks_ref[first], blocks_ref[second]], axis=1)
        return jnp.dot(pair, remote_hot[0, core, x], preferred_element_type=F32)

    for x in range(NX):
        send_ref[x, 0] = product(1 - own_c, x).astype(BF16)
    last = jnp.where(i == NY - 1, 1.0, 0.0)
    for x in range(NX):
        keep_ref[x, 0] = (product(own_c, x) + last * total[:, x * T : (x + 1) * T]).astype(BF16)


def partials(scalars, blocks, remote_hot, local_hot):
    def turn(i, s):
        return lax.rem(s[0] + 1 + i, NY)

    shape = jax.ShapeDtypeStruct((NX, NY, T, T), BF16)
    return pl.pallas_call(
        partial_kernel,
        grid_spec=pltpu.PrefetchScalarGridSpec(
            num_scalar_prefetch=1,
            grid=(NY,),
            in_specs=[
                pl.BlockSpec((OWNERS, T, T), lambda i, s: (0, 0, 0)),
                pl.BlockSpec((1, NC, NX, CAP * T, T), lambda i, s: (turn(i, s), 0, 0, 0, 0)),
                pl.BlockSpec((4 * T, NX * T), lambda i, s: (i, 0)),
            ],
            out_specs=[
                pl.BlockSpec((NX, 1, T, T), lambda i, s: (0, turn(i, s), 0, 0)),
                pl.BlockSpec((NX, 1, T, T), lambda i, s: (0, turn(i, s), 0, 0)),
            ],
            scratch_shapes=[pltpu.VMEM((T, NX * T), F32)],
        ),
        out_shape=[shape, shape],
        compiler_params=pltpu.CompilerParams(vmem_limit_bytes=VMEM_LIMIT),
        cost_estimate=pl.CostEstimate(flops=1_000_000_000, bytes_accessed=11_000_000, transcendentals=0),
        name="partial_sums",
    )(scalars, blocks, remote_hot, local_hot)


def dense_kernel(scalars, arrived, weights_t, features, features_t, w_agg, w_self, cotangent, hidden_ref, send_ref, keep_ref, agg_t):
    own_c = scalars[0]
    degree = 1.0 + jnp.sum(weights_t[...], axis=0, keepdims=True)
    for x in range(NX):
        summed = arrived[x, 0].astype(F32)
        for y in range(1, NY):
            summed = summed + arrived[x, y].astype(F32)
        agg_t[x * T : (x + 1) * T, :] = (summed / degree).astype(BF16)
    contract = (((0,), (0,)), ((), ()))
    preact = lax.dot_general(agg_t[...], w_agg[...], contract, preferred_element_type=F32) + jnp.dot(
        features[...], w_self[...], preferred_element_type=F32
    )
    sigma = jax.nn.sigmoid(preact)
    hidden_ref[...] = (preact * sigma).astype(BF16)
    grad_pre = (cotangent[...].astype(F32) * sigma * (1.0 + preact * (1.0 - sigma))).astype(BF16)
    of_agg = jnp.dot(agg_t[...], grad_pre, preferred_element_type=F32)
    of_self = jnp.dot(features_t[...], grad_pre, preferred_element_type=F32)

    @pl.when(own_c == 0)
    def _():
        keep_ref[...] = of_agg
        send_ref[...] = of_self

    @pl.when(own_c != 0)
    def _():
        keep_ref[...] = of_self
        send_ref[...] = of_agg


def dense(scalars, *operands):
    width = NX * T
    vmem = pl.BlockSpec(memory_space=pltpu.VMEM)
    return pl.pallas_call(
        dense_kernel,
        in_specs=[pl.BlockSpec(memory_space=pltpu.SMEM)] + [vmem] * 7,
        out_specs=[vmem] * 3,
        out_shape=[
            jax.ShapeDtypeStruct((T, width), BF16),
            jax.ShapeDtypeStruct((width, width), F32),
            jax.ShapeDtypeStruct((width, width), F32),
        ],
        scratch_shapes=[pltpu.VMEM((width, T), BF16)],
        compiler_params=pltpu.CompilerParams(vmem_limit_bytes=VMEM_LIMIT),
        cost_estimate=pl.CostEstimate(flops=300_000_000, bytes_accessed=5_000_000, transcendentals=65536),
        name="dense",
    )(scalars, *operands)


def body(features, edge_weights, neighbours, send_list, send_count, w_agg, w_self, cotangent):
    width = features.shape[1]
    z, x, y, c = (lax.axis_index(a).astype(jnp.int32) for a in ("z", "x", "y", "c"))
    swap = [(0, 1), (1, 0)]

    features_t = features.T
    quarters = jnp.broadcast_to(features_t.reshape(1, NX, T, T), (NZ, NX, T, T)).reshape(OWNERS, T, T)
    blocks = lax.all_to_all(quarters, ("z", "x"), 0, 0, tiled=True)

    codes_t = neighbours.T.astype(F32)
    weights_t = edge_weights.T.astype(F32)
    counted = jnp.pad(send_count[0].astype(F32), ((0, 0), (0, T - GROUPS)))
    listed = jnp.pad(send_list[0].reshape(1, GROUPS * CAP).astype(F32), ((0, 0), (0, T - GROUPS * CAP)))
    small = jnp.concatenate(
        [codes_t[:K_LOC], weights_t[:K_LOC], codes_t[K_LOC:], weights_t[K_LOC:], counted, listed, jnp.zeros((6, T), F32)], axis=0
    )
    along_x = lax.all_gather(small, "x", axis=0)
    everyone = lax.all_gather(along_x[:, 24:40], ("y", "c"), axis=0)

    group = y * NC + c
    counts = everyone[:, :, 8, :GROUPS].astype(jnp.int32)
    sources = jnp.arange(GROUPS, dtype=jnp.int32)[:, None, None]
    start = jnp.sum(jnp.where(sources < group, counts, 0), axis=0)
    here = jnp.sum(jnp.where(sources == group, counts, 0), axis=0)
    build_scalars = jnp.concatenate([start.reshape(-1), here.reshape(-1), z[None]])
    remote_hot, local_hot = build(build_scalars, along_x, everyone)
    lists = along_x[:, 33, : GROUPS * CAP].astype(jnp.int32)
    partial_scalars = jnp.concatenate([y[None], c[None], lists.reshape(-1)])

    send, keep = partials(partial_scalars, blocks, remote_hot.reshape(NY, NC, NX, CAP * T, T), local_hot)
    received = lax.ppermute(send, "c", swap)
    chip_sum = (keep.astype(F32) + received.astype(F32)).astype(BF16)
    arrived = lax.all_to_all(chip_sum.reshape(NX * NY, T, T), ("x", "y"), 0, 0, tiled=True)

    hidden, send, keep = dense(
        c[None], arrived.reshape(NX, NY, T, T), weights_t, features, features_t, w_agg, w_self, cotangent
    )
    received = lax.ppermute(send, "c", swap)
    share = width // OWNERS
    chip_grad = (keep + received).astype(BF16).reshape(OWNERS, share, width)
    rows = lax.all_to_all(chip_grad, ("z", "x"), 0, 0, tiled=True)
    plane = jnp.sum(rows.astype(F32), axis=0)
    both = lax.all_gather(plane, ("y", "c"), axis=0).reshape(NY, NC, share, width)
    grads = jnp.sum(both, axis=0)
    return hidden, grads[0], grads[1]


def solution(mesh):
    fine = Mesh(mesh.devices.reshape(NZ, NX, NY, NC), ("z", "x", "y", "c"))
    row, rep = ("z", "x"), ("y", "c")
    nodes = P(row + rep, None)
    in_specs = (nodes, nodes, nodes, P(row, rep, None, None), P(row, rep, None), P(), P(), nodes)
    out_specs = (nodes, P(row, None), P(row, None))
    return jax.shard_map(body, mesh=fine, in_specs=in_specs, out_specs=out_specs, check_vma=False)
```

```python
import jax
import jax.numpy as jnp
from jax import lax
from jax.experimental import pallas as pl
from jax.experimental.pallas import tpu as pltpu
from jax.sharding import Mesh, PartitionSpec as P

NZ, NX, NY, NC = 8, 4, 8, 2
OWNERS = NZ * NX
GROUPS = NY * NC
T = 128
K_LOC = 12
K_REM = 4
CAP = 2
F32 = jnp.float32
BF16 = jnp.bfloat16
VMEM_LIMIT = 16 * 1024 * 1024


def vmem_call(kernel, name, scalar_inputs, array_inputs, outputs, scratch=(), flops=0, bytes_accessed=0, transcendentals=0):
    vmem = pl.BlockSpec(memory_space=pltpu.VMEM)
    return pl.pallas_call(
        kernel,
        in_specs=[pl.BlockSpec(memory_space=pltpu.SMEM)] * len(scalar_inputs) + [vmem] * len(array_inputs),
        out_specs=[vmem] * len(outputs),
        out_shape=[jax.ShapeDtypeStruct(shape, dtype) for shape, dtype in outputs],
        scratch_shapes=list(scratch),
        compiler_params=pltpu.CompilerParams(vmem_limit_bytes=VMEM_LIMIT),
        cost_estimate=pl.CostEstimate(flops=flops, bytes_accessed=bytes_accessed, transcendentals=transcendentals),
        name=name,
    )(*scalar_inputs, *array_inputs)


def remote_kernel(scalars, blocks_ref, remote_ref, sums_ref):
    core = scalars[0]
    rows = lax.broadcasted_iota(jnp.int32, (T, T), 0).astype(F32)

    def product(x, y):
        at = x * GROUPS + y * NC + core
        first = jnp.clip(scalars[1 + at * CAP], 0, OWNERS - 1)
        second = jnp.clip(scalars[2 + at * CAP], 0, OWNERS - 1)
        start = scalars[1 + NX * GROUPS * CAP + at].astype(F32)
        count = scalars[1 + NX * GROUPS * (CAP + 1) + at].astype(F32)
        told = remote_ref[y * NC + core, x].astype(F32)
        entry = told[0:K_REM] - start
        row = jnp.where(entry < count, entry * T + told[K_REM : 2 * K_REM], -1.0)
        weight = told[2 * K_REM : 3 * K_REM]
        halves = []
        for m in range(CAP):
            hot = jnp.zeros((T, T), F32)
            for k in range(K_REM):
                hot = jnp.where(rows == row[k : k + 1] - float(m * T), weight[k : k + 1], hot)
            halves.append(hot.astype(BF16))
        pair = jnp.concatenate([blocks_ref[first], blocks_ref[second]], axis=1)
        return jnp.dot(pair, jnp.concatenate(halves, axis=0), preferred_element_type=F32).astype(BF16)

    def of_y(y, carry):
        for x in range(NX):
            sums_ref[x, y] = product(x, y)
        return carry

    lax.fori_loop(0, NY, of_y, 0)


def local_kernel(scalars, blocks_ref, local_ref, out_0, out_1, out_2, out_3, hot_ref, total):
    own_z, own_x = scalars[0], scalars[1]
    rows = lax.broadcasted_iota(jnp.int32, (T, T), 0).astype(F32)
    lanes = lax.broadcasted_iota(jnp.int32, (1, T), 1).astype(F32)
    total[...] = jnp.zeros_like(total)

    def of_four(i, carry):
        for j in range(4):
            p = 4 * i + j
            for x in range(NX):
                code = local_ref[x, 16 : 16 + K_LOC, :].astype(F32) - p.astype(F32)
                code = code * T + local_ref[x, 32 : 32 + K_LOC, :].astype(F32)
                weight = local_ref[x, 48 : 48 + K_LOC, :].astype(F32)
                own = lanes - jnp.where(p == own_z * NX + x, 0.0, 1024.0)
                hot = jnp.where(rows == own, 1.0, 0.0)
                for k in range(K_LOC):
                    hot = jnp.where(rows == code[k : k + 1], weight[k : k + 1], hot)
                hot_ref[x, j * T : (j + 1) * T, :] = hot.astype(BF16)
        four = jnp.concatenate([blocks_ref[4 * i + j] for j in range(4)], axis=1)
        for x in range(NX):
            total[x] += jnp.dot(four, hot_ref[x], preferred_element_type=F32)
        return carry

    lax.fori_loop(0, OWNERS // 4, of_four, 0)
    for k, out in enumerate((out_0, out_1, out_2, out_3)):
        out[...] = total[lax.rem(own_x + k, NX)]


def dense_kernel(scalars, arrived, near_0, near_1, near_2, near_3, weights_t, features, features_t, w_agg, w_self, cotangent, hidden_ref, send_ref, keep_ref, agg_t):
    own_c, own_x = scalars[0], scalars[1]
    degree = 1.0 + jnp.sum(weights_t[...], axis=0, keepdims=True)
    for k, near in enumerate((near_0, near_1, near_2, near_3)):
        quarter = lax.rem(own_x + (NX - k), NX)
        summed = near[...]
        for y in range(NY):
            summed = summed + arrived[quarter, y].astype(F32)
        agg_t[pl.ds(pl.multiple_of(quarter * T, T), T), :] = (summed / degree).astype(BF16)
    contract = (((0,), (0,)), ((), ()))
    preact = lax.dot_general(agg_t[...], w_agg[...], contract, preferred_element_type=F32) + jnp.dot(
        features[...], w_self[...], preferred_element_type=F32
    )
    sigma = jax.nn.sigmoid(preact)
    hidden_ref[...] = (preact * sigma).astype(BF16)
    grad_pre = (cotangent[...].astype(F32) * sigma * (1.0 + preact * (1.0 - sigma))).astype(BF16)
    of_agg = jnp.dot(agg_t[...], grad_pre, preferred_element_type=F32)
    of_self = jnp.dot(features_t[...], grad_pre, preferred_element_type=F32)

    @pl.when(own_c == 0)
    def _():
        keep_ref[...] = of_agg
        send_ref[...] = of_self

    @pl.when(own_c != 0)
    def _():
        keep_ref[...] = of_self
        send_ref[...] = of_agg


def add_kernel(parts_ref, sum_ref):
    summed = parts_ref[0].astype(F32)
    for i in range(1, OWNERS):
        summed = summed + parts_ref[i].astype(F32)
    sum_ref[...] = summed


def body(features, edge_weights, neighbours, send_list, send_count, w_agg, w_self, cotangent):
    width = features.shape[1]
    z, x, y, c = (lax.axis_index(a).astype(jnp.int32) for a in ("z", "x", "y", "c"))
    swap = [(0, 1), (1, 0)]

    features_t = features.T
    quarters = jnp.broadcast_to(features_t.reshape(1, NX, T, T), (NZ, NX, T, T)).reshape(OWNERS, T, T)
    blocks = lax.all_to_all(quarters, ("z", "x"), 0, 0, tiled=True)

    codes_t = neighbours.T
    weights_t = edge_weights.T
    told = jnp.concatenate([send_count[0], send_list[0].reshape(1, GROUPS * CAP)], axis=1).astype(BF16)
    told = jnp.pad(told, ((0, 3), (0, T - GROUPS * (1 + CAP))))
    block, row = (codes_t // T).astype(BF16), (codes_t % T).astype(BF16)
    gap = jnp.zeros((16 - K_LOC, T), BF16)
    parts = [block[K_LOC:], row[K_LOC:], weights_t[K_LOC:], told]
    parts += [block[:K_LOC], gap, row[:K_LOC], gap, weights_t[:K_LOC], gap]
    along_x = lax.all_gather(jnp.concatenate(parts, axis=0), "x", axis=0)
    remote_data = lax.all_gather(along_x[:, :16], ("y", "c"), axis=0)
    told = remote_data[:, :, 12].astype(jnp.int32)
    sources = jnp.arange(GROUPS, dtype=jnp.int32)[:, None, None]
    group = y * NC + c
    here = jnp.sum(jnp.where(sources == group, told, 0), axis=0)
    start = jnp.sum(jnp.where(sources < group, told[:, :, :GROUPS], 0), axis=0)
    lists = here[:, GROUPS : GROUPS * (1 + CAP)]
    scalars = jnp.concatenate([lists.reshape(-1), start.reshape(-1), here[:, :GROUPS].reshape(-1)])

    def remote_sums(core, blocks):
        (sums,) = vmem_call(
            remote_kernel, "remote_sums", [jnp.concatenate([core[None], scalars])], [blocks, remote_data],
            [((NX, NY, T, T), BF16)], flops=300_000_000, bytes_accessed=2_500_000,
        )
        return sums

    received = lax.ppermute(remote_sums(1 - c, blocks), "c", swap)
    keep = remote_sums(c, blocks)
    chip_sum = (keep.astype(F32) + received.astype(F32)).astype(BF16)
    arrived = lax.all_to_all(chip_sum.reshape(NX * NY, T, T), ("x", "y"), 0, 0, tiled=True)

    near = vmem_call(
        local_kernel, "local_sums", [jnp.stack([z, x])], [blocks, along_x], [((T, T), F32)] * NX,
        scratch=[pltpu.VMEM((NX, 4 * T, T), BF16), pltpu.VMEM((NX, T, T), F32)],
        flops=600_000_000, bytes_accessed=1_500_000,
    )
    near = [near[0]] + [lax.ppermute(near[k], "x", [(i, (i + k) % NX) for i in range(NX)]) for k in range(1, NX)]

    hidden, send, keep = vmem_call(
        dense_kernel, "dense", [jnp.stack([c, x])],
        [arrived.reshape(NX, NY, T, T), *near, weights_t.astype(F32), features, features_t, w_agg, w_self, cotangent],
        [((T, width), BF16), ((width, width), F32), ((width, width), F32)],
        scratch=[pltpu.VMEM((width, T), BF16)], flops=300_000_000, bytes_accessed=5_000_000, transcendentals=65536,
    )
    received = lax.ppermute(send, "c", swap)
    share = width // OWNERS
    chip_grad = (keep + received).astype(BF16).reshape(OWNERS, share, width)
    rows = lax.all_to_all(chip_grad, ("z", "x"), 0, 0, tiled=True)
    (plane,) = vmem_call(add_kernel, "add_rows", [], [rows], [((share, width), F32)], flops=300_000, bytes_accessed=550_000)
    both = lax.all_gather(plane, ("y", "c"), axis=0).reshape(NY, NC, share, width)
    grads = jnp.sum(both, axis=0)
    return hidden, grads[0], grads[1]


def solution(mesh):
    fine = Mesh(mesh.devices.reshape(NZ, NX, NY, NC), ("z", "x", "y", "c"))
    row, rep = ("z", "x"), ("y", "c")
    nodes = P(row + rep, None)
    in_specs = (nodes, nodes, nodes, P(row, rep, None, None), P(row, rep, None), P(), P(), nodes)
    out_specs = (nodes, P(row, None), P(row, None))
    return jax.shard_map(body, mesh=fine, in_specs=in_specs, out_specs=out_specs, check_vma=False)
```

```python
import jax
import jax.numpy as jnp
from jax import lax
from jax.experimental import pallas as pl
from jax.experimental.pallas import tpu as pltpu
from jax.sharding import Mesh, PartitionSpec as P

NZ, NX, NY, NC = 8, 4, 8, 2
OWNERS = NZ * NX
GROUPS = NY * NC
T = 128
K_LOC = 12
K_REM = 4
CAP = 2
TOLD = 16
F32 = jnp.float32
BF16 = jnp.bfloat16
VMEM_LIMIT = 16 * 1024 * 1024


def vmem_call(
    kernel, name, scalar_inputs, array_inputs, outputs, scratch=(), anywhere=(), flops=0, bytes_accessed=0, transcendentals=0
):
    vmem = pl.BlockSpec(memory_space=pltpu.VMEM)
    return pl.pallas_call(
        kernel,
        in_specs=[pl.BlockSpec(memory_space=pltpu.SMEM)] * len(scalar_inputs)
        + [pl.BlockSpec(memory_space=pl.ANY)] * len(anywhere)
        + [vmem] * len(array_inputs),
        out_specs=[vmem] * len(outputs),
        out_shape=[jax.ShapeDtypeStruct(shape, dtype) for shape, dtype in outputs],
        scratch_shapes=list(scratch),
        compiler_params=pltpu.CompilerParams(vmem_limit_bytes=VMEM_LIMIT),
        cost_estimate=pl.CostEstimate(flops=flops, bytes_accessed=bytes_accessed, transcendentals=transcendentals),
        name=name,
    )(*scalar_inputs, *anywhere, *array_inputs)


def spread_kernel(features_ref, quarters_ref, features_t, sems):
    features_t[...] = features_ref[...].astype(F32).T.astype(BF16).reshape(NX, T, T)
    copies = [pltpu.make_async_copy(features_t, quarters_ref.at[z], sems.at[z]) for z in range(NZ)]
    for copy in copies:
        copy.start()
    for copy in copies:
        copy.wait()


def spread(features):
    vmem, anywhere = pl.BlockSpec(memory_space=pltpu.VMEM), pl.BlockSpec(memory_space=pl.ANY)
    return pl.pallas_call(
        spread_kernel,
        in_specs=[vmem],
        out_specs=[anywhere, vmem],
        out_shape=[jax.ShapeDtypeStruct((NZ, NX, T, T), BF16), jax.ShapeDtypeStruct((NX, T, T), BF16)],
        scratch_shapes=[pltpu.SemaphoreType.DMA((NZ,))],
        compiler_params=pltpu.CompilerParams(vmem_limit_bytes=VMEM_LIMIT),
        name="spread",
    )(features)


def remote_kernel(scalars, blocks_ref, told_ref, sums_ref):
    core = scalars[0]
    rows = lax.broadcasted_iota(jnp.int16, (CAP * T, T), 0)

    def product(x, y):
        group = y * NC + core
        at = x * GROUPS + group
        first = jnp.clip(scalars[1 + at * CAP], 0, OWNERS - 1)
        second = jnp.clip(scalars[2 + at * CAP], 0, OWNERS - 1)
        start = scalars[1 + NX * GROUPS * CAP + at].astype(F32)
        count = scalars[1 + NX * GROUPS * (CAP + 1) + at].astype(F32)
        told = told_ref[x, pl.ds(pl.multiple_of(group * TOLD, TOLD), TOLD), :].astype(F32)
        entry = told[0:K_REM] - start
        row = jnp.where(entry < count, entry * T + told[K_REM : 2 * K_REM], -1.0).astype(jnp.int16)
        weight = told[2 * K_REM : 3 * K_REM].astype(BF16)
        hot = jnp.zeros((CAP * T, T), BF16)
        for k in range(K_REM):
            hot = jnp.where(rows == row[k : k + 1], weight[k : k + 1], hot)
        pair = jnp.concatenate([blocks_ref[first], blocks_ref[second]], axis=1)
        return jnp.dot(pair, hot, preferred_element_type=F32).astype(BF16)

    def of_y(y, carry):
        for x in range(NX):
            sums_ref[x, y] = product(x, y)
        return carry

    lax.fori_loop(0, NY, of_y, 0, unroll=True)


def local_kernel(scalars, blocks_ref, told_ref, out_0, out_1, out_2, out_3, hot_ref, total):
    own_z, own_x = scalars[0], scalars[1]
    rows = lax.broadcasted_iota(jnp.int16, (T, T), 0)
    lanes = lax.broadcasted_iota(jnp.int32, (1, T), 1).astype(F32)
    ones, zeros = jnp.ones((T, T), BF16), jnp.zeros((T, T), BF16)
    total[...] = jnp.zeros_like(total)

    def of_four(i, carry):
        for j in range(4):
            p = 4 * i + j
            for x in range(NX):
                block, row, weight = (
                    told_ref[x, GROUPS * TOLD + n * 16 : GROUPS * TOLD + n * 16 + 16, :].astype(F32) for n in range(3)
                )
                code = ((block - p.astype(F32)) * T + row).astype(jnp.int16)
                weight = weight.astype(BF16)
                own = (lanes - jnp.where(p == own_z * NX + x, 0.0, 1024.0)).astype(jnp.int16)
                hot = jnp.where(rows == own, ones, zeros)
                for k in range(K_LOC):
                    hot = jnp.where(rows == code[k : k + 1], weight[k : k + 1], hot)
                hot_ref[x, j * T : (j + 1) * T, :] = hot
        four = jnp.concatenate([blocks_ref[4 * i + j] for j in range(4)], axis=1)
        for x in range(NX):
            total[x] += jnp.dot(four, hot_ref[x], preferred_element_type=F32)
        return carry

    lax.fori_loop(0, OWNERS // 4, of_four, 0, unroll=2)
    for k, out in enumerate((out_0, out_1, out_2, out_3)):
        out[...] = total[lax.rem(own_x + k, NX)]


def dense_kernel(scalars, near_0, arrived, near_1, near_2, near_3, weights_t, features, features_t, w_agg, w_self, cotangent, hidden_ref, send_ref, keep_ref, agg_t, near, sem):
    own_c, own_x = scalars[0], scalars[1]
    degree = 1.0 + jnp.sum(weights_t[...], axis=0, keepdims=True)
    copy = pltpu.make_async_copy(near_0, near, sem)
    copy.start()

    def of_quarter(k, own):
        quarter = lax.rem(own_x + (NX - k), NX)
        summed = own[...]
        for y in range(NY):
            summed = summed + arrived[quarter, y].astype(F32)
        agg_t[pl.ds(pl.multiple_of(quarter * T, T), T), :] = (summed / degree).astype(BF16)

    of_quarter(1, near_1)
    of_quarter(2, near_2)
    of_quarter(3, near_3)
    copy.wait()
    of_quarter(0, near)
    contract = (((0,), (0,)), ((), ()))
    preact = lax.dot_general(agg_t[...], w_agg[...], contract, preferred_element_type=F32) + jnp.dot(
        features[...], w_self[...], preferred_element_type=F32
    )
    sigma = jax.nn.sigmoid(preact)
    hidden_ref[...] = (preact * sigma).astype(BF16)
    grad_pre = (cotangent[...].astype(F32) * sigma * (1.0 + preact * (1.0 - sigma))).astype(BF16)
    of_agg = jnp.dot(agg_t[...], grad_pre, preferred_element_type=F32)
    of_self = jnp.dot(features_t[...].reshape(NX * T, T), grad_pre, preferred_element_type=F32)

    @pl.when(own_c == 0)
    def _():
        keep_ref[...] = of_agg
        send_ref[...] = of_self.astype(BF16)

    @pl.when(own_c != 0)
    def _():
        keep_ref[...] = of_self
        send_ref[...] = of_agg.astype(BF16)


def add_kernel(parts_ref, sum_ref):
    summed = parts_ref[0].astype(F32)
    for i in range(1, parts_ref.shape[0]):
        summed = summed + parts_ref[i].astype(F32)
    sum_ref[...] = summed.astype(sum_ref.dtype)


def added(parts, dtype):
    (summed,) = vmem_call(
        add_kernel, "added", [], [parts], [(parts.shape[1:], dtype)], flops=parts.size, bytes_accessed=3 * parts.size
    )
    return summed


def body(features, edge_weights, neighbours, send_list, send_count, w_agg, w_self, cotangent):
    width = features.shape[1]
    z, x, y, c = (lax.axis_index(a).astype(jnp.int32) for a in ("z", "x", "y", "c"))
    swap = [(0, 1), (1, 0)]

    quarters, features_t = spread(features)
    blocks = lax.all_to_all(quarters.reshape(OWNERS, T, T), ("z", "x"), 0, 0, tiled=True)

    codes_t = neighbours.T
    weights_t = edge_weights.T
    told = jnp.concatenate([send_count[0], send_list[0].reshape(1, GROUPS * CAP)], axis=1).astype(BF16)
    told = jnp.pad(told, ((0, 3), (0, T - GROUPS * (1 + CAP))))
    block, row = (codes_t // T).astype(BF16), (codes_t % T).astype(BF16)
    of_remote = jnp.concatenate([block[K_LOC:], row[K_LOC:], weights_t[K_LOC:], told], axis=0)
    over_rep = lax.all_gather(of_remote, ("y", "c"), axis=0)
    gap = jnp.zeros((16 - K_LOC, T), BF16)
    of_both = [over_rep.reshape(GROUPS * TOLD, T), block[:K_LOC], gap, row[:K_LOC], gap, weights_t[:K_LOC], gap]
    over_all = lax.all_gather(jnp.concatenate(of_both, axis=0), "x", axis=0)
    told = over_all[:, : GROUPS * TOLD].reshape(NX, GROUPS, TOLD, T)[:, :, 12].astype(jnp.int32)
    sources = jnp.arange(GROUPS, dtype=jnp.int32)[None, :, None]
    group = y * NC + c
    here = jnp.sum(jnp.where(sources == group, told, 0), axis=1)
    start = jnp.sum(jnp.where(sources < group, told[:, :, :GROUPS], 0), axis=1)
    lists = here[:, GROUPS : GROUPS * (1 + CAP)]
    scalars = jnp.concatenate([lists.reshape(-1), start.reshape(-1), here[:, :GROUPS].reshape(-1)])

    def remote_sums(core, blocks):
        (sums,) = vmem_call(
            remote_kernel, "remote_sums", [jnp.concatenate([core[None], scalars])], [blocks, over_all],
            [((NX, NY, T, T), BF16)], flops=300_000_000, bytes_accessed=2_500_000,
        )
        return sums

    received = lax.ppermute(remote_sums(1 - c, blocks), "c", swap)
    keep = remote_sums(c, blocks)
    chip_sum = (keep.astype(F32) + received.astype(F32)).astype(BF16)
    arrived = lax.all_to_all(chip_sum.reshape(NX * NY, T, T), ("x", "y"), 0, 0, tiled=True)

    near = vmem_call(
        local_kernel, "local_sums", [jnp.stack([z, x])], [blocks, over_all], [((T, T), F32)] * NX,
        scratch=[pltpu.VMEM((NX, 4 * T, T), BF16), pltpu.VMEM((NX, T, T), F32)],
        flops=600_000_000, bytes_accessed=1_500_000,
    )
    moved = [lax.ppermute(near[k], "x", [(i, (i + k) % NX) for i in range(NX)]) for k in range(1, NX)]

    hidden, send, keep = vmem_call(
        dense_kernel, "dense", [jnp.stack([c, x])],
        [arrived.reshape(NX, NY, T, T), *moved, weights_t.astype(F32), features, features_t, w_agg, w_self, cotangent],
        [((T, width), BF16), ((width, width), BF16), ((width, width), F32)],
        scratch=[pltpu.VMEM((width, T), BF16), pltpu.VMEM((T, T), F32), pltpu.SemaphoreType.DMA], anywhere=[near[0]], flops=300_000_000, bytes_accessed=5_000_000, transcendentals=65536,
    )
    received = lax.ppermute(send, "c", swap)
    share = width // OWNERS
    chip_grad = (keep + received.astype(F32)).reshape(NZ, NX, share, width).swapaxes(0, 1).astype(BF16)
    along_x = added(lax.all_to_all(chip_grad, "x", 0, 0, tiled=True), BF16)
    plane = added(lax.all_to_all(along_x, "z", 0, 0, tiled=True), F32)
    both = lax.all_gather(plane, ("y", "c"), axis=0).reshape(NY, NC, share, width)
    grads = jnp.sum(both, axis=0)
    return hidden, grads[0], grads[1]


def solution(mesh):
    fine = Mesh(mesh.devices.reshape(NZ, NX, NY, NC), ("z", "x", "y", "c"))
    row, rep = ("z", "x"), ("y", "c")
    nodes = P(row + rep, None)
    in_specs = (nodes, nodes, nodes, P(row, rep, None, None), P(row, rep, None), P(), P(), nodes)
    out_specs = (nodes, P(row, None), P(row, None))
    return jax.shard_map(body, mesh=fine, in_specs=in_specs, out_specs=out_specs, check_vma=False)
```

```python
import jax
import jax.numpy as jnp
from jax import lax
from jax.experimental import pallas as pl
from jax.experimental.pallas import tpu as pltpu
from jax.sharding import Mesh, PartitionSpec as P

NZ, NX, NY, NC = 8, 4, 8, 2
OWNERS = NZ * NX
GROUPS = NY * NC
T = 128
K_LOC = 12
K_REM = 4
CAP = 2
TOLD = 16
CODES = 64
F32 = jnp.float32
BF16 = jnp.bfloat16
VMEM_LIMIT = 16 * 1024 * 1024


def vmem_call(
    kernel, name, scalar_inputs, array_inputs, outputs, scratch=(), anywhere=(), outside=0, flops=0, bytes_accessed=0, transcendentals=0
):
    vmem = pl.BlockSpec(memory_space=pltpu.VMEM)
    return pl.pallas_call(
        kernel,
        in_specs=[pl.BlockSpec(memory_space=pltpu.SMEM)] * len(scalar_inputs)
        + [pl.BlockSpec(memory_space=pltpu.HBM)] * len(anywhere)
        + [vmem] * len(array_inputs),
        out_specs=[vmem] * (len(outputs) - outside) + [pl.BlockSpec(memory_space=pltpu.HBM)] * outside,
        out_shape=[jax.ShapeDtypeStruct(*of) for of in outputs[: len(outputs) - outside]]
        + [pltpu.HBM(*of) for of in outputs[len(outputs) - outside :]],
        scratch_shapes=list(scratch),
        compiler_params=pltpu.CompilerParams(vmem_limit_bytes=VMEM_LIMIT),
        cost_estimate=pl.CostEstimate(flops=flops, bytes_accessed=bytes_accessed, transcendentals=transcendentals),
        name=name,
    )(*scalar_inputs, *anywhere, *array_inputs)


def quarters_kernel(features_ref, codes_ref, features_t, parts_ref):
    turned = features_ref[...].astype(F32).T.astype(BF16).reshape(NX, T, T)
    features_t[...] = turned
    for x in range(NX):
        parts_ref[x, 0:T, :] = turned[x]
        parts_ref[x, T : T + CODES, :] = codes_ref[...]


def copies_kernel(parts_ref, codes_ref, copies_ref, sems):
    copies = [pltpu.make_async_copy(parts_ref.at[:, 0:T, :], copies_ref.at[z], sems.at[z]) for z in range(NZ)]
    copies.append(pltpu.make_async_copy(parts_ref.at[:, T : T + CODES, :], codes_ref, sems.at[NZ]))
    for copy in copies:
        copy.start()
    for copy in copies:
        copy.wait()


def remote_kernel(scalars, blocks_ref, told_ref, sums_ref):
    core = scalars[0]
    rows = lax.broadcasted_iota(jnp.int16, (CAP * T, T), 0)

    def product(x, y):
        group = y * NC + core
        at = x * GROUPS + group
        first = jnp.clip(scalars[1 + at * CAP], 0, OWNERS - 1)
        second = jnp.clip(scalars[2 + at * CAP], 0, OWNERS - 1)
        start = scalars[1 + NX * GROUPS * CAP + at].astype(F32)
        count = scalars[1 + NX * GROUPS * (CAP + 1) + at].astype(F32)
        told = told_ref[group, x].astype(F32)
        entry = told[0:K_REM] - start
        row = jnp.where(entry < count, entry * T + told[K_REM : 2 * K_REM], -1.0).astype(jnp.int16)
        weight = told[2 * K_REM : 3 * K_REM].astype(BF16)
        hot = jnp.zeros((CAP * T, T), BF16)
        for k in range(K_REM):
            hot = jnp.where(rows == row[k : k + 1], weight[k : k + 1], hot)
        pair = jnp.concatenate([blocks_ref[first], blocks_ref[second]], axis=1)
        return jnp.dot(pair, hot, preferred_element_type=F32).astype(BF16)

    def of_y(y, carry):
        for x in range(NX):
            sums_ref[x, y] = product(x, y)
        return carry

    lax.fori_loop(0, NY, of_y, 0, unroll=True)


def local_kernel(scalars, blocks_ref, told_ref, out_1, out_2, out_3, out_0, hot_ref, total, sem):
    own_z, own_x = scalars[0], scalars[1]
    rows = lax.broadcasted_iota(jnp.int16, (T, T), 0)
    lanes = lax.broadcasted_iota(jnp.int32, (1, T), 1).astype(F32)
    ones, zeros = jnp.ones((T, T), BF16), jnp.zeros((T, T), BF16)
    total[...] = jnp.zeros_like(total)

    def of_four(i, carry):
        for j in range(4):
            p = 4 * i + j
            for x in range(NX):
                block, row, weight = (
                    told_ref[x, TOLD + n * 16 : TOLD + n * 16 + 16, :].astype(F32) for n in range(3)
                )
                code = ((block - p.astype(F32)) * T + row).astype(jnp.int16)
                weight = weight.astype(BF16)
                own = (lanes - jnp.where(p == own_z * NX + x, 0.0, 1024.0)).astype(jnp.int16)
                hot = jnp.where(rows == own, ones, zeros)
                for k in range(K_LOC):
                    hot = jnp.where(rows == code[k : k + 1], weight[k : k + 1], hot)
                hot_ref[x, j * T : (j + 1) * T, :] = hot
        four = jnp.concatenate([blocks_ref[4 * i + j] for j in range(4)], axis=1)
        for x in range(NX):
            total[x] += jnp.dot(four, hot_ref[x], preferred_element_type=F32)
        return carry

    lax.fori_loop(0, OWNERS // 4, of_four, 0, unroll=2)
    copy = pltpu.make_async_copy(total.at[own_x], out_0, sem)
    copy.start()
    for k, out in enumerate((out_1, out_2, out_3)):
        out[...] = total[lax.rem(own_x + k + 1, NX)]
    copy.wait()


def dense_kernel(scalars, near_0, w_self_in, arrived, near_1, near_2, near_3, weights_t, features, features_t, w_agg, cotangent, hidden_ref, send_ref, keep_ref, agg_t, near, w_self, sems):
    own_c, own_x = scalars[0], scalars[1]
    degree = 1.0 + jnp.sum(weights_t[...], axis=0, keepdims=True)
    copy = pltpu.make_async_copy(near_0, near, sems.at[0])
    copy.start()
    copy_w = pltpu.make_async_copy(w_self_in, w_self, sems.at[1])
    copy_w.start()

    def of_quarter(k, own):
        quarter = lax.rem(own_x + (NX - k), NX)
        summed = own[...]
        for y in range(NY):
            summed = summed + arrived[quarter, y].astype(F32)
        agg_t[pl.ds(pl.multiple_of(quarter * T, T), T), :] = (summed / degree).astype(BF16)

    of_quarter(1, near_1)
    of_quarter(2, near_2)
    of_quarter(3, near_3)
    copy.wait()
    of_quarter(0, near)
    copy_w.wait()
    contract = (((0,), (0,)), ((), ()))
    preact = lax.dot_general(agg_t[...], w_agg[...], contract, preferred_element_type=F32) + jnp.dot(
        features[...], w_self[...], preferred_element_type=F32
    )
    sigma = jax.nn.sigmoid(preact)
    hidden_ref[...] = (preact * sigma).astype(BF16)
    grad_pre = (cotangent[...].astype(F32) * sigma * (1.0 + preact * (1.0 - sigma))).astype(BF16)
    of_agg = jnp.dot(agg_t[...], grad_pre, preferred_element_type=F32)
    of_self = jnp.dot(features_t[...].reshape(NX * T, T), grad_pre, preferred_element_type=F32)

    @pl.when(own_c == 0)
    def _():
        keep_ref[...] = of_agg
        send_ref[...] = of_self.astype(BF16)

    @pl.when(own_c != 0)
    def _():
        keep_ref[...] = of_self
        send_ref[...] = of_agg.astype(BF16)


def add_kernel(parts_ref, sum_ref):
    summed = parts_ref[0].astype(F32)
    for i in range(1, parts_ref.shape[0]):
        summed = summed + parts_ref[i].astype(F32)
    sum_ref[...] = summed.astype(sum_ref.dtype)


def added(parts, dtype):
    (summed,) = vmem_call(
        add_kernel, "added", [], [parts], [(parts.shape[1:], dtype)], flops=parts.size, bytes_accessed=3 * parts.size
    )
    return summed


def body(features, edge_weights, neighbours, send_list, send_count, w_agg, w_self, cotangent):
    width = features.shape[1]
    z, x, y, c = (lax.axis_index(a).astype(jnp.int32) for a in ("z", "x", "y", "c"))
    swap = [(0, 1), (1, 0)]

    codes_t = neighbours.T
    weights_t = edge_weights.T
    told = jnp.concatenate([send_count[0], send_list[0].reshape(1, GROUPS * CAP)], axis=1).astype(BF16)
    told = jnp.pad(told, ((0, 3), (0, T - GROUPS * (1 + CAP))))
    block, row = (codes_t // T).astype(BF16), (codes_t % T).astype(BF16)
    gap = jnp.zeros((16 - K_LOC, T), BF16)
    codes = [block[K_LOC:], row[K_LOC:], weights_t[K_LOC:], told]
    codes += [block[:K_LOC], gap, row[:K_LOC], gap, weights_t[:K_LOC], gap]
    features_t, parts = vmem_call(
        quarters_kernel, "quarters", [], [features, jnp.concatenate(codes, axis=0)],
        [((NX, T, T), BF16), ((NX, T + CODES, T), BF16)], bytes_accessed=600_000,
    )
    parts = lax.all_to_all(parts, "x", 0, 0, tiled=True)
    codes, copies = vmem_call(
        copies_kernel, "copies", [], [parts], [((NX, CODES, T), BF16), ((NZ, NX, T, T), BF16)],
        scratch=[pltpu.SemaphoreType.DMA((NZ + 1,))], outside=2, bytes_accessed=1_500_000,
    )
    blocks = lax.all_to_all(copies, "z", 0, 0, tiled=True).reshape(OWNERS, T, T)
    remote_codes = lax.all_gather(codes[:, :TOLD], ("y", "c"), axis=0)
    told = remote_codes[:, :, 12].astype(jnp.int32)
    sources = jnp.arange(GROUPS, dtype=jnp.int32)[:, None, None]
    group = y * NC + c
    here = jnp.sum(jnp.where(sources == group, told, 0), axis=0)
    start = jnp.sum(jnp.where(sources < group, told[:, :, :GROUPS], 0), axis=0)
    lists = here[:, GROUPS : GROUPS * (1 + CAP)]
    scalars = jnp.concatenate([lists.reshape(-1), start.reshape(-1), here[:, :GROUPS].reshape(-1)])

    def remote_sums(core, blocks):
        (sums,) = vmem_call(
            remote_kernel, "remote_sums", [jnp.concatenate([core[None], scalars])], [blocks, remote_codes],
            [((NX, NY, T, T), BF16)], flops=300_000_000, bytes_accessed=2_500_000,
        )
        return sums

    received = lax.ppermute(remote_sums(1 - c, blocks), "c", swap)
    keep = remote_sums(c, blocks)
    chip_sum = (keep.astype(F32) + received.astype(F32)).astype(BF16)
    arrived = lax.all_to_all(chip_sum.reshape(NX * NY, T, T), ("x", "y"), 0, 0, tiled=True)

    *near, near_0 = vmem_call(
        local_kernel, "local_sums", [jnp.stack([z, x])], [blocks, codes], [((T, T), F32)] * NX,
        scratch=[pltpu.VMEM((NX, 4 * T, T), BF16), pltpu.VMEM((NX, T, T), F32), pltpu.SemaphoreType.DMA], outside=1,
        flops=600_000_000, bytes_accessed=1_500_000,
    )
    moved = [lax.ppermute(near[k - 1], "x", [(i, (i + k) % NX) for i in range(NX)]) for k in range(1, NX)]

    hidden, send, keep = vmem_call(
        dense_kernel, "dense", [jnp.stack([c, x])],
        [arrived.reshape(NX, NY, T, T), *moved, weights_t.astype(F32), features, features_t, w_agg, cotangent],
        [((T, width), BF16), ((width, width), BF16), ((width, width), F32)],
        scratch=[pltpu.VMEM((width, T), BF16), pltpu.VMEM((T, T), F32), pltpu.VMEM((width, width), BF16), pltpu.SemaphoreType.DMA((2,))],
        anywhere=[near_0, w_self], flops=300_000_000, bytes_accessed=5_000_000, transcendentals=65536,
    )
    received = lax.ppermute(send, "c", swap)
    share = width // OWNERS
    chip_grad = (keep + received.astype(F32)).astype(BF16).reshape(OWNERS, share, width)
    plane = added(lax.all_to_all(chip_grad, ("z", "x"), 0, 0, tiled=True), F32)
    both = lax.all_gather(plane, ("y", "c"), axis=0).reshape(NY, NC, share, width)
    grads = jnp.sum(both, axis=0)
    return hidden, grads[0], grads[1]


def solution(mesh):
    fine = Mesh(mesh.devices.reshape(NZ, NX, NY, NC), ("z", "x", "y", "c"))
    row, rep = ("z", "x"), ("y", "c")
    nodes = P(row + rep, None)
    in_specs = (nodes, nodes, nodes, P(row, rep, None, None), P(row, rep, None), P(), P(), nodes)
    out_specs = (nodes, P(row, None), P(row, None))
    return jax.shard_map(body, mesh=fine, in_specs=in_specs, out_specs=out_specs, check_vma=False)
```

```python
import jax
import jax.numpy as jnp
from jax import lax
from jax.experimental import pallas as pl
from jax.experimental.pallas import tpu as pltpu
from jax.sharding import Mesh, PartitionSpec as P

NZ, NX, NY, NC = 8, 4, 8, 2
OWNERS = NZ * NX
GROUPS = NY * NC
T = 128
K_LOC = 12
K_REM = 4
CAP = 2
TOLD = 16
X, Y = ("x1", "x0"), ("y2", "y1", "y0")
F32 = jnp.float32
BF16 = jnp.bfloat16
VMEM_LIMIT = 16 * 1024 * 1024


def vmem_call(
    kernel, name, scalar_inputs, array_inputs, outputs, scratch=(), anywhere=(), outside=0, flops=0, bytes_accessed=0, transcendentals=0
):
    vmem = pl.BlockSpec(memory_space=pltpu.VMEM)
    return pl.pallas_call(
        kernel,
        in_specs=[pl.BlockSpec(memory_space=pltpu.SMEM)] * len(scalar_inputs)
        + [pl.BlockSpec(memory_space=pltpu.HBM)] * len(anywhere)
        + [vmem] * len(array_inputs),
        out_specs=[vmem] * (len(outputs) - outside) + [pl.BlockSpec(memory_space=pltpu.HBM)] * outside,
        out_shape=[jax.ShapeDtypeStruct(*of) for of in outputs[: len(outputs) - outside]]
        + [pltpu.HBM(*of) for of in outputs[len(outputs) - outside :]],
        scratch_shapes=list(scratch),
        compiler_params=pltpu.CompilerParams(vmem_limit_bytes=VMEM_LIMIT),
        cost_estimate=pl.CostEstimate(flops=flops, bytes_accessed=bytes_accessed, transcendentals=transcendentals),
        name=name,
    )(*scalar_inputs, *anywhere, *array_inputs)


def spread_kernel(features_ref, features_t, quarters_ref, sems):
    features_t[...] = features_ref[...].astype(F32).T.astype(BF16).reshape(NX, T, T)
    copies = [pltpu.make_async_copy(features_t, quarters_ref.at[z], sems.at[z]) for z in range(NZ)]
    for copy in copies:
        copy.start()
    for copy in copies:
        copy.wait()


def remote_kernel(scalars, blocks_ref, told_ref, sums_ref):
    core = scalars[0]
    rows = lax.broadcasted_iota(jnp.int16, (CAP * T, T), 0)

    def product(x, y):
        group = y * NC + core
        at = x * GROUPS + group
        first = jnp.clip(scalars[1 + at * CAP], 0, OWNERS - 1)
        second = jnp.clip(scalars[2 + at * CAP], 0, OWNERS - 1)
        start = scalars[1 + NX * GROUPS * CAP + at].astype(F32)
        count = scalars[1 + NX * GROUPS * (CAP + 1) + at].astype(F32)
        told = told_ref[core, y, x].astype(F32)
        entry = told[0:K_REM] - start
        row = jnp.where(entry < count, entry * T + told[K_REM : 2 * K_REM], -1.0).astype(jnp.int16)
        weight = told[2 * K_REM : 3 * K_REM].astype(BF16)
        hot = jnp.zeros((CAP * T, T), BF16)
        for k in range(K_REM):
            hot = jnp.where(rows == row[k : k + 1], weight[k : k + 1], hot)
        pair = jnp.concatenate([blocks_ref[first], blocks_ref[second]], axis=1)
        return jnp.dot(pair, hot, preferred_element_type=F32).astype(BF16)

    def of_y(y, carry):
        for x in range(NX):
            sums_ref[x, y] = product(x, y)
        return carry

    lax.fori_loop(0, NY, of_y, 0, unroll=True)


def local_kernel(scalars, blocks_ref, told_ref, out_1, out_2, out_3, out_0, hot_ref, total, sem):
    own_z, own_x = scalars[0], scalars[1]
    rows = lax.broadcasted_iota(jnp.int16, (T, T), 0)
    lanes = lax.broadcasted_iota(jnp.int32, (1, T), 1).astype(F32)
    ones, zeros = jnp.ones((T, T), BF16), jnp.zeros((T, T), BF16)
    total[...] = jnp.zeros_like(total)

    def of_four(i, carry):
        for j in range(4):
            p = 4 * i + j
            for x in range(NX):
                block, row, weight = (
                    told_ref[x, TOLD + n * 16 : TOLD + n * 16 + 16, :].astype(F32) for n in range(3)
                )
                code = ((block - p.astype(F32)) * T + row).astype(jnp.int16)
                weight = weight.astype(BF16)
                own = (lanes - jnp.where(p == own_z * NX + x, 0.0, 1024.0)).astype(jnp.int16)
                hot = jnp.where(rows == own, ones, zeros)
                for k in range(K_LOC):
                    hot = jnp.where(rows == code[k : k + 1], weight[k : k + 1], hot)
                hot_ref[x, j * T : (j + 1) * T, :] = hot
        four = jnp.concatenate([blocks_ref[4 * i + j] for j in range(4)], axis=1)
        for x in range(NX):
            total[x] += jnp.dot(four, hot_ref[x], preferred_element_type=F32)
        return carry

    lax.fori_loop(0, OWNERS // 4, of_four, 0, unroll=2)
    copy = pltpu.make_async_copy(total.at[own_x], out_0, sem)
    copy.start()
    for k, out in enumerate((out_1, out_2, out_3)):
        out[...] = total[lax.rem(own_x + k + 1, NX)]
    copy.wait()


def dense_kernel(scalars, near_0, w_self_in, arrived, near_1, near_2, near_3, weights_t, features, features_t, w_agg, cotangent, hidden_ref, send_ref, keep_ref, agg_t, near, w_self, sems):
    own_c, own_x = scalars[0], scalars[1]
    degree = 1.0 + jnp.sum(weights_t[...], axis=0, keepdims=True)
    copy = pltpu.make_async_copy(near_0, near, sems.at[0])
    copy.start()
    copy_w = pltpu.make_async_copy(w_self_in, w_self, sems.at[1])
    copy_w.start()

    def of_quarter(k, own):
        quarter = lax.rem(own_x + (NX - k), NX)
        summed = own[...]
        for y in range(NY):
            summed = summed + arrived[quarter, y].astype(F32)
        agg_t[pl.ds(pl.multiple_of(quarter * T, T), T), :] = (summed / degree).astype(BF16)

    of_quarter(1, near_1)
    of_quarter(2, near_2)
    of_quarter(3, near_3)
    copy.wait()
    of_quarter(0, near)
    copy_w.wait()
    contract = (((0,), (0,)), ((), ()))
    preact = lax.dot_general(agg_t[...], w_agg[...], contract, preferred_element_type=F32) + jnp.dot(
        features[...], w_self[...], preferred_element_type=F32
    )
    sigma = jax.nn.sigmoid(preact)
    hidden_ref[...] = (preact * sigma).astype(BF16)
    grad_pre = (cotangent[...].astype(F32) * sigma * (1.0 + preact * (1.0 - sigma))).astype(BF16)
    of_agg = jnp.dot(agg_t[...], grad_pre, preferred_element_type=F32)
    of_self = jnp.dot(features_t[...].reshape(NX * T, T), grad_pre, preferred_element_type=F32)

    @pl.when(own_c == 0)
    def _():
        keep_ref[...] = of_agg
        send_ref[...] = of_self.astype(BF16)

    @pl.when(own_c != 0)
    def _():
        keep_ref[...] = of_self
        send_ref[...] = of_agg.astype(BF16)


def add_kernel(parts_ref, sum_ref):
    summed = parts_ref[0].astype(F32)
    for i in range(1, parts_ref.shape[0]):
        summed = summed + parts_ref[i].astype(F32)
    sum_ref[...] = summed.astype(sum_ref.dtype)


def added(parts, dtype):
    (summed,) = vmem_call(
        add_kernel, "added", [], [parts], [(parts.shape[1:], dtype)], flops=parts.size, bytes_accessed=3 * parts.size
    )
    return summed


def body(features, edge_weights, neighbours, send_list, send_count, w_agg, w_self, cotangent):
    width = features.shape[1]
    z, x, y, c = (lax.axis_index(a).astype(jnp.int32) for a in ("z", X, Y, "c"))
    swap = [(0, 1), (1, 0)]

    features_t, quarters = vmem_call(
        spread_kernel, "spread", [], [features], [((NX, T, T), BF16), ((NZ, NX, T, T), BF16)],
        scratch=[pltpu.SemaphoreType.DMA((NZ,))], outside=1, bytes_accessed=1_500_000,
    )
    blocks = lax.all_to_all(quarters.reshape(OWNERS, T, T), ("z",) + X, 0, 0, tiled=True)

    codes_t = neighbours.T
    weights_t = edge_weights.T
    told = jnp.concatenate([send_count[0], send_list[0].reshape(1, GROUPS * CAP)], axis=1).astype(BF16)
    told = jnp.pad(told, ((0, 3), (0, T - GROUPS * (1 + CAP))))
    block, row = (codes_t // T).astype(BF16), (codes_t % T).astype(BF16)
    gap = jnp.zeros((16 - K_LOC, T), BF16)
    codes = [block[K_LOC:], row[K_LOC:], weights_t[K_LOC:], told]
    codes += [block[:K_LOC], gap, row[:K_LOC], gap, weights_t[:K_LOC], gap]
    codes = jnp.concatenate(codes, axis=0)
    for axis in reversed(X):
        codes = lax.all_gather(codes, axis, axis=0)
    codes = codes.reshape(NX, 64, T)
    remote_codes = codes[:, :TOLD]
    for axis in reversed(Y):
        remote_codes = lax.all_gather(remote_codes, axis, axis=0)
    remote_codes = lax.all_gather(remote_codes, "c", axis=0).reshape(NC, NY, NX, TOLD, T)
    told = remote_codes[:, :, :, 12].swapaxes(0, 1).reshape(GROUPS, NX, T).astype(jnp.int32)
    sources = jnp.arange(GROUPS, dtype=jnp.int32)[:, None, None]
    group = y * NC + c
    here = jnp.sum(jnp.where(sources == group, told, 0), axis=0)
    start = jnp.sum(jnp.where(sources < group, told[:, :, :GROUPS], 0), axis=0)
    lists = here[:, GROUPS : GROUPS * (1 + CAP)]
    scalars = jnp.concatenate([lists.reshape(-1), start.reshape(-1), here[:, :GROUPS].reshape(-1)])

    def remote_sums(core, blocks):
        (sums,) = vmem_call(
            remote_kernel, "remote_sums", [jnp.concatenate([core[None], scalars])], [blocks, remote_codes],
            [((NX, NY, T, T), BF16)], flops=300_000_000, bytes_accessed=2_500_000,
        )
        return sums

    received = lax.ppermute(remote_sums(1 - c, blocks), "c", swap)
    keep = remote_sums(c, blocks)
    chip_sum = (keep.astype(F32) + received.astype(F32)).astype(BF16)
    arrived = lax.all_to_all(chip_sum.reshape(NX * NY, T, T), X + Y, 0, 0, tiled=True)

    *near, near_0 = vmem_call(
        local_kernel, "local_sums", [jnp.stack([z, x])], [blocks, codes], [((T, T), F32)] * NX,
        scratch=[pltpu.VMEM((NX, 4 * T, T), BF16), pltpu.VMEM((NX, T, T), F32), pltpu.SemaphoreType.DMA], outside=1,
        flops=600_000_000, bytes_accessed=1_500_000,
    )
    moved = [lax.ppermute(near[k - 1], X, [(i, (i + k) % NX) for i in range(NX)]) for k in range(1, NX)]

    hidden, send, keep = vmem_call(
        dense_kernel, "dense", [jnp.stack([c, x])],
        [arrived.reshape(NX, NY, T, T), *moved, weights_t.astype(F32), features, features_t, w_agg, cotangent],
        [((T, width), BF16), ((width, width), BF16), ((width, width), F32)],
        scratch=[pltpu.VMEM((width, T), BF16), pltpu.VMEM((T, T), F32), pltpu.VMEM((width, width), BF16), pltpu.SemaphoreType.DMA((2,))],
        anywhere=[near_0, w_self], flops=300_000_000, bytes_accessed=5_000_000, transcendentals=65536,
    )
    received = lax.ppermute(send, "c", swap)
    share = width // OWNERS
    chip_grad = (keep + received.astype(F32)).astype(BF16).reshape(OWNERS, share, width)
    plane = added(lax.all_to_all(chip_grad, ("z",) + X, 0, 0, tiled=True), BF16)
    planes = lax.all_to_all(jnp.broadcast_to(plane, (NY, share, width)), Y, 0, 0, tiled=True)
    grads = lax.all_gather(added(planes, F32), "c", axis=0)
    return hidden, grads[0], grads[1]


def solution(mesh):
    axes = ("z",) + X + Y + ("c",)
    fine = Mesh(mesh.devices.reshape(NZ, 2, 2, 2, 2, 2, NC), axes)
    row, rep = ("z",) + X, Y + ("c",)
    nodes = P(row + rep, None)
    in_specs = (nodes, nodes, nodes, P(row, rep, None, None), P(row, rep, None), P(), P(), nodes)
    out_specs = (nodes, P(row, None), P(row, None))
    return jax.shard_map(body, mesh=fine, in_specs=in_specs, out_specs=out_specs, check_vma=False)
```

```python
import jax
import jax.numpy as jnp
from jax import lax
from jax.experimental import pallas as pl
from jax.experimental.pallas import tpu as pltpu
from jax.sharding import Mesh, PartitionSpec as P

NZ, NX, NY, NC = 8, 4, 8, 2
OWNERS = NZ * NX
GROUPS = NY * NC
T = 128
K_LOC = 12
K_REM = 4
CAP = 2
TOLD = 16
X, Y = ("x1", "x0"), ("y2", "y1", "y0")
F32 = jnp.float32
BF16 = jnp.bfloat16
VMEM_LIMIT = 16 * 1024 * 1024


def vmem_call(
    kernel, name, scalar_inputs, array_inputs, outputs, scratch=(), anywhere=(), outside=0, flops=0, bytes_accessed=0, transcendentals=0
):
    vmem = pl.BlockSpec(memory_space=pltpu.VMEM)
    return pl.pallas_call(
        kernel,
        in_specs=[pl.BlockSpec(memory_space=pltpu.SMEM)] * len(scalar_inputs)
        + [pl.BlockSpec(memory_space=pltpu.HBM)] * len(anywhere)
        + [vmem] * len(array_inputs),
        out_specs=[vmem] * (len(outputs) - outside) + [pl.BlockSpec(memory_space=pltpu.HBM)] * outside,
        out_shape=[jax.ShapeDtypeStruct(*of) for of in outputs[: len(outputs) - outside]]
        + [pltpu.HBM(*of) for of in outputs[len(outputs) - outside :]],
        scratch_shapes=list(scratch),
        compiler_params=pltpu.CompilerParams(vmem_limit_bytes=VMEM_LIMIT),
        cost_estimate=pl.CostEstimate(flops=flops, bytes_accessed=bytes_accessed, transcendentals=transcendentals),
        name=name,
    )(*scalar_inputs, *anywhere, *array_inputs)


def spread_kernel(features_ref, features_t, quarters_ref, sems):
    features_t[...] = features_ref[...].astype(F32).T.astype(BF16).reshape(NX, T, T)
    copies = [pltpu.make_async_copy(features_t, quarters_ref.at[z], sems.at[z]) for z in range(NZ)]
    for copy in copies:
        copy.start()
    for copy in copies:
        copy.wait()


def remote_kernel(scalars, blocks_ref, told_ref, sums_ref):
    core = scalars[0]
    rows = lax.broadcasted_iota(jnp.int16, (CAP * T, T), 0)

    def product(x, y):
        group = y * NC + core
        at = x * GROUPS + group
        first = jnp.clip(scalars[1 + at * CAP], 0, OWNERS - 1)
        second = jnp.clip(scalars[2 + at * CAP], 0, OWNERS - 1)
        start = scalars[1 + NX * GROUPS * CAP + at].astype(F32)
        count = scalars[1 + NX * GROUPS * (CAP + 1) + at].astype(F32)
        told = told_ref[core, y % 2, y // 2 % 2, x % 2, x // 2, y // 4].astype(F32)
        entry = told[0:K_REM] - start
        row = jnp.where(entry < count, entry * T + told[K_REM : 2 * K_REM], -1.0).astype(jnp.int16)
        weight = told[2 * K_REM : 3 * K_REM].astype(BF16)
        hot = jnp.zeros((CAP * T, T), BF16)
        for k in range(K_REM):
            hot = jnp.where(rows == row[k : k + 1], weight[k : k + 1], hot)
        pair = jnp.concatenate([blocks_ref[first], blocks_ref[second]], axis=1)
        return jnp.dot(pair, hot, preferred_element_type=F32).astype(BF16)

    for y in range(NY):
        for x in range(NX):
            sums_ref[x, y] = product(x, y)


def local_kernel(scalars, blocks_ref, told_ref, out_1, out_2, out_3, out_0, hot_ref, total, sem):
    own_z, own_x = scalars[0], scalars[1]
    rows = lax.broadcasted_iota(jnp.int16, (T, T), 0)
    lanes = lax.broadcasted_iota(jnp.int32, (1, T), 1).astype(F32)
    ones, zeros = jnp.ones((T, T), BF16), jnp.zeros((T, T), BF16)
    total[...] = jnp.zeros_like(total)

    def of_four(i, carry):
        for j in range(4):
            p = 4 * i + j
            for x in range(NX):
                block, row, weight = (
                    told_ref[x % 2, x // 2, n * 16 : n * 16 + 16, :].astype(F32) for n in range(3)
                )
                code = ((block - p.astype(F32)) * T + row).astype(jnp.int16)
                weight = weight.astype(BF16)
                own = (lanes - jnp.where(p == own_z * NX + x, 0.0, 1024.0)).astype(jnp.int16)
                hot = jnp.where(rows == own, ones, zeros)
                for k in range(K_LOC):
                    hot = jnp.where(rows == code[k : k + 1], weight[k : k + 1], hot)
                hot_ref[x, j * T : (j + 1) * T, :] = hot
        four = jnp.concatenate([blocks_ref[4 * i + j] for j in range(4)], axis=1)
        for x in range(NX):
            total[x] += jnp.dot(four, hot_ref[x], preferred_element_type=F32)
        return carry

    lax.fori_loop(0, OWNERS // 4, of_four, 0, unroll=2)
    copy = pltpu.make_async_copy(total.at[own_x], out_0, sem)
    copy.start()
    for k, out in enumerate((out_1, out_2, out_3)):
        out[...] = total[lax.rem(own_x + k + 1, NX)]
    copy.wait()


def dense_kernel(scalars, near_0, w_self_in, arrived, near_1, near_2, near_3, weights_t, features, features_t, w_agg, cotangent, hidden_ref, send_ref, keep_ref, agg_t, near, w_self, sems):
    own_c, own_x = scalars[0], scalars[1]
    degree = 1.0 + jnp.sum(weights_t[...], axis=0, keepdims=True)
    copy = pltpu.make_async_copy(near_0, near, sems.at[0])
    copy.start()
    copy_w = pltpu.make_async_copy(w_self_in, w_self, sems.at[1])
    copy_w.start()

    def of_quarter(k, own):
        quarter = lax.rem(own_x + (NX - k), NX)
        summed = own[...]
        for y in range(NY):
            summed = summed + arrived[quarter, y].astype(F32)
        agg_t[pl.ds(pl.multiple_of(quarter * T, T), T), :] = (summed / degree).astype(BF16)

    of_quarter(1, near_1)
    of_quarter(2, near_2)
    of_quarter(3, near_3)
    copy.wait()
    of_quarter(0, near)
    copy_w.wait()
    contract = (((0,), (0,)), ((), ()))
    preact = lax.dot_general(agg_t[...], w_agg[...], contract, preferred_element_type=F32) + jnp.dot(
        features[...], w_self[...], preferred_element_type=F32
    )
    sigma = jax.nn.sigmoid(preact)
    hidden_ref[...] = (preact * sigma).astype(BF16)
    grad_pre = (cotangent[...].astype(F32) * sigma * (1.0 + preact * (1.0 - sigma))).astype(BF16)
    of_agg = jnp.dot(agg_t[...], grad_pre, preferred_element_type=F32)
    of_self = jnp.dot(features_t[...].reshape(NX * T, T), grad_pre, preferred_element_type=F32)

    def lay(ref, product):
        for j in range(NX):
            ref[:, j] = product[:, j * T : (j + 1) * T].reshape(OWNERS, ref.shape[2], T).astype(ref.dtype)

    @pl.when(own_c == 0)
    def _():
        lay(keep_ref, of_agg)
        lay(send_ref, of_self)

    @pl.when(own_c != 0)
    def _():
        lay(keep_ref, of_self)
        lay(send_ref, of_agg)


def add_kernel(parts_ref, sum_ref):
    summed = parts_ref[0].astype(F32)
    for i in range(1, parts_ref.shape[0]):
        summed = summed + parts_ref[i].astype(F32)
    sum_ref[...] = summed.astype(sum_ref.dtype)


def added(parts, dtype):
    (summed,) = vmem_call(
        add_kernel, "added", [], [parts], [(parts.shape[1:], dtype)], flops=parts.size, bytes_accessed=3 * parts.size
    )
    return summed


def body(features, edge_weights, neighbours, send_list, send_count, w_agg, w_self, cotangent):
    width = features.shape[1]
    z, x, y, c = (lax.axis_index(a).astype(jnp.int32) for a in ("z", X, Y, "c"))
    swap = [(0, 1), (1, 0)]

    features_t, quarters = vmem_call(
        spread_kernel, "spread", [], [features], [((NX, T, T), BF16), ((NZ, NX, T, T), BF16)],
        scratch=[pltpu.SemaphoreType.DMA((NZ,))], outside=1, bytes_accessed=1_500_000,
    )
    blocks = lax.all_to_all(quarters.reshape(OWNERS, T, T), ("z",) + X, 0, 0, tiled=True)

    codes_t = neighbours.T
    weights_t = edge_weights.T
    told = jnp.concatenate([send_count[0], send_list[0].reshape(1, GROUPS * CAP)], axis=1).astype(BF16)
    told = jnp.pad(told, ((0, 3), (0, T - GROUPS * (1 + CAP))))
    block, row = (codes_t // T).astype(BF16), (codes_t % T).astype(BF16)
    gap = jnp.zeros((16 - K_LOC, T), BF16)
    codes = jnp.concatenate([block[K_LOC:], row[K_LOC:], weights_t[K_LOC:], told], axis=0)
    codes = lax.all_gather(codes, "y2", axis=0).reshape(2 * TOLD, T)
    codes = jnp.concatenate([codes, block[:K_LOC], gap, row[:K_LOC], gap, weights_t[:K_LOC], gap], axis=0)
    codes = lax.all_gather(lax.all_gather(codes, "x1", axis=0), "x0", axis=0)
    remote_codes, local_codes = codes[:, :, : 2 * TOLD], codes[:, :, 2 * TOLD :]
    for axis in ("y1", "y0", "c"):
        remote_codes = lax.all_gather(remote_codes, axis, axis=0)
    remote_codes = remote_codes.reshape(NC, 2, 2, 2, 2, 2, TOLD, T)
    told = remote_codes[:, :, :, :, :, :, 12].transpose(5, 2, 1, 0, 4, 3, 6)
    told = told.reshape(GROUPS, NX, T).astype(jnp.int32)
    sources = jnp.arange(GROUPS, dtype=jnp.int32)[:, None, None]
    group = y * NC + c
    here = jnp.sum(jnp.where(sources == group, told, 0), axis=0)
    start = jnp.sum(jnp.where(sources < group, told[:, :, :GROUPS], 0), axis=0)
    lists = here[:, GROUPS : GROUPS * (1 + CAP)]
    scalars = jnp.concatenate([lists.reshape(-1), start.reshape(-1), here[:, :GROUPS].reshape(-1)])

    def remote_sums(core, blocks):
        (sums,) = vmem_call(
            remote_kernel, "remote_sums", [jnp.concatenate([core[None], scalars])], [blocks, remote_codes],
            [((NX, NY, T, T), BF16)], flops=300_000_000, bytes_accessed=2_500_000,
        )
        return sums

    received = lax.ppermute(remote_sums(1 - c, blocks), "c", swap)
    keep = remote_sums(c, blocks)
    chip_sum = (keep.astype(F32) + received.astype(F32)).astype(BF16)
    arrived = lax.all_to_all(chip_sum.reshape(NX * NY, T, T), X + Y, 0, 0, tiled=True)

    *near, near_0 = vmem_call(
        local_kernel, "local_sums", [jnp.stack([z, x])], [blocks, local_codes], [((T, T), F32)] * NX,
        scratch=[pltpu.VMEM((NX, 4 * T, T), BF16), pltpu.VMEM((NX, T, T), F32), pltpu.SemaphoreType.DMA], outside=1,
        flops=600_000_000, bytes_accessed=1_500_000,
    )
    near_0 = pltpu.with_memory_space_constraint(near_0, pltpu.HBM)
    moved = [lax.ppermute(near[k - 1], X, [(i, (i + k) % NX) for i in range(NX)]) for k in range(1, NX)]

    share = width // OWNERS
    hidden, send, keep = vmem_call(
        dense_kernel, "dense", [jnp.stack([c, x])],
        [arrived.reshape(NX, NY, T, T), *moved, weights_t.astype(F32), features, features_t, w_agg, cotangent],
        [((T, width), BF16), ((OWNERS, NX, share, T), BF16), ((OWNERS, NX, share, T), F32)],
        scratch=[pltpu.VMEM((width, T), BF16), pltpu.VMEM((T, T), F32), pltpu.VMEM((width, width), BF16), pltpu.SemaphoreType.DMA((2,))],
        anywhere=[near_0, w_self], flops=300_000_000, bytes_accessed=5_000_000, transcendentals=65536,
    )
    received = lax.ppermute(send, "c", swap)
    chip_grad = (keep + received.astype(F32)).astype(BF16).reshape(OWNERS, NX * share, T)
    plane = added(lax.all_to_all(chip_grad, ("z",) + X, 0, 0, tiled=True), BF16)
    planes = lax.all_to_all(jnp.broadcast_to(plane, (NY,) + plane.shape), Y, 0, 0, tiled=True)
    grads = lax.all_gather(added(planes, F32), "c", axis=0)
    grads = grads.reshape(NC, NX, share, T).swapaxes(1, 2).reshape(NC, share, width)
    return hidden, grads[0], grads[1]


def solution(mesh):
    axes = ("z",) + X + Y + ("c",)
    fine = Mesh(mesh.devices.reshape(NZ, 2, 2, 2, 2, 2, NC), axes)
    row, rep = ("z",) + X, Y + ("c",)
    nodes = P(row + rep, None)
    in_specs = (nodes, nodes, nodes, P(row, rep, None, None), P(row, rep, None), P(), P(), nodes)
    out_specs = (nodes, P(row, None), P(row, None))
    return jax.shard_map(body, mesh=fine, in_specs=in_specs, out_specs=out_specs, check_vma=False)
```

```python
import jax
import jax.numpy as jnp
from jax import lax
from jax.experimental import pallas as pl
from jax.experimental.pallas import tpu as pltpu
from jax.sharding import Mesh, PartitionSpec as P

NZ, NX, NY, NC = 8, 4, 8, 2
OWNERS = NZ * NX
GROUPS = NY * NC
T = 128
K_LOC = 12
K_REM = 4
CAP = 2
TOLD = 16
X, Y = ("x1", "x0"), ("y2", "y1", "y0")
F32 = jnp.float32
BF16 = jnp.bfloat16
VMEM_LIMIT = 16 * 1024 * 1024


def vmem_call(
    kernel, name, scalar_inputs, array_inputs, outputs, scratch=(), anywhere=(), outside=0, flops=0, bytes_accessed=0, transcendentals=0
):
    vmem = pl.BlockSpec(memory_space=pltpu.VMEM)
    return pl.pallas_call(
        kernel,
        in_specs=[pl.BlockSpec(memory_space=pltpu.SMEM)] * len(scalar_inputs)
        + [pl.BlockSpec(memory_space=pltpu.HBM)] * len(anywhere)
        + [vmem] * len(array_inputs),
        out_specs=[vmem] * (len(outputs) - outside) + [pl.BlockSpec(memory_space=pltpu.HBM)] * outside,
        out_shape=[jax.ShapeDtypeStruct(*of) for of in outputs[: len(outputs) - outside]]
        + [pltpu.HBM(*of) for of in outputs[len(outputs) - outside :]],
        scratch_shapes=list(scratch),
        compiler_params=pltpu.CompilerParams(vmem_limit_bytes=VMEM_LIMIT),
        cost_estimate=pl.CostEstimate(flops=flops, bytes_accessed=bytes_accessed, transcendentals=transcendentals),
        name=name,
    )(*scalar_inputs, *anywhere, *array_inputs)


def spread_kernel(features_ref, features_t, quarters_ref, sems):
    features_t[...] = features_ref[...].astype(F32).T.astype(BF16).reshape(NX, T, T)
    copies = [pltpu.make_async_copy(features_t, quarters_ref.at[z], sems.at[z]) for z in range(NZ)]
    for copy in copies:
        copy.start()
    for copy in copies:
        copy.wait()


def remote_kernel(scalars, blocks_ref, told_ref, sums_ref):
    core, own_x = scalars[0], scalars[1]
    rows = lax.broadcasted_iota(jnp.int16, (CAP * T, T), 0)

    def product(k, y):
        group = y * NC + core
        at = k * GROUPS + group
        first = jnp.clip(scalars[2 + at * CAP], 0, OWNERS - 1)
        second = jnp.clip(scalars[3 + at * CAP], 0, OWNERS - 1)
        start = scalars[2 + NX * GROUPS * CAP + at].astype(F32)
        count = scalars[2 + NX * GROUPS * (CAP + 1) + at].astype(F32)
        told = told_ref[group, k].astype(F32)
        entry = told[0:K_REM] - start
        row = jnp.where(entry < count, entry * T + told[K_REM : 2 * K_REM], -1.0).astype(jnp.int16)
        weight = told[2 * K_REM : 3 * K_REM].astype(BF16)
        hot = jnp.zeros((CAP * T, T), BF16)
        for slot in range(K_REM):
            hot = jnp.where(rows == row[slot : slot + 1], weight[slot : slot + 1], hot)
        pair = jnp.concatenate([blocks_ref[first], blocks_ref[second]], axis=1)
        return jnp.dot(pair, hot, preferred_element_type=F32).astype(BF16)

    for y in range(NY):
        for k in range(NX):
            sums_ref[lax.rem(own_x + (NX - k), NX), y] = product(k, y)


def local_kernel(scalars, blocks_ref, told_ref, out_1, out_2, out_3, out_0, hot_ref, total, sem):
    own_z, own_x = scalars[0], scalars[1]
    rows = lax.broadcasted_iota(jnp.int16, (T, T), 0)
    lanes = lax.broadcasted_iota(jnp.int32, (1, T), 1).astype(F32)
    ones, zeros = jnp.ones((T, T), BF16), jnp.zeros((T, T), BF16)
    total[...] = jnp.zeros_like(total)

    def of_four(i, carry):
        for j in range(4):
            p = 4 * i + j
            for k in range(NX):
                block, row, weight = (told_ref[k, n * 16 : n * 16 + 16, :].astype(F32) for n in range(1, 4))
                code = ((block - p.astype(F32)) * T + row).astype(jnp.int16)
                weight = weight.astype(BF16)
                here = p == own_z * NX + lax.rem(own_x + (NX - k), NX)
                own = (lanes - jnp.where(here, 0.0, 1024.0)).astype(jnp.int16)
                hot = jnp.where(rows == own, ones, zeros)
                for slot in range(K_LOC):
                    hot = jnp.where(rows == code[slot : slot + 1], weight[slot : slot + 1], hot)
                hot_ref[k, j * T : (j + 1) * T, :] = hot
        four = jnp.concatenate([blocks_ref[4 * i + j] for j in range(4)], axis=1)
        for k in range(NX):
            total[k] += jnp.dot(four, hot_ref[k], preferred_element_type=F32)
        return carry

    lax.fori_loop(0, OWNERS // 4, of_four, 0, unroll=2)
    copy = pltpu.make_async_copy(total.at[0], out_0, sem)
    copy.start()
    for k, out in enumerate((out_1, out_2, out_3)):
        out[...] = total[NX - 1 - k]
    copy.wait()


def dense_kernel(scalars, near_0, w_self_in, arrived, near_1, near_2, near_3, weights_t, features, features_t, w_agg, cotangent, hidden_ref, send_ref, keep_ref, agg_t, near, w_self, sems):
    own_c, own_x = scalars[0], scalars[1]
    degree = 1.0 + jnp.sum(weights_t[...], axis=0, keepdims=True)
    copy = pltpu.make_async_copy(near_0, near, sems.at[0])
    copy.start()
    copy_w = pltpu.make_async_copy(w_self_in, w_self, sems.at[1])
    copy_w.start()

    def of_quarter(k, own):
        quarter = lax.rem(own_x + (NX - k), NX)
        summed = own[...]
        for y in range(NY):
            summed = summed + arrived[quarter, y].astype(F32)
        agg_t[pl.ds(pl.multiple_of(quarter * T, T), T), :] = (summed / degree).astype(BF16)

    of_quarter(1, near_1)
    of_quarter(2, near_2)
    of_quarter(3, near_3)
    copy.wait()
    of_quarter(0, near)
    copy_w.wait()
    contract = (((0,), (0,)), ((), ()))
    preact = lax.dot_general(agg_t[...], w_agg[...], contract, preferred_element_type=F32) + jnp.dot(
        features[...], w_self[...], preferred_element_type=F32
    )
    sigma = jax.nn.sigmoid(preact)
    hidden_ref[...] = (preact * sigma).astype(BF16)
    grad_pre = (cotangent[...].astype(F32) * sigma * (1.0 + preact * (1.0 - sigma))).astype(BF16)
    of_agg = jnp.dot(agg_t[...], grad_pre, preferred_element_type=F32)
    of_self = jnp.dot(features_t[...].reshape(NX * T, T), grad_pre, preferred_element_type=F32)

    def lay(ref, product):
        for j in range(NX):
            ref[:, j] = product[:, j * T : (j + 1) * T].reshape(OWNERS, ref.shape[2], T).astype(ref.dtype)

    @pl.when(own_c == 0)
    def _():
        lay(keep_ref, of_agg)
        lay(send_ref, of_self)

    @pl.when(own_c != 0)
    def _():
        lay(keep_ref, of_self)
        lay(send_ref, of_agg)


def add_kernel(parts_ref, sum_ref):
    summed = parts_ref[0].astype(F32)
    for i in range(1, parts_ref.shape[0]):
        summed = summed + parts_ref[i].astype(F32)
    sum_ref[...] = summed.astype(sum_ref.dtype)


def added(parts, dtype):
    (summed,) = vmem_call(
        add_kernel, "added", [], [parts], [(parts.shape[1:], dtype)], flops=parts.size, bytes_accessed=3 * parts.size
    )
    return summed


def body(features, edge_weights, neighbours, send_list, send_count, w_agg, w_self, cotangent):
    width = features.shape[1]
    z, x, y, c = (lax.axis_index(a).astype(jnp.int32) for a in ("z", X, Y, "c"))
    swap = [(0, 1), (1, 0)]

    features_t, quarters = vmem_call(
        spread_kernel, "spread", [], [features], [((NX, T, T), BF16), ((NZ, NX, T, T), BF16)],
        scratch=[pltpu.SemaphoreType.DMA((NZ,))], outside=1, bytes_accessed=1_500_000,
    )
    blocks = lax.all_to_all(quarters.reshape(OWNERS, T, T), ("z",) + X, 0, 0, tiled=True)

    codes_t = neighbours.T
    weights_t = edge_weights.T
    told = jnp.concatenate([send_count[0], send_list[0].reshape(1, GROUPS * CAP)], axis=1).astype(BF16)
    told = jnp.pad(told, ((0, 3), (0, T - GROUPS * (1 + CAP))))
    block, row = (codes_t // T).astype(BF16), (codes_t % T).astype(BF16)
    gap = jnp.zeros((16 - K_LOC, T), BF16)
    codes = [block[K_LOC:], row[K_LOC:], weights_t[K_LOC:], told]
    codes += [block[:K_LOC], gap, row[:K_LOC], gap, weights_t[:K_LOC], gap]
    codes = jnp.concatenate(codes, axis=0)
    forward = [[(i, (i + k) % NX) for i in range(NX)] for k in range(NX)]
    codes = jnp.stack([codes] + [lax.ppermute(codes, X, forward[k]) for k in range(1, NX)])
    remote_codes = lax.all_gather(codes[:, :TOLD], Y + ("c",), axis=0)
    told = remote_codes[:, :, 12].astype(jnp.int32)
    sources = jnp.arange(GROUPS, dtype=jnp.int32)[:, None, None]
    group = y * NC + c
    here = jnp.sum(jnp.where(sources == group, told, 0), axis=0)
    start = jnp.sum(jnp.where(sources < group, told[:, :, :GROUPS], 0), axis=0)
    lists = here[:, GROUPS : GROUPS * (1 + CAP)]
    scalars = jnp.concatenate([lists.reshape(-1), start.reshape(-1), here[:, :GROUPS].reshape(-1)])

    def remote_sums(core, blocks):
        (sums,) = vmem_call(
            remote_kernel, "remote_sums", [jnp.concatenate([core[None], x[None], scalars])], [blocks, remote_codes],
            [((NX, NY, T, T), BF16)], flops=300_000_000, bytes_accessed=2_500_000,
        )
        return sums

    received = lax.ppermute(remote_sums(1 - c, blocks), "c", swap)
    keep = remote_sums(c, blocks)
    chip_sum = (keep.astype(F32) + received.astype(F32)).astype(BF16)
    arrived = lax.all_to_all(chip_sum.reshape(NX * NY, T, T), X + Y, 0, 0, tiled=True)

    *near, near_0 = vmem_call(
        local_kernel, "local_sums", [jnp.stack([z, x])], [blocks, codes], [((T, T), F32)] * NX,
        scratch=[pltpu.VMEM((NX, 4 * T, T), BF16), pltpu.VMEM((NX, T, T), F32), pltpu.SemaphoreType.DMA], outside=1,
        flops=600_000_000, bytes_accessed=1_500_000,
    )
    near_0 = pltpu.with_memory_space_constraint(near_0, pltpu.HBM)
    moved = [lax.ppermute(near[k - 1], X, forward[k]) for k in range(1, NX)]

    share = width // OWNERS
    hidden, send, keep = vmem_call(
        dense_kernel, "dense", [jnp.stack([c, x])],
        [arrived.reshape(NX, NY, T, T), *moved, weights_t.astype(F32), features, features_t, w_agg, cotangent],
        [((T, width), BF16), ((OWNERS, NX, share, T), BF16), ((OWNERS, NX, share, T), F32)],
        scratch=[pltpu.VMEM((width, T), BF16), pltpu.VMEM((T, T), F32), pltpu.VMEM((width, width), BF16), pltpu.SemaphoreType.DMA((2,))],
        anywhere=[near_0, w_self], flops=300_000_000, bytes_accessed=5_000_000, transcendentals=65536,
    )
    received = lax.ppermute(send, "c", swap)
    chip_grad = (keep + received.astype(F32)).astype(BF16).reshape(OWNERS, NX * share, T)
    plane = added(lax.all_to_all(chip_grad, ("z",) + X, 0, 0, tiled=True), BF16)
    planes = lax.all_to_all(jnp.broadcast_to(plane, (NY,) + plane.shape), Y, 0, 0, tiled=True)
    grads = lax.all_gather(added(planes, F32), "c", axis=0)
    grads = grads.reshape(NC, NX, share, T).swapaxes(1, 2).reshape(NC, share, width)
    return hidden, grads[0], grads[1]


def solution(mesh):
    axes = ("z",) + X + Y + ("c",)
    fine = Mesh(mesh.devices.reshape(NZ, 2, 2, 2, 2, 2, NC), axes)
    row, rep = ("z",) + X, Y + ("c",)
    nodes = P(row + rep, None)
    in_specs = (nodes, nodes, nodes, P(row, rep, None, None), P(row, rep, None), P(), P(), nodes)
    out_specs = (nodes, P(row, None), P(row, None))
    return jax.shard_map(body, mesh=fine, in_specs=in_specs, out_specs=out_specs, check_vma=False)
```

```python
import jax
import jax.numpy as jnp
from jax import lax
from jax.experimental import pallas as pl
from jax.experimental.pallas import tpu as pltpu
from jax.sharding import Mesh, PartitionSpec as P

NZ, NX, NY, NC = 8, 4, 8, 2
OWNERS = NZ * NX
GROUPS = NY * NC
T = 128
K_LOC = 12
K_REM = 4
CAP = 2
TOLD = 16
X, Y = ("x1", "x0"), ("y2", "y1", "y0")
F32 = jnp.float32
BF16 = jnp.bfloat16
VMEM_LIMIT = 16 * 1024 * 1024


def vmem_call(
    kernel, name, scalar_inputs, array_inputs, outputs, scratch=(), anywhere=(), outside=0, flops=0, bytes_accessed=0, transcendentals=0
):
    vmem = pl.BlockSpec(memory_space=pltpu.VMEM)
    return pl.pallas_call(
        kernel,
        in_specs=[pl.BlockSpec(memory_space=pltpu.SMEM)] * len(scalar_inputs)
        + [pl.BlockSpec(memory_space=pltpu.HBM)] * len(anywhere)
        + [vmem] * len(array_inputs),
        out_specs=[vmem] * (len(outputs) - outside) + [pl.BlockSpec(memory_space=pltpu.HBM)] * outside,
        out_shape=[jax.ShapeDtypeStruct(*of) for of in outputs[: len(outputs) - outside]]
        + [pltpu.HBM(*of) for of in outputs[len(outputs) - outside :]],
        scratch_shapes=list(scratch),
        compiler_params=pltpu.CompilerParams(vmem_limit_bytes=VMEM_LIMIT),
        cost_estimate=pl.CostEstimate(flops=flops, bytes_accessed=bytes_accessed, transcendentals=transcendentals),
        name=name,
    )(*scalar_inputs, *anywhere, *array_inputs)


def spread_kernel(features_ref, features_t, quarters_ref, sems):
    features_t[...] = features_ref[...].astype(F32).T.astype(BF16).reshape(NX, T, T)
    copies = [pltpu.make_async_copy(features_t, quarters_ref.at[z], sems.at[z]) for z in range(NZ)]
    for copy in copies:
        copy.start()
    for copy in copies:
        copy.wait()


def split_kernel(codes_0, codes_1, codes_2, codes_3, remote_ref, local_ref, sems):
    copies = []
    for k, codes in enumerate((codes_0, codes_1, codes_2, codes_3)):
        copies.append(pltpu.make_async_copy(codes.at[TOLD:], local_ref.at[k], sems.at[k]))
        copies[-1].start()
        remote_ref[k] = codes[0:TOLD]
    for copy in copies:
        copy.wait()


def remote_product(scalars, blocks_ref, told_ref, k, y):
    group = y * NC + scalars[0]
    at = k * GROUPS + group
    first = jnp.clip(scalars[2 + at * CAP], 0, OWNERS - 1)
    second = jnp.clip(scalars[3 + at * CAP], 0, OWNERS - 1)
    start = scalars[2 + NX * GROUPS * CAP + at].astype(F32)
    count = scalars[2 + NX * GROUPS * (CAP + 1) + at].astype(F32)
    told = told_ref[group, k].astype(F32)
    entry = told[0:K_REM] - start
    row = jnp.where(entry < count, entry * T + told[K_REM : 2 * K_REM], -1.0).astype(jnp.int16)
    weight = told[2 * K_REM : 3 * K_REM].astype(BF16)
    rows = lax.broadcasted_iota(jnp.int16, (CAP * T, T), 0)
    hot = jnp.zeros((CAP * T, T), BF16)
    for slot in range(K_REM):
        hot = jnp.where(rows == row[slot : slot + 1], weight[slot : slot + 1], hot)
    pair = jnp.concatenate([blocks_ref[first], blocks_ref[second]], axis=1)
    return jnp.dot(pair, hot, preferred_element_type=F32)


def first_kernel(scalars, blocks_ref, told_ref, part_ref):
    for y in range(NY):
        for k in range(NX):
            part_ref[lax.rem(scalars[1] + (NX - k), NX), y] = remote_product(scalars, blocks_ref, told_ref, k, y)


def second_kernel(scalars, blocks_ref, told_ref, part_ref, sums_ref, sums, sems):
    copies = []
    for y in range(NY):
        for k in range(NX):
            x = lax.rem(scalars[1] + (NX - k), NX)
            sums[x, y] = (part_ref[x, y] + remote_product(scalars, blocks_ref, told_ref, k, y)).astype(BF16)
        copies.append(pltpu.make_async_copy(sums.at[:, y], sums_ref.at[:, y], sems.at[y]))
        copies[-1].start()
    for copy in copies:
        copy.wait()


def local_kernel(scalars, codes_ref, blocks_ref, out_1, out_2, out_3, out_0, hot_ref, total, told_ref, sems):
    own_z, own_x = scalars[0], scalars[1]
    copy = pltpu.make_async_copy(codes_ref, told_ref, sems.at[0])
    copy.start()
    rows = lax.broadcasted_iota(jnp.int16, (T, T), 0)
    lanes = lax.broadcasted_iota(jnp.int32, (1, T), 1).astype(F32)
    ones, zeros = jnp.ones((T, T), BF16), jnp.zeros((T, T), BF16)
    total[...] = jnp.zeros_like(total)
    copy.wait()

    def of_four(i, carry):
        for j in range(4):
            p = 4 * i + j
            for k in range(NX):
                block, row, weight = (told_ref[k, n * 16 : n * 16 + 16, :].astype(F32) for n in range(3))
                code = ((block - p.astype(F32)) * T + row).astype(jnp.int16)
                weight = weight.astype(BF16)
                here = p == own_z * NX + lax.rem(own_x + (NX - k), NX)
                own = (lanes - jnp.where(here, 0.0, 1024.0)).astype(jnp.int16)
                hot = jnp.where(rows == own, ones, zeros)
                for slot in range(K_LOC):
                    hot = jnp.where(rows == code[slot : slot + 1], weight[slot : slot + 1], hot)
                hot_ref[k, j * T : (j + 1) * T, :] = hot
        four = jnp.concatenate([blocks_ref[4 * i + j] for j in range(4)], axis=1)
        for k in range(NX):
            total[k] += jnp.dot(four, hot_ref[k], preferred_element_type=F32)
        return carry

    lax.fori_loop(0, OWNERS // 4, of_four, 0, unroll=2)
    copy = pltpu.make_async_copy(total.at[0], out_0, sems.at[1])
    copy.start()
    for k, out in enumerate((out_1, out_2, out_3)):
        out[...] = total[NX - 1 - k]
    copy.wait()


def dense_kernel(
    scalars, near_0, w_self_in, arrived, near_1, near_2, near_3, weights_t, features, features_t, w_agg, cotangent,
    hidden_ref, send_ref, keep_ref, agg_t, near, w_self, sems,
):
    own_c, own_x = scalars[0], scalars[1]
    degree = 1.0 + jnp.sum(weights_t[...], axis=0, keepdims=True)
    copy = pltpu.make_async_copy(near_0, near, sems.at[0])
    copy.start()
    copy_w = pltpu.make_async_copy(w_self_in, w_self, sems.at[1])
    copy_w.start()

    def of_quarter(k, own):
        quarter = lax.rem(own_x + (NX - k), NX)
        summed = own[...]
        for y in range(NY):
            summed = summed + arrived[quarter, y].astype(F32)
        agg_t[pl.ds(pl.multiple_of(quarter * T, T), T), :] = (summed / degree).astype(BF16)

    of_quarter(1, near_1)
    of_quarter(2, near_2)
    of_quarter(3, near_3)
    copy.wait()
    of_quarter(0, near)
    copy_w.wait()
    contract = (((0,), (0,)), ((), ()))
    preact = lax.dot_general(agg_t[...], w_agg[...], contract, preferred_element_type=F32) + jnp.dot(
        features[...], w_self[...], preferred_element_type=F32
    )
    sigma = jax.nn.sigmoid(preact)
    hidden_ref[...] = (preact * sigma).astype(BF16)
    grad_pre = (cotangent[...].astype(F32) * sigma * (1.0 + preact * (1.0 - sigma))).astype(BF16)
    for j in range(NX):
        columns = grad_pre[:, j * T : (j + 1) * T]
        keep_ref[NX + j] = columns
        send_ref[NX + j] = columns
        of_agg, of_self = agg_t[j * T : (j + 1) * T, :], features_t[j]
        keep_ref[j] = jnp.where(own_c == 0, of_agg, of_self)
        send_ref[j] = jnp.where(own_c == 0, of_self, of_agg)


def grad_kernel(keep_ref, received_ref, grad_ref):
    both = (keep_ref, received_ref)
    left = jnp.concatenate([ref[0:NX].reshape(NX * T, T) for ref in both], axis=1)
    for j in range(NX):
        right = jnp.concatenate([ref[NX + j] for ref in both], axis=0)
        product = jnp.dot(left, right, preferred_element_type=F32)
        grad_ref[:, :, j * T : (j + 1) * T] = product.reshape(OWNERS, grad_ref.shape[1], T).astype(BF16)


def add_kernel(parts_ref, sum_ref):
    summed = parts_ref[0].astype(F32)
    for i in range(1, parts_ref.shape[0]):
        summed = summed + parts_ref[i].astype(F32)
    sum_ref[...] = summed.astype(sum_ref.dtype)


def added(parts, dtype):
    (summed,) = vmem_call(
        add_kernel, "added", [], [parts], [(parts.shape[1:], dtype)], flops=parts.size, bytes_accessed=3 * parts.size
    )
    return summed


def body(features, edge_weights, neighbours, send_list, send_count, w_agg, w_self, cotangent):
    width = features.shape[1]
    z, x, y, c = (lax.axis_index(a).astype(jnp.int32) for a in ("z", X, Y, "c"))
    swap = [(0, 1), (1, 0)]

    features_t, quarters = vmem_call(
        spread_kernel, "spread", [], [features], [((NX, T, T), BF16), ((NZ, NX, T, T), BF16)],
        scratch=[pltpu.SemaphoreType.DMA((NZ,))], outside=1, bytes_accessed=1_500_000,
    )
    blocks = lax.all_to_all(quarters.reshape(OWNERS, T, T), ("z",) + X, 0, 0, tiled=True)

    codes_t = neighbours.T
    weights_t = edge_weights.T
    told = jnp.concatenate([send_count[0], send_list[0].reshape(1, GROUPS * CAP)], axis=1).astype(BF16)
    told = jnp.pad(told, ((0, 3), (0, T - GROUPS * (1 + CAP))))
    block, row = (codes_t // T).astype(BF16), (codes_t % T).astype(BF16)
    gap = jnp.zeros((16 - K_LOC, T), BF16)
    of_remote = jnp.concatenate([block[K_LOC:], row[K_LOC:], weights_t[K_LOC:], told], axis=0)
    of_local = jnp.concatenate([block[:K_LOC], gap, row[:K_LOC], gap, weights_t[:K_LOC], gap], axis=0)
    codes = jnp.concatenate([of_remote, of_local], axis=0)
    forward = [[(i, (i + k) % NX) for i in range(NX)] for k in range(NX)]
    codes = [codes] + [lax.ppermute(codes, X, forward[k]) for k in range(1, NX)]
    remote_codes, local_codes = vmem_call(
        split_kernel, "split", [], codes, [((NX, TOLD, T), BF16), ((NX, 48, T), BF16)],
        scratch=[pltpu.SemaphoreType.DMA((NX,))], outside=1, bytes_accessed=100_000,
    )
    remote_codes = lax.all_gather(remote_codes, Y + ("c",), axis=0)
    local_codes = pltpu.with_memory_space_constraint(local_codes, pltpu.HBM)
    blocks, remote_codes = lax.optimization_barrier((blocks, remote_codes))
    told = remote_codes[:, :, 12].astype(jnp.int32)
    sources = jnp.arange(GROUPS, dtype=jnp.int32)[:, None, None]

    def of_source(group):
        here = jnp.sum(jnp.where(sources == group, told, 0), axis=0)
        start = jnp.sum(jnp.where(sources < group, told[:, :, :GROUPS], 0), axis=0)
        lists = here[:, GROUPS : GROUPS * (1 + CAP)]
        return jnp.concatenate([c[None], x[None], lists.reshape(-1), start.reshape(-1), here[:, :GROUPS].reshape(-1)])

    others = lax.ppermute(blocks, "c", swap)
    (part,) = vmem_call(
        first_kernel, "own_group", [of_source(y * NC + c)], [blocks, remote_codes], [((NX, NY, T, T), F32)],
        flops=300_000_000, bytes_accessed=3_500_000,
    )
    (chip_sum,) = vmem_call(
        second_kernel, "other_group", [of_source(y * NC + 1 - c)], [others, remote_codes, part], [((NX, NY, T, T), BF16)],
        scratch=[pltpu.VMEM((NX, NY, T, T), BF16), pltpu.SemaphoreType.DMA((NY,))], outside=1,
        flops=300_000_000, bytes_accessed=5_500_000,
    )
    arrived = lax.all_to_all(chip_sum.reshape(NX * NY, T, T), X + Y, 0, 0, tiled=True)

    *near, near_0 = vmem_call(
        local_kernel, "local_sums", [jnp.stack([z, x])], [blocks], [((T, T), F32)] * NX,
        scratch=[
            pltpu.VMEM((NX, 4 * T, T), BF16), pltpu.VMEM((NX, T, T), F32), pltpu.VMEM((NX, 48, T), BF16), pltpu.SemaphoreType.DMA((2,)),
        ],
        anywhere=[local_codes], outside=1,
        flops=600_000_000, bytes_accessed=1_500_000,
    )
    near_0 = pltpu.with_memory_space_constraint(near_0, pltpu.HBM)
    moved = [lax.ppermute(near[k - 1], X, forward[k]) for k in range(1, NX)]

    share = width // OWNERS
    operands = ((2 * NX, T, T), BF16)
    hidden, send, keep = vmem_call(
        dense_kernel, "dense", [jnp.stack([c, x])],
        [arrived.reshape(NX, NY, T, T), *moved, weights_t.astype(F32), features, features_t, w_agg, cotangent],
        [((T, width), BF16), operands, operands],
        scratch=[pltpu.VMEM((width, T), BF16), pltpu.VMEM((T, T), F32), pltpu.VMEM((width, width), BF16), pltpu.SemaphoreType.DMA((2,))],
        anywhere=[near_0, w_self], flops=150_000_000, bytes_accessed=3_500_000, transcendentals=65536,
    )
    received = lax.ppermute(send, "c", swap)
    (chip_grad,) = vmem_call(
        grad_kernel, "gradient", [], [keep, received], [((OWNERS, share, width), BF16)], flops=300_000_000, bytes_accessed=1_000_000
    )
    plane = added(lax.all_to_all(chip_grad, ("z",) + X, 0, 0, tiled=True), BF16)
    planes = lax.all_to_all(jnp.broadcast_to(plane, (NY,) + plane.shape), Y, 0, 0, tiled=True)
    grads = lax.all_gather(added(planes, F32), "c", axis=0)
    return hidden, grads[0], grads[1]


def solution(mesh):
    axes = ("z",) + X + Y + ("c",)
    fine = Mesh(mesh.devices.reshape(NZ, 2, 2, 2, 2, 2, NC), axes)
    row, rep = ("z",) + X, Y + ("c",)
    nodes = P(row + rep, None)
    in_specs = (nodes, nodes, nodes, P(row, rep, None, None), P(row, rep, None), P(), P(), nodes)
    out_specs = (nodes, P(row, None), P(row, None))
    return jax.shard_map(body, mesh=fine, in_specs=in_specs, out_specs=out_specs, check_vma=False)
```

```python
import functools

import jax
import jax.numpy as jnp
from jax import lax
from jax.experimental import pallas as pl
from jax.experimental.pallas import tpu as pltpu
from jax.sharding import Mesh, PartitionSpec as P

NZ, NX, NY, NC = 8, 4, 8, 2
OWNERS = NZ * NX
GROUPS = NY * NC
T = 128
K_LOC = 12
K_REM = 4
CAP = 2
TOLD = 16
X, Y = ("x1", "x0"), ("y2", "y1", "y0")
F32 = jnp.float32
BF16 = jnp.bfloat16
VMEM_LIMIT = 16 * 1024 * 1024


def vmem_call(
    kernel, name, scalar_inputs, array_inputs, outputs, scratch=(), anywhere=(), outside=0, flops=0, bytes_accessed=0, transcendentals=0
):
    vmem = pl.BlockSpec(memory_space=pltpu.VMEM)
    return pl.pallas_call(
        kernel,
        in_specs=[pl.BlockSpec(memory_space=pltpu.SMEM)] * len(scalar_inputs)
        + [pl.BlockSpec(memory_space=pltpu.HBM)] * len(anywhere)
        + [vmem] * len(array_inputs),
        out_specs=[vmem] * (len(outputs) - outside) + [pl.BlockSpec(memory_space=pltpu.HBM)] * outside,
        out_shape=[jax.ShapeDtypeStruct(*of) for of in outputs[: len(outputs) - outside]]
        + [pltpu.HBM(*of) for of in outputs[len(outputs) - outside :]],
        scratch_shapes=list(scratch),
        compiler_params=pltpu.CompilerParams(vmem_limit_bytes=VMEM_LIMIT),
        cost_estimate=pl.CostEstimate(flops=flops, bytes_accessed=bytes_accessed, transcendentals=transcendentals),
        name=name,
    )(*scalar_inputs, *anywhere, *array_inputs)


def spread_kernel(features_in, features_out, quarters_ref, quarters, features_t, sems_in, sems):
    loads = [pltpu.make_async_copy(features_in.at[:, x * T : (x + 1) * T], quarters.at[x], sems_in.at[x]) for x in range(NX)]
    for load in loads:
        load.start()
    copies = []
    for x in range(NX):
        loads[x].wait()
        features_t[x] = quarters[x].astype(F32).T.astype(BF16)
        for z in range(NZ):
            copies.append(pltpu.make_async_copy(features_t.at[x], quarters_ref.at[z, x], sems.at[x, z]))
            copies[-1].start()
        copies.append(pltpu.make_async_copy(features_t.at[x], features_out.at[x], sems.at[x, NZ]))
        copies[-1].start()
    for copy in copies:
        copy.wait()


def split_kernel(codes_0, codes_1, codes_2, codes_3, remote_ref, local_ref, sems):
    copies = []
    for k, codes in enumerate((codes_0, codes_1, codes_2, codes_3)):
        copies.append(pltpu.make_async_copy(codes.at[TOLD:], local_ref.at[k], sems.at[k]))
        copies[-1].start()
        remote_ref[k] = codes[0:TOLD]
    for copy in copies:
        copy.wait()


def remote_product(own, here, before, blocks_ref, told_ref, k, y):
    group = y * NC + own[0]
    first = jnp.clip(here[k, GROUPS + group * CAP], 0, OWNERS - 1)
    second = jnp.clip(here[k, GROUPS + group * CAP + 1], 0, OWNERS - 1)
    start, count = before[k, group].astype(F32), here[k, group].astype(F32)
    told = told_ref[group, k].astype(F32)
    entry = told[0:K_REM] - start
    row = jnp.where(entry < count, entry * T + told[K_REM : 2 * K_REM], -1.0).astype(jnp.int16)
    weight = told[2 * K_REM : 3 * K_REM].astype(BF16)
    rows = lax.broadcasted_iota(jnp.int16, (CAP * T, T), 0)
    hot = jnp.zeros((CAP * T, T), BF16)
    for slot in range(K_REM):
        hot = jnp.where(rows == row[slot : slot + 1], weight[slot : slot + 1], hot)
    pair = jnp.concatenate([blocks_ref[first], blocks_ref[second]], axis=1)
    return jnp.dot(pair, hot, preferred_element_type=F32)


def first_kernel(own, here, before, blocks_ref, told_ref, part_ref):
    for y in range(NY):
        for k in range(NX):
            part_ref[lax.rem(own[1] + (NX - k), NX), y] = remote_product(own, here, before, blocks_ref, told_ref, k, y)


def second_kernel(own, here, before, blocks_ref, told_ref, part_ref, sums_ref, sums, sems):
    copies = []
    for y in range(NY):
        for k in range(NX):
            x = lax.rem(own[1] + (NX - k), NX)
            sums[x, y] = (part_ref[x, y] + remote_product(own, here, before, blocks_ref, told_ref, k, y)).astype(BF16)
        copies.append(pltpu.make_async_copy(sums.at[:, y], sums_ref.at[:, y], sems.at[y]))
        copies[-1].start()
    for copy in copies:
        copy.wait()


def local_kernel(k, outside, scalars, blocks_ref, told_ref, out, hot_ref, total=None, sem=None):
    owner = scalars[0] * NX + lax.rem(scalars[1] + (NX - k), NX)
    rows = lax.broadcasted_iota(jnp.int16, (T, T), 0)
    lanes = lax.broadcasted_iota(jnp.int32, (1, T), 1).astype(F32)
    ones, zeros = jnp.ones((T, T), BF16), jnp.zeros((T, T), BF16)
    block, row, weight = (told_ref[k, n * 16 : n * 16 + 16, :].astype(F32) for n in range(3))
    weight = weight.astype(BF16)

    def of_four(i, summed):
        for j in range(4):
            p = 4 * i + j
            code = ((block - p.astype(F32)) * T + row).astype(jnp.int16)
            own = (lanes - jnp.where(p == owner, 0.0, 1024.0)).astype(jnp.int16)
            hot = jnp.where(rows == own, ones, zeros)
            for slot in range(K_LOC):
                hot = jnp.where(rows == code[slot : slot + 1], weight[slot : slot + 1], hot)
            hot_ref[j * T : (j + 1) * T, :] = hot
        four = jnp.concatenate([blocks_ref[4 * i + j] for j in range(4)], axis=1)
        return summed + jnp.dot(four, hot_ref[...], preferred_element_type=F32)

    summed = lax.fori_loop(0, OWNERS // 4, of_four, jnp.zeros((T, T), F32), unroll=2)
    if outside:
        total[...] = summed
        copy = pltpu.make_async_copy(total, out, sem)
        copy.start()
        copy.wait()
    else:
        out[...] = summed.astype(out.dtype)


def dense_kernel(
    scalars, near_in, weights_in, w_agg_in, w_self_in, features_in, features_t_in, cotangent_in, arrived, near_1, near_2, near_3,
    hidden_ref, send_ref, keep_ref, agg_t, near_0, weights_t, w_agg, w_self, features, features_t, cotangent, sems,
):
    own_x, own_c = scalars[0], scalars[1]
    sources = (near_in, weights_in, w_agg_in, features_in, w_self_in, cotangent_in, features_t_in)
    targets = (near_0, weights_t, w_agg, features, w_self, cotangent, features_t)
    copies = [pltpu.make_async_copy(of, to, sems.at[i]) for i, (of, to) in enumerate(zip(sources, targets))]
    for copy in copies:
        copy.start()

    def total(k, own):
        quarter = lax.rem(own_x + (NX - k), NX)
        summed = arrived[quarter, 0].astype(F32)
        for y in range(1, NY):
            summed = summed + arrived[quarter, y].astype(F32)
        agg_t[pl.ds(pl.multiple_of(quarter * T, T), T), :] = summed + own[...].astype(F32)

    total(1, near_1)
    total(2, near_2)
    total(3, near_3)
    copies[0].wait()
    total(0, near_0)
    copies[1].wait()
    degree = 1.0 + jnp.sum(weights_t[...].astype(F32), axis=0, keepdims=True)
    aggregate = (agg_t[...] / degree).astype(BF16)
    contract = (((0,), (0,)), ((), ()))
    copies[2].wait()
    preact = lax.dot_general(aggregate, w_agg[...], contract, preferred_element_type=F32)
    copies[3].wait()
    copies[4].wait()
    preact = preact + jnp.dot(features[...], w_self[...], preferred_element_type=F32)
    sigma = jax.nn.sigmoid(preact)
    hidden_ref[...] = (preact * sigma).astype(BF16)
    copies[5].wait()
    grad_pre = (cotangent[...].astype(F32) * sigma * (1.0 + preact * (1.0 - sigma))).astype(BF16)
    copies[6].wait()
    for j in range(NX):
        columns = grad_pre[:, j * T : (j + 1) * T]
        keep_ref[NX + j] = columns
        send_ref[NX + j] = columns
        of_agg, of_self = aggregate[j * T : (j + 1) * T, :], features_t[j]
        keep_ref[j] = jnp.where(own_c == 0, of_agg, of_self)
        send_ref[j] = jnp.where(own_c == 0, of_self, of_agg)


def grad_kernel(keep_ref, received_ref, grad_ref):
    both = (keep_ref, received_ref)
    left = jnp.concatenate([ref[0:NX].reshape(NX * T, T) for ref in both], axis=1)
    for j in range(NX):
        right = jnp.concatenate([ref[NX + j] for ref in both], axis=0)
        product = jnp.dot(left, right, preferred_element_type=F32)
        grad_ref[:, :, j * T : (j + 1) * T] = product.reshape(OWNERS, grad_ref.shape[1], T).astype(BF16)


def add_kernel(parts_ref, sum_ref):
    summed = parts_ref[0].astype(F32)
    for i in range(1, parts_ref.shape[0]):
        summed = summed + parts_ref[i].astype(F32)
    sum_ref[...] = summed.astype(sum_ref.dtype)


def added(parts, dtype):
    (summed,) = vmem_call(
        add_kernel, "added", [], [parts], [(parts.shape[1:], dtype)], flops=parts.size, bytes_accessed=3 * parts.size
    )
    return summed


def body(features, edge_weights, neighbours, send_list, send_count, w_agg, w_self, cotangent):
    width = features.shape[1]
    z, x, y, c = (lax.axis_index(a).astype(jnp.int32) for a in ("z", X, Y, "c"))
    swap = [(0, 1), (1, 0)]

    features_t, quarters = vmem_call(
        spread_kernel, "spread", [], [], [((NX, T, T), BF16), ((NZ, NX, T, T), BF16)],
        scratch=[
            pltpu.VMEM((NX, T, T), BF16), pltpu.VMEM((NX, T, T), BF16),
            pltpu.SemaphoreType.DMA((NX,)), pltpu.SemaphoreType.DMA((NX, NZ + 1)),
        ],
        anywhere=[pltpu.with_memory_space_constraint(features, pltpu.HBM)], outside=2, bytes_accessed=1_500_000,
    )
    blocks = lax.all_to_all(quarters.reshape(OWNERS, T, T), ("z",) + X, 0, 0, tiled=True)

    codes_t = neighbours.T
    weights_t = edge_weights.T
    told = jnp.concatenate([send_count[0], send_list[0].reshape(1, GROUPS * CAP)], axis=1).astype(BF16)
    told = jnp.pad(told, ((0, 3), (0, T - GROUPS * (1 + CAP))))
    block, row = (codes_t // T).astype(BF16), (codes_t % T).astype(BF16)
    gap = jnp.zeros((16 - K_LOC, T), BF16)
    of_remote = jnp.concatenate([block[K_LOC:], row[K_LOC:], weights_t[K_LOC:], told], axis=0)
    of_local = jnp.concatenate([block[:K_LOC], gap, row[:K_LOC], gap, weights_t[:K_LOC], gap], axis=0)
    codes = jnp.concatenate([of_remote, of_local], axis=0)
    forward = [[(i, (i + k) % NX) for i in range(NX)] for k in range(NX)]
    codes = [codes] + [lax.ppermute(codes, X, forward[k]) for k in range(1, NX)]
    remote_codes, local_codes = vmem_call(
        split_kernel, "split", [], codes, [((NX, TOLD, T), BF16), ((NX, 48, T), BF16)],
        scratch=[pltpu.SemaphoreType.DMA((NX,))], outside=1, bytes_accessed=100_000,
    )
    remote_codes = lax.all_gather(remote_codes, Y + ("c",), axis=0)
    blocks, remote_codes = lax.optimization_barrier((blocks, remote_codes))
    told = remote_codes[:, :, 12].astype(jnp.int32)
    sources = jnp.arange(GROUPS, dtype=jnp.int32)[:, None, None]

    def of_source(group):
        here = jnp.sum(jnp.where(sources == group, told, 0), axis=0)
        return here, jnp.sum(jnp.where(sources < group, told[:, :, :GROUPS], 0), axis=0)

    own = jnp.stack([c, x])
    others = lax.ppermute(blocks, "c", swap)
    (part,) = vmem_call(
        first_kernel, "own_group", [own, *of_source(y * NC + c)], [blocks, remote_codes], [((NX, NY, T, T), F32)],
        flops=300_000_000, bytes_accessed=3_500_000,
    )
    (chip_sum,) = vmem_call(
        second_kernel, "other_group", [own, *of_source(y * NC + 1 - c)], [others, remote_codes, part], [((NX, NY, T, T), BF16)],
        scratch=[pltpu.VMEM((NX, NY, T, T), BF16), pltpu.SemaphoreType.DMA((NY,))], outside=1,
        flops=300_000_000, bytes_accessed=5_500_000,
    )
    arrived = lax.all_to_all(chip_sum.reshape(NX * NY, T, T), X + Y, 0, 0, tiled=True)

    near = []
    for k in (2, 1, 3, 0):
        (sums,) = vmem_call(
            functools.partial(local_kernel, k, k == 0), "local_sums", [jnp.stack([z, x])], [blocks, local_codes],
            [((T, T), BF16 if k else F32)],
            scratch=[pltpu.VMEM((4 * T, T), BF16)] + ([] if k else [pltpu.VMEM((T, T), F32), pltpu.SemaphoreType.DMA]),
            outside=int(k == 0), flops=150_000_000, bytes_accessed=1_200_000,
        )
        near.append(lax.ppermute(sums, X, forward[NX - k]) if k else sums)
    two, three, one, near_0 = near

    share = width // OWNERS
    operands = ((2 * NX, T, T), BF16)
    arrived, x, c = lax.optimization_barrier((arrived, x, c))
    outside = [near_0, weights_t, w_agg, w_self, features, features_t, cotangent]
    hidden, send, keep = vmem_call(
        dense_kernel, "dense", [jnp.stack([x, c])], [arrived.reshape(NX, NY, T, T), one, two, three],
        [((T, width), BF16), operands, operands],
        scratch=[pltpu.VMEM((width, T), F32)]
        + [pltpu.VMEM(of.shape, of.dtype) for of in outside]
        + [pltpu.SemaphoreType.DMA((len(outside),))],
        anywhere=[pltpu.with_memory_space_constraint(of, pltpu.HBM) for of in outside],
        flops=150_000_000, bytes_accessed=3_500_000, transcendentals=65536,
    )
    received = lax.ppermute(send, "c", swap)
    (chip_grad,) = vmem_call(
        grad_kernel, "gradient", [], [keep, received], [((OWNERS, share, width), BF16)], flops=300_000_000, bytes_accessed=1_000_000
    )
    plane = added(lax.all_to_all(chip_grad, ("z",) + X, 0, 0, tiled=True), BF16)
    planes = lax.all_to_all(jnp.broadcast_to(plane, (NY,) + plane.shape), Y, 0, 0, tiled=True)
    grads = lax.all_gather(added(planes, F32), "c", axis=0)
    return hidden, grads[0], grads[1]


def solution(mesh):
    axes = ("z",) + X + Y + ("c",)
    fine = Mesh(mesh.devices.reshape(NZ, 2, 2, 2, 2, 2, NC), axes)
    row, rep = ("z",) + X, Y + ("c",)
    nodes = P(row + rep, None)
    in_specs = (nodes, nodes, nodes, P(row, rep, None, None), P(row, rep, None), P(), P(), nodes)
    out_specs = (nodes, P(row, None), P(row, None))
    return jax.shard_map(body, mesh=fine, in_specs=in_specs, out_specs=out_specs, check_vma=False)
```

```python
import functools

import jax
import jax.numpy as jnp
from jax import lax
from jax.experimental import pallas as pl
from jax.experimental.pallas import tpu as pltpu
from jax.sharding import Mesh, PartitionSpec as P

NZ, NX, NY, NC = 8, 4, 8, 2
OWNERS = NZ * NX
GROUPS = NY * NC
T = 128
K_LOC = 12
K_REM = 4
CAP = 2
TOLD = 16
X, Y = ("x1", "x0"), ("y2", "y1", "y0")
F32 = jnp.float32
BF16 = jnp.bfloat16
VMEM_LIMIT = 16 * 1024 * 1024


def vmem_call(
    kernel, name, scalar_inputs, array_inputs, outputs, scratch=(), anywhere=(), outside=0, flops=0, bytes_accessed=0, transcendentals=0
):
    vmem = pl.BlockSpec(memory_space=pltpu.VMEM)
    return pl.pallas_call(
        kernel,
        in_specs=[pl.BlockSpec(memory_space=pltpu.SMEM)] * len(scalar_inputs)
        + [pl.BlockSpec(memory_space=pltpu.HBM)] * len(anywhere)
        + [vmem] * len(array_inputs),
        out_specs=[vmem] * (len(outputs) - outside) + [pl.BlockSpec(memory_space=pltpu.HBM)] * outside,
        out_shape=[jax.ShapeDtypeStruct(*of) for of in outputs[: len(outputs) - outside]]
        + [pltpu.HBM(*of) for of in outputs[len(outputs) - outside :]],
        scratch_shapes=list(scratch),
        compiler_params=pltpu.CompilerParams(vmem_limit_bytes=VMEM_LIMIT),
        cost_estimate=pl.CostEstimate(flops=flops, bytes_accessed=bytes_accessed, transcendentals=transcendentals),
        name=name,
    )(*scalar_inputs, *anywhere, *array_inputs)


def spread_kernel(features_ref, features_out, quarters_ref, features_t, sems):
    features_t[...] = features_ref[...].astype(F32).T.astype(BF16).reshape(NX, T, T)
    copies = [pltpu.make_async_copy(features_t, quarters_ref.at[z], sems.at[z]) for z in range(NZ)]
    copies.append(pltpu.make_async_copy(features_t, features_out, sems.at[NZ]))
    for copy in copies:
        copy.start()
    for copy in copies:
        copy.wait()


def split_kernel(codes_0, codes_1, codes_2, codes_3, remote_ref, local_ref, sems):
    copies = []
    for k, codes in enumerate((codes_0, codes_1, codes_2, codes_3)):
        copies.append(pltpu.make_async_copy(codes.at[TOLD:], local_ref.at[k], sems.at[k]))
        copies[-1].start()
        remote_ref[k] = codes[0:TOLD]
    for copy in copies:
        copy.wait()


def remote_product(own, here, before, blocks_ref, told_ref, k, y):
    group = y * NC + own[0]
    first = jnp.clip(here[k, GROUPS + group * CAP], 0, OWNERS - 1)
    second = jnp.clip(here[k, GROUPS + group * CAP + 1], 0, OWNERS - 1)
    start, count = before[k, group].astype(F32), here[k, group].astype(F32)
    told = told_ref[group, k].astype(F32)
    entry = told[0:K_REM] - start
    row = jnp.where(entry < count, entry * T + told[K_REM : 2 * K_REM], -1.0).astype(jnp.int16)
    weight = told[2 * K_REM : 3 * K_REM].astype(BF16)
    rows = lax.broadcasted_iota(jnp.int16, (CAP * T, T), 0)
    hot = jnp.zeros((CAP * T, T), BF16)
    for slot in range(K_REM):
        hot = jnp.where(rows == row[slot : slot + 1], weight[slot : slot + 1], hot)
    pair = jnp.concatenate([blocks_ref[first], blocks_ref[second]], axis=1)
    return jnp.dot(pair, hot, preferred_element_type=F32)


def first_kernel(own, here, before, blocks_ref, told_ref, part_ref):
    for y in range(NY):
        for k in range(NX):
            part_ref[lax.rem(own[1] + (NX - k), NX), y] = remote_product(own, here, before, blocks_ref, told_ref, k, y)


def second_kernel(own, here, before, blocks_ref, told_ref, part_ref, sums_ref, sums, sems):
    copies = []
    for y in range(NY):
        for k in range(NX):
            x = lax.rem(own[1] + (NX - k), NX)
            sums[x, y] = (part_ref[x, y] + remote_product(own, here, before, blocks_ref, told_ref, k, y)).astype(BF16)
        copies.append(pltpu.make_async_copy(sums.at[:, y], sums_ref.at[:, y], sems.at[y]))
        copies[-1].start()
    for copy in copies:
        copy.wait()


def local_kernel(k, outside, scalars, blocks_ref, told_ref, out, hot_ref, total=None, sem=None):
    owner = scalars[0] * NX + lax.rem(scalars[1] + (NX - k), NX)
    rows = lax.broadcasted_iota(jnp.int16, (T, T), 0)
    lanes = lax.broadcasted_iota(jnp.int32, (1, T), 1).astype(F32)
    ones, zeros = jnp.ones((T, T), BF16), jnp.zeros((T, T), BF16)
    block, row, weight = (told_ref[k, n * 16 : n * 16 + 16, :].astype(F32) for n in range(3))
    weight = weight.astype(BF16)

    def of_four(i, summed):
        for j in range(4):
            p = 4 * i + j
            code = ((block - p.astype(F32)) * T + row).astype(jnp.int16)
            own = (lanes - jnp.where(p == owner, 0.0, 1024.0)).astype(jnp.int16)
            hot = jnp.where(rows == own, ones, zeros)
            for slot in range(K_LOC):
                hot = jnp.where(rows == code[slot : slot + 1], weight[slot : slot + 1], hot)
            hot_ref[j * T : (j + 1) * T, :] = hot
        four = jnp.concatenate([blocks_ref[4 * i + j] for j in range(4)], axis=1)
        return summed + jnp.dot(four, hot_ref[...], preferred_element_type=F32)

    summed = lax.fori_loop(0, OWNERS // 4, of_four, jnp.zeros((T, T), F32), unroll=2)
    if outside:
        total[...] = summed
        copy = pltpu.make_async_copy(total, out, sem)
        copy.start()
        copy.wait()
    else:
        out[...] = summed


def dense_kernel(
    scalars, near_0_in, near_1_in, near_2_in, near_3_in, weights_in, features_t_in, arrived, features, w_agg, w_self, cotangent,
    hidden_ref, send_ref, keep_ref, agg_t, near_0, near_1, near_2, near_3, weights_t, features_t, sems,
):
    own_x, own_c = scalars[0], scalars[1]
    sources = (near_0_in, near_1_in, near_2_in, near_3_in, weights_in, features_t_in)
    targets = (near_0, near_1, near_2, near_3, weights_t, features_t)
    copies = [pltpu.make_async_copy(of, to, sems.at[i]) for i, (of, to) in enumerate(zip(sources, targets))]
    for copy in copies:
        copy.start()

    for x in range(NX):
        summed = arrived[x, 0].astype(F32)
        for y in range(1, NY):
            summed = summed + arrived[x, y].astype(F32)
        agg_t[x * T : (x + 1) * T, :] = summed
    for k, near in enumerate((near_0, near_1, near_2, near_3)):
        copies[k].wait()
        quarter = lax.rem(own_x + (NX - k), NX)
        agg_t[pl.ds(pl.multiple_of(quarter * T, T), T), :] += near[...]
    copies[4].wait()
    degree = 1.0 + jnp.sum(weights_t[...].astype(F32), axis=0, keepdims=True)
    aggregate = (agg_t[...] / degree).astype(BF16)
    contract = (((0,), (0,)), ((), ()))
    preact = lax.dot_general(aggregate, w_agg[...], contract, preferred_element_type=F32)
    preact = preact + jnp.dot(features[...], w_self[...], preferred_element_type=F32)
    sigma = jax.nn.sigmoid(preact)
    hidden_ref[...] = (preact * sigma).astype(BF16)
    grad_pre = (cotangent[...].astype(F32) * sigma * (1.0 + preact * (1.0 - sigma))).astype(BF16)
    copies[5].wait()
    for j in range(NX):
        columns = grad_pre[:, j * T : (j + 1) * T]
        keep_ref[NX + j] = columns
        send_ref[NX + j] = columns
        of_agg, of_self = aggregate[j * T : (j + 1) * T, :], features_t[j]
        keep_ref[j] = jnp.where(own_c == 0, of_agg, of_self)
        send_ref[j] = jnp.where(own_c == 0, of_self, of_agg)


def grad_kernel(keep_ref, received_ref, grad_ref):
    both = (keep_ref, received_ref)
    left = jnp.concatenate([ref[0:NX].reshape(NX * T, T) for ref in both], axis=1)
    for j in range(NX):
        right = jnp.concatenate([ref[NX + j] for ref in both], axis=0)
        product = jnp.dot(left, right, preferred_element_type=F32)
        grad_ref[:, :, j * T : (j + 1) * T] = product.reshape(OWNERS, grad_ref.shape[1], T).astype(BF16)


def add_kernel(parts_ref, sum_ref):
    summed = parts_ref[0].astype(F32)
    for i in range(1, parts_ref.shape[0]):
        summed = summed + parts_ref[i].astype(F32)
    sum_ref[...] = summed.astype(sum_ref.dtype)


def added(parts, dtype):
    (summed,) = vmem_call(
        add_kernel, "added", [], [parts], [(parts.shape[1:], dtype)], flops=parts.size, bytes_accessed=3 * parts.size
    )
    return summed


def body(features, edge_weights, neighbours, send_list, send_count, w_agg, w_self, cotangent):
    width = features.shape[1]
    z, x, y, c = (lax.axis_index(a).astype(jnp.int32) for a in ("z", X, Y, "c"))
    swap = [(0, 1), (1, 0)]

    features_t, quarters = vmem_call(
        spread_kernel, "spread", [], [features], [((NX, T, T), BF16), ((NZ, NX, T, T), BF16)],
        scratch=[pltpu.VMEM((NX, T, T), BF16), pltpu.SemaphoreType.DMA((NZ + 1,))], outside=2, bytes_accessed=1_500_000,
    )
    blocks = lax.all_to_all(quarters.reshape(OWNERS, T, T), ("z",) + X, 0, 0, tiled=True)

    codes_t = neighbours.T
    weights_t = edge_weights.T
    told = jnp.concatenate([send_count[0], send_list[0].reshape(1, GROUPS * CAP)], axis=1).astype(BF16)
    told = jnp.pad(told, ((0, 3), (0, T - GROUPS * (1 + CAP))))
    block, row = (codes_t // T).astype(BF16), (codes_t % T).astype(BF16)
    gap = jnp.zeros((16 - K_LOC, T), BF16)
    of_remote = jnp.concatenate([block[K_LOC:], row[K_LOC:], weights_t[K_LOC:], told], axis=0)
    of_local = jnp.concatenate([block[:K_LOC], gap, row[:K_LOC], gap, weights_t[:K_LOC], gap], axis=0)
    codes = jnp.concatenate([of_remote, of_local], axis=0)
    forward = [[(i, (i + k) % NX) for i in range(NX)] for k in range(NX)]
    codes = [codes] + [lax.ppermute(codes, X, forward[k]) for k in range(1, NX)]
    remote_codes, local_codes = vmem_call(
        split_kernel, "split", [], codes, [((NX, TOLD, T), BF16), ((NX, 48, T), BF16)],
        scratch=[pltpu.SemaphoreType.DMA((NX,))], outside=1, bytes_accessed=100_000,
    )
    remote_codes = lax.all_gather(remote_codes, Y + ("c",), axis=0)
    blocks, remote_codes = lax.optimization_barrier((blocks, remote_codes))
    told = remote_codes[:, :, 12].astype(jnp.int32)
    sources = jnp.arange(GROUPS, dtype=jnp.int32)[:, None, None]

    def of_source(group):
        here = jnp.sum(jnp.where(sources == group, told, 0), axis=0)
        return here, jnp.sum(jnp.where(sources < group, told[:, :, :GROUPS], 0), axis=0)

    own = jnp.stack([c, x])
    others = lax.ppermute(blocks, "c", swap)
    (part,) = vmem_call(
        first_kernel, "own_group", [own, *of_source(y * NC + c)], [blocks, remote_codes], [((NX, NY, T, T), F32)],
        flops=300_000_000, bytes_accessed=3_500_000,
    )
    (chip_sum,) = vmem_call(
        second_kernel, "other_group", [own, *of_source(y * NC + 1 - c)], [others, remote_codes, part], [((NX, NY, T, T), BF16)],
        scratch=[pltpu.VMEM((NX, NY, T, T), BF16), pltpu.SemaphoreType.DMA((NY,))], outside=1,
        flops=300_000_000, bytes_accessed=5_500_000,
    )
    arrived = lax.all_to_all(chip_sum.reshape(NX * NY, T, T), X + Y, 0, 0, tiled=True)

    near = []
    for k in (2, 1, 3, 0):
        (sums,) = vmem_call(
            functools.partial(local_kernel, k, k == 0), "local_sums", [jnp.stack([z, x])], [blocks, local_codes],
            [((T, T), F32)],
            scratch=[pltpu.VMEM((4 * T, T), BF16)] + ([] if k else [pltpu.VMEM((T, T), F32), pltpu.SemaphoreType.DMA]),
            outside=int(k == 0), flops=150_000_000, bytes_accessed=1_200_000,
        )
        near.append(lax.ppermute(sums, X, forward[NX - k]) if k else sums)
    two, three, one, near_0 = near

    share = width // OWNERS
    operands = ((2 * NX, T, T), BF16)
    arrived, x, c = lax.optimization_barrier((arrived, x, c))
    outside = [near_0, one, two, three, weights_t, features_t]
    hidden, send, keep = vmem_call(
        dense_kernel, "dense", [jnp.stack([x, c])], [arrived.reshape(NX, NY, T, T), features, w_agg, w_self, cotangent],
        [((T, width), BF16), operands, operands],
        scratch=[pltpu.VMEM((width, T), F32)]
        + [pltpu.VMEM(of.shape, of.dtype) for of in outside]
        + [pltpu.SemaphoreType.DMA((len(outside),))],
        anywhere=[pltpu.with_memory_space_constraint(of, pltpu.HBM) for of in outside],
        flops=150_000_000, bytes_accessed=3_500_000, transcendentals=65536,
    )
    received = lax.ppermute(send, "c", swap)
    (chip_grad,) = vmem_call(
        grad_kernel, "gradient", [], [keep, received], [((OWNERS, share, width), BF16)], flops=300_000_000, bytes_accessed=1_000_000
    )
    plane = added(lax.all_to_all(chip_grad, ("z",) + X, 0, 0, tiled=True), BF16)
    planes = lax.all_to_all(jnp.broadcast_to(plane, (NY,) + plane.shape), Y, 0, 0, tiled=True)
    grads = lax.all_gather(added(planes, F32), "c", axis=0)
    return hidden, grads[0], grads[1]


def solution(mesh):
    axes = ("z",) + X + Y + ("c",)
    fine = Mesh(mesh.devices.reshape(NZ, 2, 2, 2, 2, 2, NC), axes)
    row, rep = ("z",) + X, Y + ("c",)
    nodes = P(row + rep, None)
    in_specs = (nodes, nodes, nodes, P(row, rep, None, None), P(row, rep, None), P(), P(), nodes)
    out_specs = (nodes, P(row, None), P(row, None))
    return jax.shard_map(body, mesh=fine, in_specs=in_specs, out_specs=out_specs, check_vma=False)
```

```python
import functools

import jax
import jax.numpy as jnp
from jax import lax
from jax.experimental import pallas as pl
from jax.experimental.pallas import tpu as pltpu
from jax.sharding import Mesh, PartitionSpec as P

NZ, NX, NY, NC = 8, 4, 8, 2
OWNERS = NZ * NX
GROUPS = NY * NC
T = 128
K_LOC = 12
K_REM = 4
CAP = 2
TOLD = 16
X, Y = ("x1", "x0"), ("y2", "y1", "y0")
F32 = jnp.float32
BF16 = jnp.bfloat16
VMEM_LIMIT = 16 * 1024 * 1024


def vmem_call(
    kernel, name, scalar_inputs, array_inputs, outputs, scratch=(), anywhere=(), outside=0, flops=0, bytes_accessed=0, transcendentals=0
):
    vmem = pl.BlockSpec(memory_space=pltpu.VMEM)
    return pl.pallas_call(
        kernel,
        in_specs=[pl.BlockSpec(memory_space=pltpu.SMEM)] * len(scalar_inputs)
        + [pl.BlockSpec(memory_space=pltpu.HBM)] * len(anywhere)
        + [vmem] * len(array_inputs),
        out_specs=[vmem] * (len(outputs) - outside) + [pl.BlockSpec(memory_space=pltpu.HBM)] * outside,
        out_shape=[jax.ShapeDtypeStruct(*of) for of in outputs[: len(outputs) - outside]]
        + [pltpu.HBM(*of) for of in outputs[len(outputs) - outside :]],
        scratch_shapes=list(scratch),
        compiler_params=pltpu.CompilerParams(vmem_limit_bytes=VMEM_LIMIT),
        cost_estimate=pl.CostEstimate(flops=flops, bytes_accessed=bytes_accessed, transcendentals=transcendentals),
        name=name,
    )(*scalar_inputs, *anywhere, *array_inputs)


def spread_kernel(features_ref, features_out, quarters_ref, features_t, sems):
    features_t[...] = features_ref[...].astype(F32).T.astype(BF16).reshape(NX, T, T)
    copies = [pltpu.make_async_copy(features_t, quarters_ref.at[z], sems.at[z]) for z in range(NZ)]
    copies.append(pltpu.make_async_copy(features_t, features_out, sems.at[NZ]))
    for copy in copies:
        copy.start()
    for copy in copies:
        copy.wait()


def split_kernel(codes_ref, remote_ref, local_ref, sems):
    copies = []
    for x in range(NX):
        codes = codes_ref.at[x % 2, x // 2]
        copies.append(pltpu.make_async_copy(codes.at[TOLD:], local_ref.at[x], sems.at[x]))
        copies[-1].start()
        remote_ref[x] = codes[0:TOLD]
    for copy in copies:
        copy.wait()


def remote_product(core, here, before, blocks_ref, told_ref, x, y):
    group = y * NC + core[0]
    first = jnp.clip(here[x, GROUPS + group * CAP], 0, OWNERS - 1)
    second = jnp.clip(here[x, GROUPS + group * CAP + 1], 0, OWNERS - 1)
    start, count = before[x, group].astype(F32), here[x, group].astype(F32)
    told = told_ref[group, x].astype(F32)
    entry = told[0:K_REM] - start
    row = jnp.where(entry < count, entry * T + told[K_REM : 2 * K_REM], -1.0).astype(jnp.int16)
    weight = told[2 * K_REM : 3 * K_REM].astype(BF16)
    rows = lax.broadcasted_iota(jnp.int16, (CAP * T, T), 0)
    hot = jnp.zeros((CAP * T, T), BF16)
    for slot in range(K_REM):
        hot = jnp.where(rows == row[slot : slot + 1], weight[slot : slot + 1], hot)
    pair = jnp.concatenate([blocks_ref[first], blocks_ref[second]], axis=1)
    return jnp.dot(pair, hot, preferred_element_type=F32)


def first_kernel(core, here, before, blocks_ref, told_ref, part_ref):
    for y in range(NY):
        for x in range(NX):
            part_ref[x, y] = remote_product(core, here, before, blocks_ref, told_ref, x, y)


def second_kernel(core, here, before, blocks_ref, told_ref, part_ref, sums_ref, sums, sems):
    copies = []
    for y in range(NY):
        for x in range(NX):
            sums[x, y] = (part_ref[x, y] + remote_product(core, here, before, blocks_ref, told_ref, x, y)).astype(BF16)
        copies.append(pltpu.make_async_copy(sums.at[:, y], sums_ref.at[:, y], sems.at[y]))
        copies[-1].start()
    for copy in copies:
        copy.wait()


def local_kernel(k, outside, scalars, blocks_ref, told_ref, out, hot_ref, total=None, sem=None):
    x = lax.rem(scalars[1] + (NX - k), NX)
    owner = scalars[0] * NX + x
    rows = lax.broadcasted_iota(jnp.int16, (T, T), 0)
    lanes = lax.broadcasted_iota(jnp.int32, (1, T), 1).astype(F32)
    ones, zeros = jnp.ones((T, T), BF16), jnp.zeros((T, T), BF16)
    block, row, weight = (told_ref[x, n * 16 : n * 16 + 16, :].astype(F32) for n in range(3))
    weight = weight.astype(BF16)

    def of_four(i, summed):
        for j in range(4):
            p = 4 * i + j
            code = ((block - p.astype(F32)) * T + row).astype(jnp.int16)
            own = (lanes - jnp.where(p == owner, 0.0, 1024.0)).astype(jnp.int16)
            hot = jnp.where(rows == own, ones, zeros)
            for slot in range(K_LOC):
                hot = jnp.where(rows == code[slot : slot + 1], weight[slot : slot + 1], hot)
            hot_ref[j * T : (j + 1) * T, :] = hot
        four = jnp.concatenate([blocks_ref[4 * i + j] for j in range(4)], axis=1)
        return summed + jnp.dot(four, hot_ref[...], preferred_element_type=F32)

    summed = lax.fori_loop(0, OWNERS // 4, of_four, jnp.zeros((T, T), F32), unroll=2)
    if outside:
        total[...] = summed
        copy = pltpu.make_async_copy(total, out, sem)
        copy.start()
        copy.wait()
    else:
        out[...] = summed


def dense_kernel(
    scalars, near_0_in, near_1_in, near_2_in, near_3_in, weights_in, features_t_in, arrived, features, w_agg, w_self, cotangent,
    hidden_ref, send_ref, keep_ref, agg_t, near_0, near_1, near_2, near_3, weights_t, features_t, sems,
):
    own_x, own_c = scalars[0], scalars[1]
    sources = (near_0_in, near_1_in, near_2_in, near_3_in, weights_in, features_t_in)
    targets = (near_0, near_1, near_2, near_3, weights_t, features_t)
    copies = [pltpu.make_async_copy(of, to, sems.at[i]) for i, (of, to) in enumerate(zip(sources, targets))]
    for copy in copies:
        copy.start()

    for x in range(NX):
        summed = arrived[x, 0].astype(F32)
        for y in range(1, NY):
            summed = summed + arrived[x, y].astype(F32)
        agg_t[x * T : (x + 1) * T, :] = summed
    for k, near in enumerate((near_0, near_1, near_2, near_3)):
        copies[k].wait()
        quarter = lax.rem(own_x + (NX - k), NX)
        agg_t[pl.ds(pl.multiple_of(quarter * T, T), T), :] += near[...]
    copies[4].wait()
    degree = 1.0 + jnp.sum(weights_t[...].astype(F32), axis=0, keepdims=True)
    aggregate = (agg_t[...] / degree).astype(BF16)
    contract = (((0,), (0,)), ((), ()))
    preact = lax.dot_general(aggregate, w_agg[...], contract, preferred_element_type=F32)
    preact = preact + jnp.dot(features[...], w_self[...], preferred_element_type=F32)
    sigma = jax.nn.sigmoid(preact)
    hidden_ref[...] = (preact * sigma).astype(BF16)
    grad_pre = (cotangent[...].astype(F32) * sigma * (1.0 + preact * (1.0 - sigma))).astype(BF16)
    copies[5].wait()
    for j in range(NX):
        columns = grad_pre[:, j * T : (j + 1) * T]
        keep_ref[NX + j] = columns
        send_ref[NX + j] = columns
        of_agg, of_self = aggregate[j * T : (j + 1) * T, :], features_t[j]
        keep_ref[j] = jnp.where(own_c == 0, of_agg, of_self)
        send_ref[j] = jnp.where(own_c == 0, of_self, of_agg)


def grad_kernel(keep_ref, received_ref, grad_ref):
    both = (keep_ref, received_ref)
    left = jnp.concatenate([ref[0:NX].reshape(NX * T, T) for ref in both], axis=1)
    for j in range(NX):
        right = jnp.concatenate([ref[NX + j] for ref in both], axis=0)
        product = jnp.dot(left, right, preferred_element_type=F32)
        grad_ref[:, :, j * T : (j + 1) * T] = product.reshape(OWNERS, grad_ref.shape[1], T).astype(BF16)


def add_kernel(parts_ref, sum_ref):
    summed = parts_ref[0].astype(F32)
    for i in range(1, parts_ref.shape[0]):
        summed = summed + parts_ref[i].astype(F32)
    sum_ref[...] = summed.astype(sum_ref.dtype)


def added(parts, dtype):
    (summed,) = vmem_call(
        add_kernel, "added", [], [parts], [(parts.shape[1:], dtype)], flops=parts.size, bytes_accessed=3 * parts.size
    )
    return summed


def body(features, edge_weights, neighbours, send_list, send_count, w_agg, w_self, cotangent):
    width = features.shape[1]
    z, x, y, c = (lax.axis_index(a).astype(jnp.int32) for a in ("z", X, Y, "c"))
    swap = [(0, 1), (1, 0)]

    features_t, quarters = vmem_call(
        spread_kernel, "spread", [], [features], [((NX, T, T), BF16), ((NZ, NX, T, T), BF16)],
        scratch=[pltpu.VMEM((NX, T, T), BF16), pltpu.SemaphoreType.DMA((NZ + 1,))], outside=2, bytes_accessed=1_500_000,
    )
    blocks = lax.all_to_all(quarters.reshape(OWNERS, T, T), ("z",) + X, 0, 0, tiled=True)

    codes_t = neighbours.T
    weights_t = edge_weights.T
    told = jnp.concatenate([send_count[0], send_list[0].reshape(1, GROUPS * CAP)], axis=1).astype(BF16)
    told = jnp.pad(told, ((0, 3), (0, T - GROUPS * (1 + CAP))))
    block, row = (codes_t // T).astype(BF16), (codes_t % T).astype(BF16)
    gap = jnp.zeros((16 - K_LOC, T), BF16)
    of_remote = jnp.concatenate([block[K_LOC:], row[K_LOC:], weights_t[K_LOC:], told], axis=0)
    of_local = jnp.concatenate([block[:K_LOC], gap, row[:K_LOC], gap, weights_t[:K_LOC], gap], axis=0)
    codes = jnp.concatenate([of_remote, of_local], axis=0)
    forward = [[(i, (i + k) % NX) for i in range(NX)] for k in range(NX)]
    codes = lax.all_gather(lax.all_gather(codes, "x1", axis=0), "x0", axis=0)
    remote_codes, local_codes = vmem_call(
        split_kernel, "split", [], [codes], [((NX, TOLD, T), BF16), ((NX, 48, T), BF16)],
        scratch=[pltpu.SemaphoreType.DMA((NX,))], outside=1, bytes_accessed=100_000,
    )
    remote_codes = lax.all_gather(remote_codes, Y + ("c",), axis=0)
    blocks, remote_codes = lax.optimization_barrier((blocks, remote_codes))
    told = remote_codes[:, :, 12].astype(jnp.int32)
    sources = jnp.arange(GROUPS, dtype=jnp.int32)[:, None, None]

    def of_source(group):
        here = jnp.sum(jnp.where(sources == group, told, 0), axis=0)
        return here, jnp.sum(jnp.where(sources < group, told[:, :, :GROUPS], 0), axis=0)

    core = c[None]
    others = lax.ppermute(blocks, "c", swap)
    (part,) = vmem_call(
        first_kernel, "own_group", [core, *of_source(y * NC + c)], [blocks, remote_codes], [((NX, NY, T, T), F32)],
        flops=300_000_000, bytes_accessed=3_500_000,
    )
    (chip_sum,) = vmem_call(
        second_kernel, "other_group", [core, *of_source(y * NC + 1 - c)], [others, remote_codes, part], [((NX, NY, T, T), BF16)],
        scratch=[pltpu.VMEM((NX, NY, T, T), BF16), pltpu.SemaphoreType.DMA((NY,))], outside=1,
        flops=300_000_000, bytes_accessed=5_500_000,
    )
    arrived = lax.all_to_all(chip_sum.reshape(NX * NY, T, T), X + Y, 0, 0, tiled=True)

    near = []
    for k in (2, 1, 3, 0):
        (sums,) = vmem_call(
            functools.partial(local_kernel, k, k == 0), "local_sums", [jnp.stack([z, x])], [blocks, local_codes],
            [((T, T), F32)],
            scratch=[pltpu.VMEM((4 * T, T), BF16)] + ([] if k else [pltpu.VMEM((T, T), F32), pltpu.SemaphoreType.DMA]),
            outside=int(k == 0), flops=150_000_000, bytes_accessed=1_200_000,
        )
        near.append(lax.ppermute(sums, X, forward[NX - k]) if k else sums)
    two, three, one, near_0 = near

    share = width // OWNERS
    operands = ((2 * NX, T, T), BF16)
    arrived, x, c = lax.optimization_barrier((arrived, x, c))
    outside = [near_0, one, two, three, weights_t, features_t]
    hidden, send, keep = vmem_call(
        dense_kernel, "dense", [jnp.stack([x, c])], [arrived.reshape(NX, NY, T, T), features, w_agg, w_self, cotangent],
        [((T, width), BF16), operands, operands],
        scratch=[pltpu.VMEM((width, T), F32)]
        + [pltpu.VMEM(of.shape, of.dtype) for of in outside]
        + [pltpu.SemaphoreType.DMA((len(outside),))],
        anywhere=[pltpu.with_memory_space_constraint(of, pltpu.HBM) for of in outside],
        flops=150_000_000, bytes_accessed=3_500_000, transcendentals=65536,
    )
    received = lax.ppermute(send, "c", swap)
    (chip_grad,) = vmem_call(
        grad_kernel, "gradient", [], [keep, received], [((OWNERS, share, width), BF16)], flops=300_000_000, bytes_accessed=1_000_000
    )
    plane = added(lax.all_to_all(chip_grad, ("z",) + X, 0, 0, tiled=True), BF16)
    planes = lax.all_to_all(jnp.broadcast_to(plane, (NY,) + plane.shape), Y, 0, 0, tiled=True)
    grads = lax.all_gather(added(planes, F32), "c", axis=0)
    return hidden, grads[0], grads[1]


def solution(mesh):
    axes = ("z",) + X + Y + ("c",)
    fine = Mesh(mesh.devices.reshape(NZ, 2, 2, 2, 2, 2, NC), axes)
    row, rep = ("z",) + X, Y + ("c",)
    nodes = P(row + rep, None)
    in_specs = (nodes, nodes, nodes, P(row, rep, None, None), P(row, rep, None), P(), P(), nodes)
    out_specs = (nodes, P(row, None), P(row, None))
    return jax.shard_map(body, mesh=fine, in_specs=in_specs, out_specs=out_specs, check_vma=False)
```

```python
import functools

import jax
import jax.numpy as jnp
from jax import lax
from jax.experimental import pallas as pl
from jax.experimental.pallas import tpu as pltpu
from jax.sharding import Mesh, PartitionSpec as P

NZ, NX, NY, NC = 8, 4, 8, 2
OWNERS = NZ * NX
GROUPS = NY * NC
T = 128
K_LOC = 12
K_REM = 4
CAP = 2
TOLD = 16
X, Y = ("x1", "x0"), ("y2", "y1", "y0")
F32 = jnp.float32
BF16 = jnp.bfloat16
VMEM_LIMIT = 16 * 1024 * 1024


def vmem_call(
    kernel, name, scalar_inputs, array_inputs, outputs, scratch=(), anywhere=(), outside=0, flops=0, bytes_accessed=0, transcendentals=0
):
    vmem = pl.BlockSpec(memory_space=pltpu.VMEM)
    return pl.pallas_call(
        kernel,
        in_specs=[pl.BlockSpec(memory_space=pltpu.SMEM)] * len(scalar_inputs)
        + [pl.BlockSpec(memory_space=pltpu.HBM)] * len(anywhere)
        + [vmem] * len(array_inputs),
        out_specs=[vmem] * (len(outputs) - outside) + [pl.BlockSpec(memory_space=pltpu.HBM)] * outside,
        out_shape=[jax.ShapeDtypeStruct(*of) for of in outputs[: len(outputs) - outside]]
        + [pltpu.HBM(*of) for of in outputs[len(outputs) - outside :]],
        scratch_shapes=list(scratch),
        compiler_params=pltpu.CompilerParams(vmem_limit_bytes=VMEM_LIMIT),
        cost_estimate=pl.CostEstimate(flops=flops, bytes_accessed=bytes_accessed, transcendentals=transcendentals),
        name=name,
    )(*scalar_inputs, *anywhere, *array_inputs)


def spread_kernel(features_ref, features_out, quarters_ref, features_t, sems):
    features_t[...] = features_ref[...].astype(F32).T.astype(BF16).reshape(NX, T, T)
    copies = [pltpu.make_async_copy(features_t, quarters_ref.at[z], sems.at[z]) for z in range(NZ)]
    copies.append(pltpu.make_async_copy(features_t, features_out, sems.at[NZ]))
    for copy in copies:
        copy.start()
    for copy in copies:
        copy.wait()


def split_kernel(scalars, codes_ref, remote_ref, local_ref, sems):
    copies = []
    for x in range(NX):
        codes = codes_ref.at[x % 2, lax.rem(x // 2 + scalars[0], 2)]
        copies.append(pltpu.make_async_copy(codes.at[TOLD:], local_ref.at[x], sems.at[x]))
        copies[-1].start()
        remote_ref[x] = codes[0:TOLD]
    for copy in copies:
        copy.wait()


def remote_product(core, here, before, blocks_ref, told_ref, x, y):
    group = y * NC + core[0]
    first = jnp.clip(here[x, GROUPS + group * CAP], 0, OWNERS - 1)
    second = jnp.clip(here[x, GROUPS + group * CAP + 1], 0, OWNERS - 1)
    start, count = before[x, group].astype(F32), here[x, group].astype(F32)
    told = told_ref[group, x].astype(F32)
    entry = told[0:K_REM] - start
    row = jnp.where(entry < count, entry * T + told[K_REM : 2 * K_REM], -1.0).astype(jnp.int16)
    weight = told[2 * K_REM : 3 * K_REM].astype(BF16)
    rows = lax.broadcasted_iota(jnp.int16, (CAP * T, T), 0)
    hot = jnp.zeros((CAP * T, T), BF16)
    for slot in range(K_REM):
        hot = jnp.where(rows == row[slot : slot + 1], weight[slot : slot + 1], hot)
    pair = jnp.concatenate([blocks_ref[first], blocks_ref[second]], axis=1)
    return jnp.dot(pair, hot, preferred_element_type=F32)


def first_kernel(core, here, before, blocks_ref, told_ref, part_ref):
    for y in range(NY):
        for x in range(NX):
            part_ref[x, y] = remote_product(core, here, before, blocks_ref, told_ref, x, y)


def second_kernel(core, here, before, blocks_ref, told_ref, part_ref, sums_ref, sums, sems):
    copies = []
    for y in range(NY):
        for x in range(NX):
            sums[x, y] = (part_ref[x, y] + remote_product(core, here, before, blocks_ref, told_ref, x, y)).astype(BF16)
        copies.append(pltpu.make_async_copy(sums.at[:, y], sums_ref.at[:, y], sems.at[y]))
        copies[-1].start()
    for copy in copies:
        copy.wait()


def local_kernel(k, outside, scalars, blocks_ref, told_ref, out, hot_ref, total=None, sem=None):
    x = lax.rem(scalars[1] + (NX - k), NX)
    owner = scalars[0] * NX + x
    rows = lax.broadcasted_iota(jnp.int16, (T, T), 0)
    lanes = lax.broadcasted_iota(jnp.int32, (1, T), 1).astype(F32)
    ones, zeros = jnp.ones((T, T), BF16), jnp.zeros((T, T), BF16)
    block, row, weight = (told_ref[x, n * 16 : n * 16 + 16, :].astype(F32) for n in range(3))
    weight = weight.astype(BF16)

    def of_four(i, summed):
        for j in range(4):
            p = 4 * i + j
            code = ((block - p.astype(F32)) * T + row).astype(jnp.int16)
            own = (lanes - jnp.where(p == owner, 0.0, 1024.0)).astype(jnp.int16)
            hot = jnp.where(rows == own, ones, zeros)
            for slot in range(K_LOC):
                hot = jnp.where(rows == code[slot : slot + 1], weight[slot : slot + 1], hot)
            hot_ref[j * T : (j + 1) * T, :] = hot
        four = jnp.concatenate([blocks_ref[4 * i + j] for j in range(4)], axis=1)
        return summed + jnp.dot(four, hot_ref[...], preferred_element_type=F32)

    summed = lax.fori_loop(0, OWNERS // 4, of_four, jnp.zeros((T, T), F32), unroll=2)
    if outside:
        total[...] = summed
        copy = pltpu.make_async_copy(total, out, sem)
        copy.start()
        copy.wait()
    else:
        out[...] = summed


def dense_kernel(
    scalars, near_0_in, near_1_in, near_2_in, near_3_in, weights_in, features_t_in, arrived, features, w_agg, w_self, cotangent,
    hidden_ref, send_ref, keep_ref, agg_t, near_0, near_1, near_2, near_3, weights_t, features_t, sems,
):
    own_x, own_c = scalars[0], scalars[1]
    sources = (near_0_in, near_1_in, near_2_in, near_3_in, weights_in, features_t_in)
    targets = (near_0, near_1, near_2, near_3, weights_t, features_t)
    copies = [pltpu.make_async_copy(of, to, sems.at[i]) for i, (of, to) in enumerate(zip(sources, targets))]
    for copy in copies:
        copy.start()

    for x in range(NX):
        summed = arrived[x, 0].astype(F32)
        for y in range(1, NY):
            summed = summed + arrived[x, y].astype(F32)
        agg_t[x * T : (x + 1) * T, :] = summed
    for k, near in enumerate((near_0, near_1, near_2, near_3)):
        copies[k].wait()
        quarter = lax.rem(own_x + (NX - k), NX)
        agg_t[pl.ds(pl.multiple_of(quarter * T, T), T), :] += near[...]
    copies[4].wait()
    degree = 1.0 + jnp.sum(weights_t[...].astype(F32), axis=0, keepdims=True)
    aggregate = (agg_t[...] / degree).astype(BF16)
    contract = (((0,), (0,)), ((), ()))
    preact = lax.dot_general(aggregate, w_agg[...], contract, preferred_element_type=F32)
    preact = preact + jnp.dot(features[...], w_self[...], preferred_element_type=F32)
    sigma = jax.nn.sigmoid(preact)
    hidden_ref[...] = (preact * sigma).astype(BF16)
    grad_pre = (cotangent[...].astype(F32) * sigma * (1.0 + preact * (1.0 - sigma))).astype(BF16)
    copies[5].wait()
    for j in range(NX):
        columns = grad_pre[:, j * T : (j + 1) * T]
        keep_ref[NX + j] = columns
        send_ref[NX + j] = columns
        of_agg, of_self = aggregate[j * T : (j + 1) * T, :], features_t[j]
        keep_ref[j] = jnp.where(own_c == 0, of_agg, of_self)
        send_ref[j] = jnp.where(own_c == 0, of_self, of_agg)


def grad_kernel(keep_ref, received_ref, grad_ref):
    both = (keep_ref, received_ref)
    left = jnp.concatenate([ref[0:NX].reshape(NX * T, T) for ref in both], axis=1)
    for j in range(NX):
        right = jnp.concatenate([ref[NX + j] for ref in both], axis=0)
        product = jnp.dot(left, right, preferred_element_type=F32)
        grad_ref[:, :, j * T : (j + 1) * T] = product.reshape(OWNERS, grad_ref.shape[1], T).astype(BF16)


def add_kernel(parts_ref, sum_ref):
    summed = parts_ref[0].astype(F32)
    for i in range(1, parts_ref.shape[0]):
        summed = summed + parts_ref[i].astype(F32)
    sum_ref[...] = summed.astype(sum_ref.dtype)


def added(parts, dtype):
    (summed,) = vmem_call(
        add_kernel, "added", [], [parts], [(parts.shape[1:], dtype)], flops=parts.size, bytes_accessed=3 * parts.size
    )
    return summed


def body(features, edge_weights, neighbours, send_list, send_count, w_agg, w_self, cotangent):
    width = features.shape[1]
    z, x, y, c = (lax.axis_index(a).astype(jnp.int32) for a in ("z", X, Y, "c"))
    swap = [(0, 1), (1, 0)]

    codes_t = neighbours.T
    weights_t = edge_weights.T
    told = jnp.concatenate([send_count[0], send_list[0].reshape(1, GROUPS * CAP)], axis=1).astype(BF16)
    told = jnp.pad(told, ((0, 3), (0, T - GROUPS * (1 + CAP))))
    block, row = (codes_t // T).astype(BF16), (codes_t % T).astype(BF16)
    gap = jnp.zeros((16 - K_LOC, T), BF16)
    of_remote = jnp.concatenate([block[K_LOC:], row[K_LOC:], weights_t[K_LOC:], told], axis=0)
    of_local = jnp.concatenate([block[:K_LOC], gap, row[:K_LOC], gap, weights_t[:K_LOC], gap], axis=0)
    codes = jnp.concatenate([of_remote, of_local], axis=0)
    features_after, codes = lax.optimization_barrier((features, codes))
    features_t, quarters = vmem_call(
        spread_kernel, "spread", [], [features_after], [((NX, T, T), BF16), ((NZ, NX, T, T), BF16)],
        scratch=[pltpu.VMEM((NX, T, T), BF16), pltpu.SemaphoreType.DMA((NZ + 1,))], outside=2, bytes_accessed=1_500_000,
    )
    beside = lax.ppermute(codes, "x1", swap)
    quarters, beside = lax.optimization_barrier((quarters, beside))
    blocks = lax.all_to_all(quarters.reshape(OWNERS, T, T), ("z",) + X, 0, 0, tiled=True)
    forward = [[(i, (i + k) % NX) for i in range(NX)] for k in range(NX)]
    codes = lax.all_gather(jnp.stack([codes, beside]), "x0", axis=0)
    remote_codes, local_codes = vmem_call(
        split_kernel, "split", [lax.axis_index("x1").astype(jnp.int32)[None]], [codes], [((NX, TOLD, T), BF16), ((NX, 48, T), BF16)],
        scratch=[pltpu.SemaphoreType.DMA((NX,))], outside=1, bytes_accessed=100_000,
    )
    remote_codes = lax.all_gather(remote_codes, Y + ("c",), axis=0)
    blocks, remote_codes = lax.optimization_barrier((blocks, remote_codes))
    told = remote_codes[:, :, 12].astype(jnp.int32)
    sources = jnp.arange(GROUPS, dtype=jnp.int32)[:, None, None]

    def of_source(group):
        here = jnp.sum(jnp.where(sources == group, told, 0), axis=0)
        return here, jnp.sum(jnp.where(sources < group, told[:, :, :GROUPS], 0), axis=0)

    core = c[None]
    others = lax.ppermute(blocks, "c", swap)
    (part,) = vmem_call(
        first_kernel, "own_group", [core, *of_source(y * NC + c)], [blocks, remote_codes], [((NX, NY, T, T), F32)],
        flops=300_000_000, bytes_accessed=3_500_000,
    )
    (chip_sum,) = vmem_call(
        second_kernel, "other_group", [core, *of_source(y * NC + 1 - c)], [others, remote_codes, part], [((NX, NY, T, T), BF16)],
        scratch=[pltpu.VMEM((NX, NY, T, T), BF16), pltpu.SemaphoreType.DMA((NY,))], outside=1,
        flops=300_000_000, bytes_accessed=5_500_000,
    )
    arrived = lax.all_to_all(chip_sum.reshape(NX * NY, T, T), X + Y, 0, 0, tiled=True)

    near = []
    for k in (2, 1, 3, 0):
        (sums,) = vmem_call(
            functools.partial(local_kernel, k, k == 0), "local_sums", [jnp.stack([z, x])], [blocks, local_codes],
            [((T, T), F32)],
            scratch=[pltpu.VMEM((4 * T, T), BF16)] + ([] if k else [pltpu.VMEM((T, T), F32), pltpu.SemaphoreType.DMA]),
            outside=int(k == 0), flops=150_000_000, bytes_accessed=1_200_000,
        )
        near.append(lax.ppermute(sums, X, forward[NX - k]) if k else sums)
    two, three, one, near_0 = near

    share = width // OWNERS
    operands = ((2 * NX, T, T), BF16)
    arrived, x, c = lax.optimization_barrier((arrived, x, c))
    outside = [near_0, one, two, three, weights_t, features_t]
    hidden, send, keep = vmem_call(
        dense_kernel, "dense", [jnp.stack([x, c])], [arrived.reshape(NX, NY, T, T), features, w_agg, w_self, cotangent],
        [((T, width), BF16), operands, operands],
        scratch=[pltpu.VMEM((width, T), F32)]
        + [pltpu.VMEM(of.shape, of.dtype) for of in outside]
        + [pltpu.SemaphoreType.DMA((len(outside),))],
        anywhere=[pltpu.with_memory_space_constraint(of, pltpu.HBM) for of in outside],
        flops=150_000_000, bytes_accessed=3_500_000, transcendentals=65536,
    )
    received = lax.ppermute(send, "c", swap)
    (chip_grad,) = vmem_call(
        grad_kernel, "gradient", [], [keep, received], [((OWNERS, share, width), BF16)], flops=300_000_000, bytes_accessed=1_000_000
    )
    plane = added(lax.all_to_all(chip_grad, ("z",) + X, 0, 0, tiled=True), BF16)
    planes = lax.all_to_all(jnp.broadcast_to(plane, (NY,) + plane.shape), Y, 0, 0, tiled=True)
    grads = lax.all_gather(added(planes, F32), "c", axis=0)
    return hidden, grads[0], grads[1]


def solution(mesh):
    axes = ("z",) + X + Y + ("c",)
    fine = Mesh(mesh.devices.reshape(NZ, 2, 2, 2, 2, 2, NC), axes)
    row, rep = ("z",) + X, Y + ("c",)
    nodes = P(row + rep, None)
    in_specs = (nodes, nodes, nodes, P(row, rep, None, None), P(row, rep, None), P(), P(), nodes)
    out_specs = (nodes, P(row, None), P(row, None))
    return jax.shard_map(body, mesh=fine, in_specs=in_specs, out_specs=out_specs, check_vma=False)
```

```python
import functools

import jax
import jax.numpy as jnp
from jax import lax
from jax.experimental import pallas as pl
from jax.experimental.pallas import tpu as pltpu
from jax.sharding import Mesh, PartitionSpec as P

NZ, NX, NY, NC = 8, 4, 8, 2
OWNERS = NZ * NX
GROUPS = NY * NC
T = 128
K_LOC = 12
K_REM = 4
CAP = 2
TOLD = 16
X, Y = ("x1", "x0"), ("y2", "y1", "y0")
F32 = jnp.float32
BF16 = jnp.bfloat16
VMEM_LIMIT = 16 * 1024 * 1024


def vmem_call(
    kernel, name, scalar_inputs, array_inputs, outputs, scratch=(), anywhere=(), outside=0, flops=0, bytes_accessed=0, transcendentals=0
):
    vmem = pl.BlockSpec(memory_space=pltpu.VMEM)
    return pl.pallas_call(
        kernel,
        in_specs=[pl.BlockSpec(memory_space=pltpu.SMEM)] * len(scalar_inputs)
        + [pl.BlockSpec(memory_space=pltpu.HBM)] * len(anywhere)
        + [vmem] * len(array_inputs),
        out_specs=[vmem] * (len(outputs) - outside) + [pl.BlockSpec(memory_space=pltpu.HBM)] * outside,
        out_shape=[jax.ShapeDtypeStruct(*of) for of in outputs[: len(outputs) - outside]]
        + [pltpu.HBM(*of) for of in outputs[len(outputs) - outside :]],
        scratch_shapes=list(scratch),
        compiler_params=pltpu.CompilerParams(vmem_limit_bytes=VMEM_LIMIT),
        cost_estimate=pl.CostEstimate(flops=flops, bytes_accessed=bytes_accessed, transcendentals=transcendentals),
        name=name,
    )(*scalar_inputs, *anywhere, *array_inputs)


def spread_kernel(features_ref, features_out, quarters_ref, features_t, sems):
    features_t[...] = features_ref[...].astype(F32).T.astype(BF16).reshape(NX, T, T)
    copies = [pltpu.make_async_copy(features_t, quarters_ref.at[z], sems.at[z]) for z in range(NZ)]
    copies.append(pltpu.make_async_copy(features_t, features_out, sems.at[NZ]))
    for copy in copies:
        copy.start()
    for copy in copies:
        copy.wait()


def split_kernel(codes_ref, remote_ref, local_ref, sems):
    copies = []
    for x in range(NX):
        codes = codes_ref.at[x % 2, x // 2]
        copies.append(pltpu.make_async_copy(codes.at[TOLD:], local_ref.at[x], sems.at[x]))
        copies[-1].start()
        remote_ref[x] = codes[0:TOLD]
    for copy in copies:
        copy.wait()


def remote_product(core, here, before, blocks_ref, told_ref, x, y):
    group = y * NC + core[0]
    first = jnp.clip(here[x, GROUPS + group * CAP], 0, OWNERS - 1)
    second = jnp.clip(here[x, GROUPS + group * CAP + 1], 0, OWNERS - 1)
    start, count = before[x, group].astype(F32), here[x, group].astype(F32)
    told = told_ref[group, x].astype(F32)
    entry = told[0:K_REM] - start
    row = jnp.where(entry < count, entry * T + told[K_REM : 2 * K_REM], -1.0).astype(jnp.int16)
    weight = told[2 * K_REM : 3 * K_REM].astype(BF16)
    rows = lax.broadcasted_iota(jnp.int16, (CAP * T, T), 0)
    hot = jnp.zeros((CAP * T, T), BF16)
    for slot in range(K_REM):
        hot = jnp.where(rows == row[slot : slot + 1], weight[slot : slot + 1], hot)
    pair = jnp.concatenate([blocks_ref[first], blocks_ref[second]], axis=1)
    return jnp.dot(pair, hot, preferred_element_type=F32)


def first_kernel(core, here, before, blocks_ref, told_ref, part_ref):
    for y in range(NY):
        for x in range(NX):
            part_ref[x, y] = remote_product(core, here, before, blocks_ref, told_ref, x, y)


def second_kernel(core, here, before, blocks_ref, told_ref, part_ref, sums_ref, sums, sems):
    copies = []
    for y in range(NY):
        for x in range(NX):
            sums[x, y] = (part_ref[x, y] + remote_product(core, here, before, blocks_ref, told_ref, x, y)).astype(BF16)
        copies.append(pltpu.make_async_copy(sums.at[:, y], sums_ref.at[:, y], sems.at[y]))
        copies[-1].start()
    for copy in copies:
        copy.wait()


def local_kernel(k, outside, scalars, blocks_ref, told_ref, out, hot_ref, total=None, sem=None):
    x = lax.rem(scalars[1] + (NX - k), NX)
    owner = scalars[0] * NX + x
    rows = lax.broadcasted_iota(jnp.int16, (T, T), 0)
    lanes = lax.broadcasted_iota(jnp.int32, (1, T), 1).astype(F32)
    ones, zeros = jnp.ones((T, T), BF16), jnp.zeros((T, T), BF16)
    block, row, weight = (told_ref[x, n * 16 : n * 16 + 16, :].astype(F32) for n in range(3))
    weight = weight.astype(BF16)

    def of_four(i, summed):
        for j in range(4):
            p = 4 * i + j
            code = ((block - p.astype(F32)) * T + row).astype(jnp.int16)
            own = (lanes - jnp.where(p == owner, 0.0, 1024.0)).astype(jnp.int16)
            hot = jnp.where(rows == own, ones, zeros)
            for slot in range(K_LOC):
                hot = jnp.where(rows == code[slot : slot + 1], weight[slot : slot + 1], hot)
            hot_ref[j * T : (j + 1) * T, :] = hot
        four = jnp.concatenate([blocks_ref[4 * i + j] for j in range(4)], axis=1)
        return summed + jnp.dot(four, hot_ref[...], preferred_element_type=F32)

    summed = lax.fori_loop(0, OWNERS // 4, of_four, jnp.zeros((T, T), F32), unroll=2)
    if outside:
        total[...] = summed
        copy = pltpu.make_async_copy(total, out, sem)
        copy.start()
        copy.wait()
    else:
        out[...] = summed


def dense_kernel(
    scalars, near_0_in, weights_in, from_self_in, features_t_in, arrived, near_1, near_2, near_3, w_agg, cotangent,
    preact_ref, send_ref, keep_ref, agg_t, near_0, weights_t, from_self, features_t, sems,
):
    own_x, own_c = scalars[0], scalars[1]
    sources = (near_0_in, weights_in, from_self_in, features_t_in)
    targets = (near_0, weights_t, from_self, features_t)
    copies = [pltpu.make_async_copy(of, to, sems.at[i]) for i, (of, to) in enumerate(zip(sources, targets))]
    for copy in copies:
        copy.start()

    for x in range(NX):
        summed = arrived[x, 0].astype(F32)
        for y in range(1, NY):
            summed = summed + arrived[x, y].astype(F32)
        agg_t[x * T : (x + 1) * T, :] = summed
    for k, near in ((1, near_1), (2, near_2), (3, near_3), (0, near_0)):
        if k == 0:
            copies[0].wait()
        quarter = lax.rem(own_x + (NX - k), NX)
        agg_t[pl.ds(pl.multiple_of(quarter * T, T), T), :] += near[...]
    copies[1].wait()
    degree = 1.0 + jnp.sum(weights_t[...].astype(F32), axis=0, keepdims=True)
    aggregate = (agg_t[...] / degree).astype(BF16)
    contract = (((0,), (0,)), ((), ()))
    preact = lax.dot_general(aggregate, w_agg[...], contract, preferred_element_type=F32)
    copies[2].wait()
    preact = preact + from_self[...]
    preact_ref[...] = preact
    sigma = jax.nn.sigmoid(preact)
    grad_pre = (cotangent[...].astype(F32) * sigma * (1.0 + preact * (1.0 - sigma))).astype(BF16)
    copies[3].wait()
    for j in range(NX):
        columns = grad_pre[:, j * T : (j + 1) * T]
        keep_ref[NX + j] = columns
        send_ref[NX + j] = columns
        of_agg, of_self = aggregate[j * T : (j + 1) * T, :], features_t[j]
        keep_ref[j] = jnp.where(own_c == 0, of_agg, of_self)
        send_ref[j] = jnp.where(own_c == 0, of_self, of_agg)


def self_kernel(features, w_self, out_ref, product, sem):
    product[...] = jnp.dot(features[...], w_self[...], preferred_element_type=F32)
    copy = pltpu.make_async_copy(product, out_ref, sem)
    copy.start()
    copy.wait()


def hidden_kernel(preact_ref, hidden_ref):
    preact = preact_ref[...]
    hidden_ref[...] = (preact * jax.nn.sigmoid(preact)).astype(BF16)


def grad_kernel(keep_ref, received_ref, grad_ref):
    both = (keep_ref, received_ref)
    left = jnp.concatenate([ref[0:NX].reshape(NX * T, T) for ref in both], axis=1)
    for j in range(NX):
        right = jnp.concatenate([ref[NX + j] for ref in both], axis=0)
        product = jnp.dot(left, right, preferred_element_type=F32)
        grad_ref[:, :, j * T : (j + 1) * T] = product.reshape(OWNERS, grad_ref.shape[1], T).astype(BF16)


def add_kernel(parts_ref, sum_ref):
    summed = parts_ref[0].astype(F32)
    for i in range(1, parts_ref.shape[0]):
        summed = summed + parts_ref[i].astype(F32)
    sum_ref[...] = summed.astype(sum_ref.dtype)


def added(parts, dtype):
    (summed,) = vmem_call(
        add_kernel, "added", [], [parts], [(parts.shape[1:], dtype)], flops=parts.size, bytes_accessed=3 * parts.size
    )
    return summed


def body(features, edge_weights, neighbours, send_list, send_count, w_agg, w_self, cotangent):
    width = features.shape[1]
    z, x, y, c = (lax.axis_index(a).astype(jnp.int32) for a in ("z", X, Y, "c"))
    swap = [(0, 1), (1, 0)]

    features_t, quarters = vmem_call(
        spread_kernel, "spread", [], [features], [((NX, T, T), BF16), ((NZ, NX, T, T), BF16)],
        scratch=[pltpu.VMEM((NX, T, T), BF16), pltpu.SemaphoreType.DMA((NZ + 1,))], outside=2, bytes_accessed=1_500_000,
    )
    blocks = lax.all_to_all(quarters.reshape(OWNERS, T, T), ("z",) + X, 0, 0, tiled=True)

    codes_t = neighbours.T
    weights_t = edge_weights.T
    told = jnp.concatenate([send_count[0], send_list[0].reshape(1, GROUPS * CAP)], axis=1).astype(BF16)
    told = jnp.pad(told, ((0, 3), (0, T - GROUPS * (1 + CAP))))
    block, row = (codes_t // T).astype(BF16), (codes_t % T).astype(BF16)
    gap = jnp.zeros((16 - K_LOC, T), BF16)
    of_remote = jnp.concatenate([block[K_LOC:], row[K_LOC:], weights_t[K_LOC:], told], axis=0)
    of_local = jnp.concatenate([block[:K_LOC], gap, row[:K_LOC], gap, weights_t[:K_LOC], gap], axis=0)
    codes = jnp.concatenate([of_remote, of_local], axis=0)
    forward = [[(i, (i + k) % NX) for i in range(NX)] for k in range(NX)]
    codes = lax.all_gather(lax.all_gather(codes, "x1", axis=0), "x0", axis=0)
    remote_codes, local_codes = vmem_call(
        split_kernel, "split", [], [codes], [((NX, TOLD, T), BF16), ((NX, 48, T), BF16)],
        scratch=[pltpu.SemaphoreType.DMA((NX,))], outside=1, bytes_accessed=100_000,
    )
    remote_codes = lax.all_gather(remote_codes, Y + ("c",), axis=0)
    blocks, remote_codes = lax.optimization_barrier((blocks, remote_codes))
    told = remote_codes[:, :, 12].astype(jnp.int32)
    sources = jnp.arange(GROUPS, dtype=jnp.int32)[:, None, None]

    def of_source(group):
        here = jnp.sum(jnp.where(sources == group, told, 0), axis=0)
        return here, jnp.sum(jnp.where(sources < group, told[:, :, :GROUPS], 0), axis=0)

    core = c[None]
    others = lax.ppermute(blocks, "c", swap)
    (part,) = vmem_call(
        first_kernel, "own_group", [core, *of_source(y * NC + c)], [blocks, remote_codes], [((NX, NY, T, T), F32)],
        flops=300_000_000, bytes_accessed=3_500_000,
    )
    (chip_sum,) = vmem_call(
        second_kernel, "other_group", [core, *of_source(y * NC + 1 - c)], [others, remote_codes, part], [((NX, NY, T, T), BF16)],
        scratch=[pltpu.VMEM((NX, NY, T, T), BF16), pltpu.SemaphoreType.DMA((NY,))], outside=1,
        flops=300_000_000, bytes_accessed=5_500_000,
    )
    arrived = lax.all_to_all(chip_sum.reshape(NX * NY, T, T), X + Y, 0, 0, tiled=True)

    features_later, _ = lax.optimization_barrier((features, chip_sum))
    near = []
    for k in (2, 1, 3, 0):
        (sums,) = vmem_call(
            functools.partial(local_kernel, k, k == 0), "local_sums", [jnp.stack([z, x])], [blocks, local_codes],
            [((T, T), F32)],
            scratch=[pltpu.VMEM((4 * T, T), BF16)] + ([] if k else [pltpu.VMEM((T, T), F32), pltpu.SemaphoreType.DMA]),
            outside=int(k == 0), flops=150_000_000, bytes_accessed=1_200_000,
        )
        near.append(lax.ppermute(sums, X, forward[NX - k]) if k else sums)
    two, three, one, near_0 = near

    share = width // OWNERS
    operands = ((2 * NX, T, T), BF16)
    (from_self,) = vmem_call(
        self_kernel, "from_self", [], [features_later, w_self], [((T, width), F32)],
        scratch=[pltpu.VMEM((T, width), F32), pltpu.SemaphoreType.DMA], outside=1, flops=67_000_000, bytes_accessed=900_000,
    )
    arrived, x, c = lax.optimization_barrier((arrived, x, c))
    outside = [near_0, weights_t, from_self, features_t]
    preact, send, keep = vmem_call(
        dense_kernel, "dense", [jnp.stack([x, c])], [arrived.reshape(NX, NY, T, T), one, two, three, w_agg, cotangent],
        [((T, width), F32), operands, operands],
        scratch=[pltpu.VMEM((width, T), F32)]
        + [pltpu.VMEM(of.shape, of.dtype) for of in outside]
        + [pltpu.SemaphoreType.DMA((len(outside),))],
        anywhere=[pltpu.with_memory_space_constraint(of, pltpu.HBM) for of in outside],
        flops=150_000_000, bytes_accessed=3_500_000, transcendentals=65536,
    )
    received = lax.ppermute(send, "c", swap)
    (hidden,) = vmem_call(hidden_kernel, "hidden", [], [preact], [((T, width), BF16)], flops=1_000_000, bytes_accessed=400_000, transcendentals=65536)
    received, hidden = lax.optimization_barrier((received, hidden))
    (chip_grad,) = vmem_call(
        grad_kernel, "gradient", [], [keep, received], [((OWNERS, share, width), BF16)], flops=300_000_000, bytes_accessed=1_000_000
    )
    plane = added(lax.all_to_all(chip_grad, ("z",) + X, 0, 0, tiled=True), BF16)
    planes = lax.all_to_all(jnp.broadcast_to(plane, (NY,) + plane.shape), Y, 0, 0, tiled=True)
    grads = lax.all_gather(added(planes, F32), "c", axis=0)
    return hidden, grads[0], grads[1]


def solution(mesh):
    axes = ("z",) + X + Y + ("c",)
    fine = Mesh(mesh.devices.reshape(NZ, 2, 2, 2, 2, 2, NC), axes)
    row, rep = ("z",) + X, Y + ("c",)
    nodes = P(row + rep, None)
    in_specs = (nodes, nodes, nodes, P(row, rep, None, None), P(row, rep, None), P(), P(), nodes)
    out_specs = (nodes, P(row, None), P(row, None))
    return jax.shard_map(body, mesh=fine, in_specs=in_specs, out_specs=out_specs, check_vma=False)
```

```python
import functools

import jax
import jax.numpy as jnp
from jax import lax
from jax.experimental import pallas as pl
from jax.experimental.pallas import tpu as pltpu
from jax.sharding import Mesh, PartitionSpec as P

NZ, NX, NY, NC = 8, 4, 8, 2
OWNERS = NZ * NX
GROUPS = NY * NC
T = 128
K_LOC = 12
K_REM = 4
CAP = 2
TOLD = 16
X, Y = ("x1", "x0"), ("y2", "y1", "y0")
F32 = jnp.float32
BF16 = jnp.bfloat16
VMEM_LIMIT = 16 * 1024 * 1024


def vmem_call(
    kernel, name, scalar_inputs, array_inputs, outputs, scratch=(), anywhere=(), outside=0, flops=0, bytes_accessed=0, transcendentals=0
):
    vmem = pl.BlockSpec(memory_space=pltpu.VMEM)
    return pl.pallas_call(
        kernel,
        in_specs=[pl.BlockSpec(memory_space=pltpu.SMEM)] * len(scalar_inputs)
        + [pl.BlockSpec(memory_space=pltpu.HBM)] * len(anywhere)
        + [vmem] * len(array_inputs),
        out_specs=[vmem] * (len(outputs) - outside) + [pl.BlockSpec(memory_space=pltpu.HBM)] * outside,
        out_shape=[jax.ShapeDtypeStruct(*of) for of in outputs[: len(outputs) - outside]]
        + [pltpu.HBM(*of) for of in outputs[len(outputs) - outside :]],
        scratch_shapes=list(scratch),
        compiler_params=pltpu.CompilerParams(vmem_limit_bytes=VMEM_LIMIT),
        cost_estimate=pl.CostEstimate(flops=flops, bytes_accessed=bytes_accessed, transcendentals=transcendentals),
        name=name,
    )(*scalar_inputs, *anywhere, *array_inputs)


def spread_kernel(features_ref, features_out, quarters_ref, features_t, sems):
    features_t[...] = features_ref[...].astype(F32).T.astype(BF16).reshape(NX, T, T)
    copies = [pltpu.make_async_copy(features_t, quarters_ref.at[z], sems.at[z]) for z in range(NZ)]
    copies.append(pltpu.make_async_copy(features_t, features_out, sems.at[NZ]))
    for copy in copies:
        copy.start()
    for copy in copies:
        copy.wait()


def split_kernel(codes_ref, remote_ref, local_ref, sems):
    copies = []
    for x in range(NX):
        codes = codes_ref.at[x % 2, x // 2]
        copies.append(pltpu.make_async_copy(codes.at[TOLD:], local_ref.at[x], sems.at[x]))
        copies[-1].start()
        remote_ref[x] = codes[0:TOLD]
    for copy in copies:
        copy.wait()


def remote_product(core, here, before, blocks_ref, told_ref, x, y):
    group = y * NC + core[0]
    first = jnp.clip(here[x, GROUPS + group * CAP], 0, OWNERS - 1)
    second = jnp.clip(here[x, GROUPS + group * CAP + 1], 0, OWNERS - 1)
    start, count = before[x, group].astype(F32), here[x, group].astype(F32)
    told = told_ref[group, x].astype(F32)
    entry = told[0:K_REM] - start
    row = jnp.where(entry < count, entry * T + told[K_REM : 2 * K_REM], -1.0).astype(jnp.int16)
    weight = told[2 * K_REM : 3 * K_REM].astype(BF16)
    rows = lax.broadcasted_iota(jnp.int16, (CAP * T, T), 0)
    hot = jnp.zeros((CAP * T, T), BF16)
    for slot in range(K_REM):
        hot = jnp.where(rows == row[slot : slot + 1], weight[slot : slot + 1], hot)
    pair = jnp.concatenate([blocks_ref[first], blocks_ref[second]], axis=1)
    return jnp.dot(pair, hot, preferred_element_type=F32)


def first_kernel(core, here, before, blocks_ref, told_ref, part_ref):
    for y in range(NY):
        for x in range(NX):
            part_ref[x, y] = remote_product(core, here, before, blocks_ref, told_ref, x, y)


def second_kernel(core, here, before, blocks_ref, told_ref, part_ref, sums_ref, sums, sems):
    copies = []
    for y in range(NY):
        for x in range(NX):
            sums[y, x] = (part_ref[x, y] + remote_product(core, here, before, blocks_ref, told_ref, x, y)).astype(BF16)
        copies.append(pltpu.make_async_copy(sums.at[y], sums_ref.at[y], sems.at[y]))
        copies[-1].start()
    for copy in copies:
        copy.wait()


def local_kernel(k, outside, scalars, blocks_ref, told_ref, out, hot_ref, total=None, sem=None):
    x = lax.rem(scalars[1] + (NX - k), NX)
    owner = scalars[0] * NX + x
    rows = lax.broadcasted_iota(jnp.int16, (T, T), 0)
    lanes = lax.broadcasted_iota(jnp.int32, (1, T), 1).astype(F32)
    ones, zeros = jnp.ones((T, T), BF16), jnp.zeros((T, T), BF16)
    block, row, weight = (told_ref[x, n * 16 : n * 16 + 16, :].astype(F32) for n in range(3))
    weight = weight.astype(BF16)

    def of_four(i, summed):
        for j in range(4):
            p = 4 * i + j
            code = ((block - p.astype(F32)) * T + row).astype(jnp.int16)
            own = (lanes - jnp.where(p == owner, 0.0, 1024.0)).astype(jnp.int16)
            hot = jnp.where(rows == own, ones, zeros)
            for slot in range(K_LOC):
                hot = jnp.where(rows == code[slot : slot + 1], weight[slot : slot + 1], hot)
            hot_ref[j * T : (j + 1) * T, :] = hot
        four = jnp.concatenate([blocks_ref[4 * i + j] for j in range(4)], axis=1)
        return summed + jnp.dot(four, hot_ref[...], preferred_element_type=F32)

    summed = lax.fori_loop(0, OWNERS // 4, of_four, jnp.zeros((T, T), F32), unroll=2)
    if outside:
        total[...] = summed
        copy = pltpu.make_async_copy(total, out, sem)
        copy.start()
        copy.wait()
    else:
        out[...] = summed


def dense_kernel(
    scalars, near_0_in, weights_in, from_self_in, features_t_in, arrived, near_1, near_2, near_3, w_agg, cotangent,
    preact_ref, send_ref, keep_ref, agg_t, near_0, weights_t, from_self, features_t, sems,
):
    own_x, own_c = scalars[0], scalars[1]
    sources = (near_0_in, weights_in, from_self_in, features_t_in)
    targets = (near_0, weights_t, from_self, features_t)
    copies = [pltpu.make_async_copy(of, to, sems.at[i]) for i, (of, to) in enumerate(zip(sources, targets))]
    for copy in copies:
        copy.start()

    for x in range(NX):
        summed = arrived[0, x].astype(F32)
        for y in range(1, NY):
            summed = summed + arrived[y, x].astype(F32)
        agg_t[x * T : (x + 1) * T, :] = summed
    for k, near in ((1, near_1), (2, near_2), (3, near_3), (0, near_0)):
        if k == 0:
            copies[0].wait()
        quarter = lax.rem(own_x + (NX - k), NX)
        agg_t[pl.ds(pl.multiple_of(quarter * T, T), T), :] += near[...]
    copies[1].wait()
    degree = 1.0 + jnp.sum(weights_t[...].astype(F32), axis=0, keepdims=True)
    aggregate = (agg_t[...] / degree).astype(BF16)
    contract = (((0,), (0,)), ((), ()))
    preact = lax.dot_general(aggregate, w_agg[...], contract, preferred_element_type=F32)
    copies[2].wait()
    preact = preact + from_self[...]
    preact_ref[...] = preact
    sigma = jax.nn.sigmoid(preact)
    grad_pre = (cotangent[...].astype(F32) * sigma * (1.0 + preact * (1.0 - sigma))).astype(BF16)
    copies[3].wait()
    for j in range(NX):
        columns = grad_pre[:, j * T : (j + 1) * T]
        keep_ref[NX + j] = columns
        send_ref[NX + j] = columns
        of_agg, of_self = aggregate[j * T : (j + 1) * T, :], features_t[j]
        keep_ref[j] = jnp.where(own_c == 0, of_agg, of_self)
        send_ref[j] = jnp.where(own_c == 0, of_self, of_agg)


def self_kernel(features, w_self, out_ref, product, sem):
    product[...] = jnp.dot(features[...], w_self[...], preferred_element_type=F32)
    copy = pltpu.make_async_copy(product, out_ref, sem)
    copy.start()
    copy.wait()


def hidden_kernel(preact_ref, hidden_ref):
    preact = preact_ref[...]
    hidden_ref[...] = (preact * jax.nn.sigmoid(preact)).astype(BF16)


def grad_kernel(keep_ref, received_ref, grad_ref):
    both = (keep_ref, received_ref)
    left = jnp.concatenate([ref[0:NX].reshape(NX * T, T) for ref in both], axis=1)
    for j in range(NX):
        right = jnp.concatenate([ref[NX + j] for ref in both], axis=0)
        product = jnp.dot(left, right, preferred_element_type=F32)
        grad_ref[:, :, j * T : (j + 1) * T] = product.reshape(OWNERS, grad_ref.shape[1], T).astype(BF16)


def add_kernel(parts_ref, sum_ref):
    summed = parts_ref[0].astype(F32)
    for i in range(1, parts_ref.shape[0]):
        summed = summed + parts_ref[i].astype(F32)
    sum_ref[...] = summed.astype(sum_ref.dtype)


def added(parts, dtype):
    (summed,) = vmem_call(
        add_kernel, "added", [], [parts], [(parts.shape[1:], dtype)], flops=parts.size, bytes_accessed=3 * parts.size
    )
    return summed


def body(features, edge_weights, neighbours, send_list, send_count, w_agg, w_self, cotangent):
    width = features.shape[1]
    z, x, y, c = (lax.axis_index(a).astype(jnp.int32) for a in ("z", X, Y, "c"))
    swap = [(0, 1), (1, 0)]

    features_t, quarters = vmem_call(
        spread_kernel, "spread", [], [features], [((NX, T, T), BF16), ((NZ, NX, T, T), BF16)],
        scratch=[pltpu.VMEM((NX, T, T), BF16), pltpu.SemaphoreType.DMA((NZ + 1,))], outside=2, bytes_accessed=1_500_000,
    )
    blocks = lax.all_to_all(quarters.reshape(OWNERS, T, T), ("z",) + X, 0, 0, tiled=True)

    codes_t = neighbours.T
    weights_t = edge_weights.T
    told = jnp.concatenate([send_count[0], send_list[0].reshape(1, GROUPS * CAP)], axis=1).astype(BF16)
    told = jnp.pad(told, ((0, 3), (0, T - GROUPS * (1 + CAP))))
    block, row = (codes_t // T).astype(BF16), (codes_t % T).astype(BF16)
    gap = jnp.zeros((16 - K_LOC, T), BF16)
    of_remote = jnp.concatenate([block[K_LOC:], row[K_LOC:], weights_t[K_LOC:], told], axis=0)
    of_local = jnp.concatenate([block[:K_LOC], gap, row[:K_LOC], gap, weights_t[:K_LOC], gap], axis=0)
    codes = jnp.concatenate([of_remote, of_local], axis=0)
    forward = [[(i, (i + k) % NX) for i in range(NX)] for k in range(NX)]
    codes = lax.all_gather(lax.all_gather(codes, "x1", axis=0), "x0", axis=0)
    remote_codes, local_codes = vmem_call(
        split_kernel, "split", [], [codes], [((NX, TOLD, T), BF16), ((NX, 48, T), BF16)],
        scratch=[pltpu.SemaphoreType.DMA((NX,))], outside=1, bytes_accessed=100_000,
    )
    remote_codes = lax.all_gather(remote_codes, Y + ("c",), axis=0)
    blocks, remote_codes = lax.optimization_barrier((blocks, remote_codes))
    told = remote_codes[:, :, 12].astype(jnp.int32)
    sources = jnp.arange(GROUPS, dtype=jnp.int32)[:, None, None]

    def of_source(group):
        here = jnp.sum(jnp.where(sources == group, told, 0), axis=0)
        return here, jnp.sum(jnp.where(sources < group, told[:, :, :GROUPS], 0), axis=0)

    core = c[None]
    others = lax.ppermute(blocks, "c", swap)
    (part,) = vmem_call(
        first_kernel, "own_group", [core, *of_source(y * NC + c)], [blocks, remote_codes], [((NX, NY, T, T), F32)],
        flops=300_000_000, bytes_accessed=3_500_000,
    )
    (chip_sum,) = vmem_call(
        second_kernel, "other_group", [core, *of_source(y * NC + 1 - c)], [others, remote_codes, part], [((NY, NX, T, T), BF16)],
        scratch=[pltpu.VMEM((NY, NX, T, T), BF16), pltpu.SemaphoreType.DMA((NY,))], outside=1,
        flops=300_000_000, bytes_accessed=5_500_000,
    )
    arrived = lax.all_to_all(chip_sum.reshape(NX * NY, T, T), Y + X, 0, 0, tiled=True)

    features_later, _ = lax.optimization_barrier((features, chip_sum))
    near = []
    for k in (2, 1, 3, 0):
        (sums,) = vmem_call(
            functools.partial(local_kernel, k, k == 0), "local_sums", [jnp.stack([z, x])], [blocks, local_codes],
            [((T, T), F32)],
            scratch=[pltpu.VMEM((4 * T, T), BF16)] + ([] if k else [pltpu.VMEM((T, T), F32), pltpu.SemaphoreType.DMA]),
            outside=int(k == 0), flops=150_000_000, bytes_accessed=1_200_000,
        )
        near.append(lax.ppermute(sums, X, forward[NX - k]) if k else sums)
    two, three, one, near_0 = near

    share = width // OWNERS
    operands = ((2 * NX, T, T), BF16)
    (from_self,) = vmem_call(
        self_kernel, "from_self", [], [features_later, w_self], [((T, width), F32)],
        scratch=[pltpu.VMEM((T, width), F32), pltpu.SemaphoreType.DMA], outside=1, flops=67_000_000, bytes_accessed=900_000,
    )
    arrived, x, c = lax.optimization_barrier((arrived, x, c))
    outside = [near_0, weights_t, from_self, features_t]
    preact, send, keep = vmem_call(
        dense_kernel, "dense", [jnp.stack([x, c])], [arrived.reshape(NY, NX, T, T), one, two, three, w_agg, cotangent],
        [((T, width), F32), operands, operands],
        scratch=[pltpu.VMEM((width, T), F32)]
        + [pltpu.VMEM(of.shape, of.dtype) for of in outside]
        + [pltpu.SemaphoreType.DMA((len(outside),))],
        anywhere=[pltpu.with_memory_space_constraint(of, pltpu.HBM) for of in outside],
        flops=150_000_000, bytes_accessed=3_500_000, transcendentals=65536,
    )
    received = lax.ppermute(send, "c", swap)
    (hidden,) = vmem_call(hidden_kernel, "hidden", [], [preact], [((T, width), BF16)], flops=1_000_000, bytes_accessed=400_000, transcendentals=65536)
    received, hidden = lax.optimization_barrier((received, hidden))
    (chip_grad,) = vmem_call(
        grad_kernel, "gradient", [], [keep, received], [((OWNERS, share, width), BF16)], flops=300_000_000, bytes_accessed=1_000_000
    )
    plane = added(lax.all_to_all(chip_grad, ("z",) + X, 0, 0, tiled=True), BF16)
    planes = lax.all_to_all(jnp.broadcast_to(plane, (NY,) + plane.shape), Y, 0, 0, tiled=True)
    grads = lax.all_gather(added(planes, F32), "c", axis=0)
    return hidden, grads[0], grads[1]


def solution(mesh):
    axes = ("z",) + X + Y + ("c",)
    fine = Mesh(mesh.devices.reshape(NZ, 2, 2, 2, 2, 2, NC), axes)
    row, rep = ("z",) + X, Y + ("c",)
    nodes = P(row + rep, None)
    in_specs = (nodes, nodes, nodes, P(row, rep, None, None), P(row, rep, None), P(), P(), nodes)
    out_specs = (nodes, P(row, None), P(row, None))
    return jax.shard_map(body, mesh=fine, in_specs=in_specs, out_specs=out_specs, check_vma=False)
```

```python
import functools

import jax
import jax.numpy as jnp
from jax import lax
from jax.experimental import pallas as pl
from jax.experimental.pallas import tpu as pltpu
from jax.sharding import Mesh, PartitionSpec as P

NZ, NX, NY, NC = 8, 4, 8, 2
OWNERS = NZ * NX
GROUPS = NY * NC
T = 128
K_LOC = 12
K_REM = 4
CAP = 2
TOLD = 16
X, Y = ("x1", "x0"), ("y2", "y1", "y0")
F32 = jnp.float32
BF16 = jnp.bfloat16
VMEM_LIMIT = 16 * 1024 * 1024


def vmem_call(
    kernel, name, scalar_inputs, array_inputs, outputs, scratch=(), anywhere=(), outside=0, flops=0, bytes_accessed=0, transcendentals=0
):
    vmem = pl.BlockSpec(memory_space=pltpu.VMEM)
    return pl.pallas_call(
        kernel,
        in_specs=[pl.BlockSpec(memory_space=pltpu.SMEM)] * len(scalar_inputs)
        + [pl.BlockSpec(memory_space=pltpu.HBM)] * len(anywhere)
        + [vmem] * len(array_inputs),
        out_specs=[vmem] * (len(outputs) - outside) + [pl.BlockSpec(memory_space=pltpu.HBM)] * outside,
        out_shape=[jax.ShapeDtypeStruct(*of) for of in outputs[: len(outputs) - outside]]
        + [pltpu.HBM(*of) for of in outputs[len(outputs) - outside :]],
        scratch_shapes=list(scratch),
        compiler_params=pltpu.CompilerParams(vmem_limit_bytes=VMEM_LIMIT),
        cost_estimate=pl.CostEstimate(flops=flops, bytes_accessed=bytes_accessed, transcendentals=transcendentals),
        name=name,
    )(*scalar_inputs, *anywhere, *array_inputs)


def spread_kernel(features_ref, features_out, quarters_ref, features_t, sems):
    features_t[...] = features_ref[...].astype(F32).T.astype(BF16).reshape(NX, T, T)
    copies = [pltpu.make_async_copy(features_t, quarters_ref.at[z], sems.at[z]) for z in range(NZ)]
    copies.append(pltpu.make_async_copy(features_t, features_out, sems.at[NZ]))
    for copy in copies:
        copy.start()
    for copy in copies:
        copy.wait()


def split_kernel(codes_ref, remote_ref, local_ref, sems):
    copies = []
    for x in range(NX):
        codes = codes_ref.at[x % 2, x // 2]
        copies.append(pltpu.make_async_copy(codes.at[TOLD:], local_ref.at[x], sems.at[x]))
        copies[-1].start()
        remote_ref[x] = codes[0:TOLD]
    for copy in copies:
        copy.wait()


def remote_product(core, here, before, blocks_ref, told_ref, x, y):
    group = y * NC + core[0]
    first = jnp.clip(here[x, GROUPS + group * CAP], 0, OWNERS - 1)
    second = jnp.clip(here[x, GROUPS + group * CAP + 1], 0, OWNERS - 1)
    start, count = before[x, group].astype(F32), here[x, group].astype(F32)
    told = told_ref[group, x].astype(F32)
    entry = told[0:K_REM] - start
    row = jnp.where(entry < count, entry * T + told[K_REM : 2 * K_REM], -1.0).astype(jnp.int16)
    weight = told[2 * K_REM : 3 * K_REM].astype(BF16)
    rows = lax.broadcasted_iota(jnp.int16, (CAP * T, T), 0)
    hot = jnp.zeros((CAP * T, T), BF16)
    for slot in range(K_REM):
        hot = jnp.where(rows == row[slot : slot + 1], weight[slot : slot + 1], hot)
    pair = jnp.concatenate([blocks_ref[first], blocks_ref[second]], axis=1)
    return jnp.dot(pair, hot, preferred_element_type=F32)


def first_kernel(core, here, before, blocks_ref, told_ref, part_ref):
    for y in range(NY):
        for x in range(NX):
            part_ref[x, y] = remote_product(core, here, before, blocks_ref, told_ref, x, y)


def second_kernel(core, here, before, blocks_ref, told_ref, part_ref, sums_ref, sums, sems):
    copies = []
    for y in range(NY):
        for x in range(NX):
            sums[y, x] = (part_ref[x, y] + remote_product(core, here, before, blocks_ref, told_ref, x, y)).astype(BF16)
        copies.append(pltpu.make_async_copy(sums.at[y], sums_ref.at[y], sems.at[y]))
        copies[-1].start()
    for copy in copies:
        copy.wait()


def local_kernel(k, outside, scalars, blocks_ref, told_ref, out, hot_ref, total=None, sem=None):
    x = lax.rem(scalars[1] + (NX - k), NX)
    owner = scalars[0] * NX + x
    rows = lax.broadcasted_iota(jnp.int16, (T, T), 0)
    lanes = lax.broadcasted_iota(jnp.int32, (1, T), 1).astype(F32)
    ones, zeros = jnp.ones((T, T), BF16), jnp.zeros((T, T), BF16)
    block, row, weight = (told_ref[x, n * 16 : n * 16 + 16, :].astype(F32) for n in range(3))
    weight = weight.astype(BF16)

    def of_four(i, summed):
        for j in range(4):
            p = 4 * i + j
            code = ((block - p.astype(F32)) * T + row).astype(jnp.int16)
            own = (lanes - jnp.where(p == owner, 0.0, 1024.0)).astype(jnp.int16)
            hot = jnp.where(rows == own, ones, zeros)
            for slot in range(K_LOC):
                hot = jnp.where(rows == code[slot : slot + 1], weight[slot : slot + 1], hot)
            hot_ref[j * T : (j + 1) * T, :] = hot
        four = jnp.concatenate([blocks_ref[4 * i + j] for j in range(4)], axis=1)
        return summed + jnp.dot(four, hot_ref[...], preferred_element_type=F32)

    summed = lax.fori_loop(0, OWNERS // 4, of_four, jnp.zeros((T, T), F32), unroll=2)
    if outside:
        total[...] = summed
        copy = pltpu.make_async_copy(total, out, sem)
        copy.start()
        copy.wait()
    else:
        out[...] = summed


def dense_kernel(
    scalars, near_0_in, weights_in, from_self_in, features_t_in, arrived, near_1, near_2, near_3, w_agg, cotangent,
    preact_ref, send_ref, keep_ref, agg_t, near_0, weights_t, from_self, features_t, sems,
):
    own_x, own_c = scalars[0], scalars[1]
    sources = (near_0_in, weights_in, from_self_in, features_t_in)
    targets = (near_0, weights_t, from_self, features_t)
    copies = [pltpu.make_async_copy(of, to, sems.at[i]) for i, (of, to) in enumerate(zip(sources, targets))]
    for copy in copies:
        copy.start()

    for x in range(NX):
        summed = arrived[0, x].astype(F32)
        for y in range(1, NY):
            summed = summed + arrived[y, x].astype(F32)
        agg_t[x * T : (x + 1) * T, :] = summed
    for k, near in ((1, near_1), (2, near_2), (3, near_3), (0, near_0)):
        if k == 0:
            copies[0].wait()
        quarter = lax.rem(own_x + (NX - k), NX)
        agg_t[pl.ds(pl.multiple_of(quarter * T, T), T), :] += near[...]
    copies[1].wait()
    degree = 1.0 + jnp.sum(weights_t[...].astype(F32), axis=0, keepdims=True)
    aggregate = (agg_t[...] / degree).astype(BF16)
    contract = (((0,), (0,)), ((), ()))
    preact = lax.dot_general(aggregate, w_agg[...], contract, preferred_element_type=F32)
    copies[2].wait()
    preact = preact + from_self[...]
    preact_ref[...] = preact
    sigma = jax.nn.sigmoid(preact)
    grad_pre = (cotangent[...].astype(F32) * sigma * (1.0 + preact * (1.0 - sigma))).astype(BF16)
    copies[3].wait()
    for j in range(NX):
        columns = grad_pre[:, j * T : (j + 1) * T]
        keep_ref[NX + j] = columns
        send_ref[NX + j] = columns
        of_agg, of_self = aggregate[j * T : (j + 1) * T, :], features_t[j]
        keep_ref[j] = jnp.where(own_c == 0, of_agg, of_self)
        send_ref[j] = jnp.where(own_c == 0, of_self, of_agg)


def self_kernel(features, w_self, out_ref, product, sem):
    product[...] = jnp.dot(features[...], w_self[...], preferred_element_type=F32)
    copy = pltpu.make_async_copy(product, out_ref, sem)
    copy.start()
    copy.wait()


def hidden_kernel(preact_ref, hidden_ref):
    preact = preact_ref[...]
    hidden_ref[...] = (preact * jax.nn.sigmoid(preact)).astype(BF16)


def grad_kernel(keep_ref, received_ref, grad_ref):
    both = (keep_ref, received_ref)
    left = jnp.concatenate([ref[0:NX].reshape(NX * T, T) for ref in both], axis=1)
    for j in range(NX):
        right = jnp.concatenate([ref[NX + j] for ref in both], axis=0)
        product = jnp.dot(left, right, preferred_element_type=F32)
        shares = product.astype(BF16).reshape(NZ, NX, grad_ref.shape[1], T)
        for x in range(NX):
            grad_ref[x * NZ : (x + 1) * NZ, :, j * T : (j + 1) * T] = shares[:, x]


def add_kernel(parts_ref, sum_ref):
    summed = parts_ref[0].astype(F32)
    for i in range(1, parts_ref.shape[0]):
        summed = summed + parts_ref[i].astype(F32)
    sum_ref[...] = summed.astype(sum_ref.dtype)


def added(parts, dtype):
    (summed,) = vmem_call(
        add_kernel, "added", [], [parts], [(parts.shape[1:], dtype)], flops=parts.size, bytes_accessed=3 * parts.size
    )
    return summed


def body(features, edge_weights, neighbours, send_list, send_count, w_agg, w_self, cotangent):
    width = features.shape[1]
    z, x, y, c = (lax.axis_index(a).astype(jnp.int32) for a in ("z", X, Y, "c"))
    swap = [(0, 1), (1, 0)]

    features_t, quarters = vmem_call(
        spread_kernel, "spread", [], [features], [((NX, T, T), BF16), ((NZ, NX, T, T), BF16)],
        scratch=[pltpu.VMEM((NX, T, T), BF16), pltpu.SemaphoreType.DMA((NZ + 1,))], outside=2, bytes_accessed=1_500_000,
    )
    blocks = lax.all_to_all(quarters.reshape(OWNERS, T, T), ("z",) + X, 0, 0, tiled=True)

    codes_t = neighbours.T
    weights_t = edge_weights.T
    told = jnp.concatenate([send_count[0], send_list[0].reshape(1, GROUPS * CAP)], axis=1).astype(BF16)
    told = jnp.pad(told, ((0, 3), (0, T - GROUPS * (1 + CAP))))
    block, row = (codes_t // T).astype(BF16), (codes_t % T).astype(BF16)
    gap = jnp.zeros((16 - K_LOC, T), BF16)
    of_remote = jnp.concatenate([block[K_LOC:], row[K_LOC:], weights_t[K_LOC:], told], axis=0)
    of_local = jnp.concatenate([block[:K_LOC], gap, row[:K_LOC], gap, weights_t[:K_LOC], gap], axis=0)
    codes = jnp.concatenate([of_remote, of_local], axis=0)
    forward = [[(i, (i + k) % NX) for i in range(NX)] for k in range(NX)]
    codes = lax.all_gather(lax.all_gather(codes, "x1", axis=0), "x0", axis=0)
    remote_codes, local_codes = vmem_call(
        split_kernel, "split", [], [codes], [((NX, TOLD, T), BF16), ((NX, 48, T), BF16)],
        scratch=[pltpu.SemaphoreType.DMA((NX,))], outside=1, bytes_accessed=100_000,
    )
    remote_codes = lax.all_gather(remote_codes, Y + ("c",), axis=0)
    blocks, remote_codes = lax.optimization_barrier((blocks, remote_codes))
    told = remote_codes[:, :, 12].astype(jnp.int32)
    sources = jnp.arange(GROUPS, dtype=jnp.int32)[:, None, None]

    def of_source(group):
        here = jnp.sum(jnp.where(sources == group, told, 0), axis=0)
        return here, jnp.sum(jnp.where(sources < group, told[:, :, :GROUPS], 0), axis=0)

    core = c[None]
    others = lax.ppermute(blocks, "c", swap)
    (part,) = vmem_call(
        first_kernel, "own_group", [core, *of_source(y * NC + c)], [blocks, remote_codes], [((NX, NY, T, T), F32)],
        flops=300_000_000, bytes_accessed=3_500_000,
    )
    (chip_sum,) = vmem_call(
        second_kernel, "other_group", [core, *of_source(y * NC + 1 - c)], [others, remote_codes, part], [((NY, NX, T, T), BF16)],
        scratch=[pltpu.VMEM((NY, NX, T, T), BF16), pltpu.SemaphoreType.DMA((NY,))], outside=1,
        flops=300_000_000, bytes_accessed=5_500_000,
    )
    arrived = lax.all_to_all(chip_sum.reshape(NX * NY, T, T), Y + X, 0, 0, tiled=True)

    features_later, _ = lax.optimization_barrier((features, chip_sum))
    near = []
    for k in (2, 1, 3, 0):
        (sums,) = vmem_call(
            functools.partial(local_kernel, k, k == 0), "local_sums", [jnp.stack([z, x])], [blocks, local_codes],
            [((T, T), F32)],
            scratch=[pltpu.VMEM((4 * T, T), BF16)] + ([] if k else [pltpu.VMEM((T, T), F32), pltpu.SemaphoreType.DMA]),
            outside=int(k == 0), flops=150_000_000, bytes_accessed=1_200_000,
        )
        near.append(lax.ppermute(sums, X, forward[NX - k]) if k else sums)
    two, three, one, near_0 = near

    share = width // OWNERS
    operands = ((2 * NX, T, T), BF16)
    (from_self,) = vmem_call(
        self_kernel, "from_self", [], [features_later, w_self], [((T, width), F32)],
        scratch=[pltpu.VMEM((T, width), F32), pltpu.SemaphoreType.DMA], outside=1, flops=67_000_000, bytes_accessed=900_000,
    )
    arrived, x, c = lax.optimization_barrier((arrived, x, c))
    outside = [near_0, weights_t, from_self, features_t]
    preact, send, keep = vmem_call(
        dense_kernel, "dense", [jnp.stack([x, c])], [arrived.reshape(NY, NX, T, T), one, two, three, w_agg, cotangent],
        [((T, width), F32), operands, operands],
        scratch=[pltpu.VMEM((width, T), F32)]
        + [pltpu.VMEM(of.shape, of.dtype) for of in outside]
        + [pltpu.SemaphoreType.DMA((len(outside),))],
        anywhere=[pltpu.with_memory_space_constraint(of, pltpu.HBM) for of in outside],
        flops=150_000_000, bytes_accessed=3_500_000, transcendentals=65536,
    )
    received = lax.ppermute(send, "c", swap)
    (hidden,) = vmem_call(hidden_kernel, "hidden", [], [preact], [((T, width), BF16)], flops=1_000_000, bytes_accessed=400_000, transcendentals=65536)
    received, hidden = lax.optimization_barrier((received, hidden))
    (chip_grad,) = vmem_call(
        grad_kernel, "gradient", [], [keep, received], [((OWNERS, share, width), BF16)], flops=300_000_000, bytes_accessed=1_000_000
    )
    plane = added(lax.all_to_all(chip_grad, X + ("z",), 0, 0, tiled=True), BF16)
    planes = lax.all_to_all(jnp.broadcast_to(plane, (NY,) + plane.shape), Y, 0, 0, tiled=True)
    grads = lax.all_gather(added(planes, F32), "c", axis=0)
    return hidden, grads[0], grads[1]


def solution(mesh):
    axes = ("z",) + X + Y + ("c",)
    fine = Mesh(mesh.devices.reshape(NZ, 2, 2, 2, 2, 2, NC), axes)
    row, rep = ("z",) + X, Y + ("c",)
    nodes = P(row + rep, None)
    in_specs = (nodes, nodes, nodes, P(row, rep, None, None), P(row, rep, None), P(), P(), nodes)
    out_specs = (nodes, P(row, None), P(row, None))
    return jax.shard_map(body, mesh=fine, in_specs=in_specs, out_specs=out_specs, check_vma=False)
```

```python
import functools

import jax
import jax.numpy as jnp
from jax import lax
from jax.experimental import pallas as pl
from jax.experimental.pallas import tpu as pltpu
from jax.sharding import Mesh, PartitionSpec as P

NZ, NX, NY, NC = 8, 4, 8, 2
OWNERS = NZ * NX
GROUPS = NY * NC
T = 128
K_LOC = 12
K_REM = 4
CAP = 2
TOLD = 16
X, Y = ("x1", "x0"), ("y2", "y1", "y0")
F32 = jnp.float32
BF16 = jnp.bfloat16
VMEM_LIMIT = 16 * 1024 * 1024


def vmem_call(
    kernel, name, scalar_inputs, array_inputs, outputs, scratch=(), anywhere=(), outside=0, flops=0, bytes_accessed=0, transcendentals=0
):
    vmem = pl.BlockSpec(memory_space=pltpu.VMEM)
    return pl.pallas_call(
        kernel,
        in_specs=[pl.BlockSpec(memory_space=pltpu.SMEM)] * len(scalar_inputs)
        + [pl.BlockSpec(memory_space=pltpu.HBM)] * len(anywhere)
        + [vmem] * len(array_inputs),
        out_specs=[vmem] * (len(outputs) - outside) + [pl.BlockSpec(memory_space=pltpu.HBM)] * outside,
        out_shape=[jax.ShapeDtypeStruct(*of) for of in outputs[: len(outputs) - outside]]
        + [pltpu.HBM(*of) for of in outputs[len(outputs) - outside :]],
        scratch_shapes=list(scratch),
        compiler_params=pltpu.CompilerParams(vmem_limit_bytes=VMEM_LIMIT),
        cost_estimate=pl.CostEstimate(flops=flops, bytes_accessed=bytes_accessed, transcendentals=transcendentals),
        name=name,
    )(*scalar_inputs, *anywhere, *array_inputs)


def spread_kernel(features_ref, features_out, quarters_ref, features_t, sems):
    features_t[...] = features_ref[...].astype(F32).T.astype(BF16).reshape(NX, T, T)
    copies = [pltpu.make_async_copy(features_t, quarters_ref.at[:, z], sems.at[z]) for z in range(NZ)]
    copies.append(pltpu.make_async_copy(features_t, features_out, sems.at[NZ]))
    for copy in copies:
        copy.start()
    for copy in copies:
        copy.wait()


def split_kernel(codes_ref, remote_ref, local_ref, sems):
    copies = []
    for x in range(NX):
        codes = codes_ref.at[x % 2, x // 2]
        copies.append(pltpu.make_async_copy(codes.at[TOLD:], local_ref.at[x], sems.at[x]))
        copies[-1].start()
        remote_ref[x] = codes[0:TOLD]
    for copy in copies:
        copy.wait()


def remote_product(core, here, before, blocks_ref, told_ref, x, y):
    group = y * NC + core[0]
    first = jnp.clip(here[x, GROUPS + group * CAP], 0, OWNERS - 1)
    second = jnp.clip(here[x, GROUPS + group * CAP + 1], 0, OWNERS - 1)
    start, count = before[x, group].astype(F32), here[x, group].astype(F32)
    told = told_ref[group, x].astype(F32)
    entry = told[0:K_REM] - start
    row = jnp.where(entry < count, entry * T + told[K_REM : 2 * K_REM], -1.0).astype(jnp.int16)
    weight = told[2 * K_REM : 3 * K_REM].astype(BF16)
    rows = lax.broadcasted_iota(jnp.int16, (CAP * T, T), 0)
    hot = jnp.zeros((CAP * T, T), BF16)
    for slot in range(K_REM):
        hot = jnp.where(rows == row[slot : slot + 1], weight[slot : slot + 1], hot)
    first, second = (lax.rem(p, NX) * NZ + lax.div(p, NX) for p in (first, second))
    pair = jnp.concatenate([blocks_ref[first], blocks_ref[second]], axis=1)
    return jnp.dot(pair, hot, preferred_element_type=F32)


def first_kernel(core, here, before, blocks_ref, told_ref, part_ref):
    for y in range(NY):
        for x in range(NX):
            part_ref[x, y] = remote_product(core, here, before, blocks_ref, told_ref, x, y)


def second_kernel(core, here, before, blocks_ref, told_ref, part_ref, sums_ref, sums, sems):
    copies = []
    for y in range(NY):
        for x in range(NX):
            sums[y, x] = (part_ref[x, y] + remote_product(core, here, before, blocks_ref, told_ref, x, y)).astype(BF16)
        copies.append(pltpu.make_async_copy(sums.at[y], sums_ref.at[y], sems.at[y]))
        copies[-1].start()
    for copy in copies:
        copy.wait()


def local_kernel(k, outside, scalars, blocks_ref, told_ref, out, hot_ref, total=None, sem=None):
    x = lax.rem(scalars[1] + (NX - k), NX)
    owner = scalars[0] * NX + x
    rows = lax.broadcasted_iota(jnp.int16, (T, T), 0)
    lanes = lax.broadcasted_iota(jnp.int32, (1, T), 1).astype(F32)
    ones, zeros = jnp.ones((T, T), BF16), jnp.zeros((T, T), BF16)
    block, row, weight = (told_ref[x, n * 16 : n * 16 + 16, :].astype(F32) for n in range(3))
    weight = weight.astype(BF16)

    def of_four(i, summed):
        for j in range(4):
            p = lax.rem(4 * i + j, NZ) * NX + lax.div(4 * i + j, NZ)
            code = ((block - p.astype(F32)) * T + row).astype(jnp.int16)
            own = (lanes - jnp.where(p == owner, 0.0, 1024.0)).astype(jnp.int16)
            hot = jnp.where(rows == own, ones, zeros)
            for slot in range(K_LOC):
                hot = jnp.where(rows == code[slot : slot + 1], weight[slot : slot + 1], hot)
            hot_ref[j * T : (j + 1) * T, :] = hot
        four = jnp.concatenate([blocks_ref[4 * i + j] for j in range(4)], axis=1)
        return summed + jnp.dot(four, hot_ref[...], preferred_element_type=F32)

    summed = lax.fori_loop(0, OWNERS // 4, of_four, jnp.zeros((T, T), F32), unroll=2)
    if outside:
        total[...] = summed
        copy = pltpu.make_async_copy(total, out, sem)
        copy.start()
        copy.wait()
    else:
        out[...] = summed


def dense_kernel(
    scalars, near_0_in, weights_in, from_self_in, features_t_in, arrived, near_1, near_2, near_3, w_agg, cotangent,
    preact_ref, send_ref, keep_ref, agg_t, near_0, weights_t, from_self, features_t, sems,
):
    own_x, own_c = scalars[0], scalars[1]
    sources = (near_0_in, weights_in, from_self_in, features_t_in)
    targets = (near_0, weights_t, from_self, features_t)
    copies = [pltpu.make_async_copy(of, to, sems.at[i]) for i, (of, to) in enumerate(zip(sources, targets))]
    for copy in copies:
        copy.start()

    for x in range(NX):
        summed = arrived[0, x].astype(F32)
        for y in range(1, NY):
            summed = summed + arrived[y, x].astype(F32)
        agg_t[x * T : (x + 1) * T, :] = summed
    for k, near in ((1, near_1), (2, near_2), (3, near_3), (0, near_0)):
        if k == 0:
            copies[0].wait()
        quarter = lax.rem(own_x + (NX - k), NX)
        agg_t[pl.ds(pl.multiple_of(quarter * T, T), T), :] += near[...]
    copies[1].wait()
    degree = 1.0 + jnp.sum(weights_t[...].astype(F32), axis=0, keepdims=True)
    aggregate = (agg_t[...] / degree).astype(BF16)
    contract = (((0,), (0,)), ((), ()))
    preact = lax.dot_general(aggregate, w_agg[...], contract, preferred_element_type=F32)
    copies[2].wait()
    preact = preact + from_self[...]
    preact_ref[...] = preact
    sigma = jax.nn.sigmoid(preact)
    grad_pre = (cotangent[...].astype(F32) * sigma * (1.0 + preact * (1.0 - sigma))).astype(BF16)
    copies[3].wait()
    for j in range(NX):
        columns = grad_pre[:, j * T : (j + 1) * T]
        keep_ref[NX + j] = columns
        send_ref[NX + j] = columns
        of_agg, of_self = aggregate[j * T : (j + 1) * T, :], features_t[j]
        keep_ref[j] = jnp.where(own_c == 0, of_agg, of_self)
        send_ref[j] = jnp.where(own_c == 0, of_self, of_agg)


def self_kernel(features, w_self, out_ref, product, sem):
    product[...] = jnp.dot(features[...], w_self[...], preferred_element_type=F32)
    copy = pltpu.make_async_copy(product, out_ref, sem)
    copy.start()
    copy.wait()


def hidden_kernel(preact_ref, hidden_ref):
    preact = preact_ref[...]
    hidden_ref[...] = (preact * jax.nn.sigmoid(preact)).astype(BF16)


def grad_kernel(keep_ref, received_ref, grad_ref):
    both = (keep_ref, received_ref)
    left = jnp.concatenate([ref[0:NX].reshape(NX * T, T) for ref in both], axis=1)
    for j in range(NX):
        right = jnp.concatenate([ref[NX + j] for ref in both], axis=0)
        product = jnp.dot(left, right, preferred_element_type=F32)
        shares = product.astype(BF16).reshape(NZ, NX, grad_ref.shape[1], T)
        for x in range(NX):
            grad_ref[x * NZ : (x + 1) * NZ, :, j * T : (j + 1) * T] = shares[:, x]


def add_kernel(parts_ref, sum_ref):
    summed = parts_ref[0].astype(F32)
    for i in range(1, parts_ref.shape[0]):
        summed = summed + parts_ref[i].astype(F32)
    sum_ref[...] = summed.astype(sum_ref.dtype)


def added(parts, dtype):
    (summed,) = vmem_call(
        add_kernel, "added", [], [parts], [(parts.shape[1:], dtype)], flops=parts.size, bytes_accessed=3 * parts.size
    )
    return summed


def body(features, edge_weights, neighbours, send_list, send_count, w_agg, w_self, cotangent):
    width = features.shape[1]
    z, x, y, c = (lax.axis_index(a).astype(jnp.int32) for a in ("z", X, Y, "c"))
    swap = [(0, 1), (1, 0)]

    features_t, quarters = vmem_call(
        spread_kernel, "spread", [], [features], [((NX, T, T), BF16), ((NX, NZ, T, T), BF16)],
        scratch=[pltpu.VMEM((NX, T, T), BF16), pltpu.SemaphoreType.DMA((NZ + 1,))], outside=2, bytes_accessed=1_500_000,
    )
    blocks = lax.all_to_all(quarters.reshape(OWNERS, T, T), X + ("z",), 0, 0, tiled=True)

    codes_t = neighbours.T
    weights_t = edge_weights.T
    told = jnp.concatenate([send_count[0], send_list[0].reshape(1, GROUPS * CAP)], axis=1).astype(BF16)
    told = jnp.pad(told, ((0, 3), (0, T - GROUPS * (1 + CAP))))
    block, row = (codes_t // T).astype(BF16), (codes_t % T).astype(BF16)
    gap = jnp.zeros((16 - K_LOC, T), BF16)
    of_remote = jnp.concatenate([block[K_LOC:], row[K_LOC:], weights_t[K_LOC:], told], axis=0)
    of_local = jnp.concatenate([block[:K_LOC], gap, row[:K_LOC], gap, weights_t[:K_LOC], gap], axis=0)
    codes = jnp.concatenate([of_remote, of_local], axis=0)
    forward = [[(i, (i + k) % NX) for i in range(NX)] for k in range(NX)]
    codes = lax.all_gather(lax.all_gather(codes, "x1", axis=0), "x0", axis=0)
    remote_codes, local_codes = vmem_call(
        split_kernel, "split", [], [codes], [((NX, TOLD, T), BF16), ((NX, 48, T), BF16)],
        scratch=[pltpu.SemaphoreType.DMA((NX,))], outside=1, bytes_accessed=100_000,
    )
    remote_codes = lax.all_gather(remote_codes, Y + ("c",), axis=0)
    blocks, remote_codes = lax.optimization_barrier((blocks, remote_codes))
    told = remote_codes[:, :, 12].astype(jnp.int32)
    sources = jnp.arange(GROUPS, dtype=jnp.int32)[:, None, None]

    def of_source(group):
        here = jnp.sum(jnp.where(sources == group, told, 0), axis=0)
        return here, jnp.sum(jnp.where(sources < group, told[:, :, :GROUPS], 0), axis=0)

    core = c[None]
    others = lax.ppermute(blocks, "c", swap)
    (part,) = vmem_call(
        first_kernel, "own_group", [core, *of_source(y * NC + c)], [blocks, remote_codes], [((NX, NY, T, T), F32)],
        flops=300_000_000, bytes_accessed=3_500_000,
    )
    (chip_sum,) = vmem_call(
        second_kernel, "other_group", [core, *of_source(y * NC + 1 - c)], [others, remote_codes, part], [((NY, NX, T, T), BF16)],
        scratch=[pltpu.VMEM((NY, NX, T, T), BF16), pltpu.SemaphoreType.DMA((NY,))], outside=1,
        flops=300_000_000, bytes_accessed=5_500_000,
    )
    arrived = lax.all_to_all(chip_sum.reshape(NX * NY, T, T), Y + X, 0, 0, tiled=True)

    features_later, _ = lax.optimization_barrier((features, chip_sum))
    near = []
    for k in (2, 1, 3, 0):
        (sums,) = vmem_call(
            functools.partial(local_kernel, k, k == 0), "local_sums", [jnp.stack([z, x])], [blocks, local_codes],
            [((T, T), F32)],
            scratch=[pltpu.VMEM((4 * T, T), BF16)] + ([] if k else [pltpu.VMEM((T, T), F32), pltpu.SemaphoreType.DMA]),
            outside=int(k == 0), flops=150_000_000, bytes_accessed=1_200_000,
        )
        near.append(lax.ppermute(sums, X, forward[NX - k]) if k else sums)
    two, three, one, near_0 = near

    share = width // OWNERS
    operands = ((2 * NX, T, T), BF16)
    (from_self,) = vmem_call(
        self_kernel, "from_self", [], [features_later, w_self], [((T, width), F32)],
        scratch=[pltpu.VMEM((T, width), F32), pltpu.SemaphoreType.DMA], outside=1, flops=67_000_000, bytes_accessed=900_000,
    )
    arrived, x, c = lax.optimization_barrier((arrived, x, c))
    outside = [near_0, weights_t, from_self, features_t]
    preact, send, keep = vmem_call(
        dense_kernel, "dense", [jnp.stack([x, c])], [arrived.reshape(NY, NX, T, T), one, two, three, w_agg, cotangent],
        [((T, width), F32), operands, operands],
        scratch=[pltpu.VMEM((width, T), F32)]
        + [pltpu.VMEM(of.shape, of.dtype) for of in outside]
        + [pltpu.SemaphoreType.DMA((len(outside),))],
        anywhere=[pltpu.with_memory_space_constraint(of, pltpu.HBM) for of in outside],
        flops=150_000_000, bytes_accessed=3_500_000, transcendentals=65536,
    )
    received = lax.ppermute(send, "c", swap)
    (hidden,) = vmem_call(hidden_kernel, "hidden", [], [preact], [((T, width), BF16)], flops=1_000_000, bytes_accessed=400_000, transcendentals=65536)
    received, hidden = lax.optimization_barrier((received, hidden))
    (chip_grad,) = vmem_call(
        grad_kernel, "gradient", [], [keep, received], [((OWNERS, share, width), BF16)], flops=300_000_000, bytes_accessed=1_000_000
    )
    plane = added(lax.all_to_all(chip_grad, X + ("z",), 0, 0, tiled=True), BF16)
    planes = lax.all_to_all(jnp.broadcast_to(plane, (NY,) + plane.shape), Y, 0, 0, tiled=True)
    grads = lax.all_gather(added(planes, F32), "c", axis=0)
    return hidden, grads[0], grads[1]


def solution(mesh):
    axes = ("z",) + X + Y + ("c",)
    fine = Mesh(mesh.devices.reshape(NZ, 2, 2, 2, 2, 2, NC), axes)
    row, rep = ("z",) + X, Y + ("c",)
    nodes = P(row + rep, None)
    in_specs = (nodes, nodes, nodes, P(row, rep, None, None), P(row, rep, None), P(), P(), nodes)
    out_specs = (nodes, P(row, None), P(row, None))
    return jax.shard_map(body, mesh=fine, in_specs=in_specs, out_specs=out_specs, check_vma=False)
```

```python
import functools

import jax
import jax.numpy as jnp
from jax import lax
from jax.experimental import pallas as pl
from jax.experimental.pallas import tpu as pltpu
from jax.sharding import Mesh, PartitionSpec as P

NZ, NX, NY, NC = 8, 4, 8, 2
OWNERS = NZ * NX
GROUPS = NY * NC
T = 128
K_LOC = 12
K_REM = 4
CAP = 2
TOLD = 16
X, Y = ("x1", "x0"), ("y2", "y1", "y0")
F32 = jnp.float32
BF16 = jnp.bfloat16
VMEM_LIMIT = 16 * 1024 * 1024


def vmem_call(
    kernel, name, scalar_inputs, array_inputs, outputs, scratch=(), anywhere=(), outside=0, flops=0, bytes_accessed=0, transcendentals=0
):
    vmem = pl.BlockSpec(memory_space=pltpu.VMEM)
    return pl.pallas_call(
        kernel,
        in_specs=[pl.BlockSpec(memory_space=pltpu.SMEM)] * len(scalar_inputs)
        + [pl.BlockSpec(memory_space=pltpu.HBM)] * len(anywhere)
        + [vmem] * len(array_inputs),
        out_specs=[vmem] * (len(outputs) - outside) + [pl.BlockSpec(memory_space=pltpu.HBM)] * outside,
        out_shape=[jax.ShapeDtypeStruct(*of) for of in outputs[: len(outputs) - outside]]
        + [pltpu.HBM(*of) for of in outputs[len(outputs) - outside :]],
        scratch_shapes=list(scratch),
        compiler_params=pltpu.CompilerParams(vmem_limit_bytes=VMEM_LIMIT),
        cost_estimate=pl.CostEstimate(flops=flops, bytes_accessed=bytes_accessed, transcendentals=transcendentals),
        name=name,
    )(*scalar_inputs, *anywhere, *array_inputs)


def spread_kernel(features_ref, features_out, quarters_ref, features_t, sems):
    features_t[...] = features_ref[...].astype(F32).T.astype(BF16).reshape(NX, T, T)
    copies = [pltpu.make_async_copy(features_t, quarters_ref.at[z], sems.at[z]) for z in range(NZ)]
    copies.append(pltpu.make_async_copy(features_t, features_out, sems.at[NZ]))
    for copy in copies:
        copy.start()
    for copy in copies:
        copy.wait()


def split_kernel(codes_ref, remote_ref, local_ref, sems):
    copies = [pltpu.make_async_copy(codes_ref.at[i, :, TOLD:], local_ref.at[i], sems.at[i]) for i in range(2)]
    for copy in copies:
        copy.start()
    for x in range(NX):
        remote_ref[x] = codes_ref[x % 2, x // 2, 0:TOLD]
    for copy in copies:
        copy.wait()


def remote_product(core, here, before, blocks_ref, told_ref, x, y):
    group = y * NC + core[0]
    first = jnp.clip(here[x, GROUPS + group * CAP], 0, OWNERS - 1)
    second = jnp.clip(here[x, GROUPS + group * CAP + 1], 0, OWNERS - 1)
    start, count = before[x, group].astype(F32), here[x, group].astype(F32)
    told = told_ref[group, x].astype(F32)
    entry = told[0:K_REM] - start
    row = jnp.where(entry < count, entry * T + told[K_REM : 2 * K_REM], -1.0).astype(jnp.int16)
    weight = told[2 * K_REM : 3 * K_REM].astype(BF16)
    rows = lax.broadcasted_iota(jnp.int16, (CAP * T, T), 0)
    hot = jnp.zeros((CAP * T, T), BF16)
    for slot in range(K_REM):
        hot = jnp.where(rows == row[slot : slot + 1], weight[slot : slot + 1], hot)
    pair = jnp.concatenate([blocks_ref[first], blocks_ref[second]], axis=1)
    return jnp.dot(pair, hot, preferred_element_type=F32)


def first_kernel(core, here, before, blocks_ref, told_ref, part_ref):
    for y in range(NY):
        for x in range(NX):
            part_ref[x, y] = remote_product(core, here, before, blocks_ref, told_ref, x, y)


def second_kernel(core, here, before, blocks_ref, told_ref, part_ref, sums_ref, sums, sems):
    copies = []
    for y in range(NY):
        for x in range(NX):
            sums[y, x] = (part_ref[x, y] + remote_product(core, here, before, blocks_ref, told_ref, x, y)).astype(BF16)
        copies.append(pltpu.make_async_copy(sums.at[y], sums_ref.at[y], sems.at[y]))
        copies[-1].start()
    for copy in copies:
        copy.wait()


def local_kernel(k, outside, scalars, blocks_ref, told_ref, out, hot_ref, total=None, sem=None):
    x = lax.rem(scalars[1] + (NX - k), NX)
    owner = scalars[0] * NX + x
    rows = lax.broadcasted_iota(jnp.int16, (T, T), 0)
    lanes = lax.broadcasted_iota(jnp.int32, (1, T), 1).astype(F32)
    ones, zeros = jnp.ones((T, T), BF16), jnp.zeros((T, T), BF16)
    block, row, weight = (told_ref[lax.rem(x, 2), lax.div(x, 2), n * 16 : n * 16 + 16, :].astype(F32) for n in range(3))
    weight = weight.astype(BF16)

    def of_four(i, summed):
        for j in range(4):
            p = 4 * i + j
            code = ((block - p.astype(F32)) * T + row).astype(jnp.int16)
            own = (lanes - jnp.where(p == owner, 0.0, 1024.0)).astype(jnp.int16)
            hot = jnp.where(rows == own, ones, zeros)
            for slot in range(K_LOC):
                hot = jnp.where(rows == code[slot : slot + 1], weight[slot : slot + 1], hot)
            hot_ref[j * T : (j + 1) * T, :] = hot
        four = jnp.concatenate([blocks_ref[4 * i + j] for j in range(4)], axis=1)
        return summed + jnp.dot(four, hot_ref[...], preferred_element_type=F32)

    summed = lax.fori_loop(0, OWNERS // 4, of_four, jnp.zeros((T, T), F32), unroll=2)
    if outside:
        total[...] = summed
        copy = pltpu.make_async_copy(total, out, sem)
        copy.start()
        copy.wait()
    else:
        out[...] = summed


def dense_kernel(
    scalars, near_0_in, weights_in, from_self_in, features_t_in, arrived, near_1, near_2, near_3, w_agg, cotangent,
    preact_ref, send_ref, keep_ref, agg_t, near_0, weights_t, from_self, features_t, sems,
):
    own_x, own_c = scalars[0], scalars[1]
    sources = (near_0_in, weights_in, from_self_in, features_t_in)
    targets = (near_0, weights_t, from_self, features_t)
    copies = [pltpu.make_async_copy(of, to, sems.at[i]) for i, (of, to) in enumerate(zip(sources, targets))]
    for copy in copies:
        copy.start()

    for x in range(NX):
        summed = arrived[0, x].astype(F32)
        for y in range(1, NY):
            summed = summed + arrived[y, x].astype(F32)
        agg_t[x * T : (x + 1) * T, :] = summed
    for k, near in ((1, near_1), (2, near_2), (3, near_3), (0, near_0)):
        if k == 0:
            copies[0].wait()
        quarter = lax.rem(own_x + (NX - k), NX)
        agg_t[pl.ds(pl.multiple_of(quarter * T, T), T), :] += near[...]
    copies[1].wait()
    degree = 1.0 + jnp.sum(weights_t[...].astype(F32), axis=0, keepdims=True)
    aggregate = (agg_t[...] / degree).astype(BF16)
    contract = (((0,), (0,)), ((), ()))
    preact = lax.dot_general(aggregate, w_agg[...], contract, preferred_element_type=F32)
    copies[2].wait()
    preact = preact + from_self[...]
    preact_ref[...] = preact
    sigma = jax.nn.sigmoid(preact)
    grad_pre = (cotangent[...].astype(F32) * sigma * (1.0 + preact * (1.0 - sigma))).astype(BF16)
    copies[3].wait()
    for j in range(NX):
        columns = grad_pre[:, j * T : (j + 1) * T]
        keep_ref[NX + j] = columns
        send_ref[NX + j] = columns
        of_agg, of_self = aggregate[j * T : (j + 1) * T, :], features_t[j]
        keep_ref[j] = jnp.where(own_c == 0, of_agg, of_self)
        send_ref[j] = jnp.where(own_c == 0, of_self, of_agg)


def self_kernel(features, w_self, out_ref, product, sem):
    product[...] = jnp.dot(features[...], w_self[...], preferred_element_type=F32)
    copy = pltpu.make_async_copy(product, out_ref, sem)
    copy.start()
    copy.wait()


def hidden_kernel(preact_ref, hidden_ref):
    preact = preact_ref[...]
    hidden_ref[...] = (preact * jax.nn.sigmoid(preact)).astype(BF16)


def grad_kernel(keep_ref, received_ref, grad_ref):
    both = (keep_ref, received_ref)
    left = jnp.concatenate([ref[0:NX].reshape(NX * T, T) for ref in both], axis=1)
    for j in range(NX):
        right = jnp.concatenate([ref[NX + j] for ref in both], axis=0)
        product = jnp.dot(left, right, preferred_element_type=F32)
        shares = product.astype(BF16).reshape(NZ, NX, grad_ref.shape[1], T)
        for x in range(NX):
            grad_ref[x * NZ : (x + 1) * NZ, :, j * T : (j + 1) * T] = shares[:, x]


def add_kernel(parts_ref, sum_ref):
    summed = parts_ref[0].astype(F32)
    for i in range(1, parts_ref.shape[0]):
        summed = summed + parts_ref[i].astype(F32)
    sum_ref[...] = jnp.broadcast_to(summed.astype(sum_ref.dtype), sum_ref.shape)


def added(parts, dtype, copies=()):
    (summed,) = vmem_call(
        add_kernel, "added", [], [parts], [(copies + parts.shape[1:], dtype)], flops=parts.size, bytes_accessed=3 * parts.size
    )
    return summed


def body(features, edge_weights, neighbours, send_list, send_count, w_agg, w_self, cotangent):
    width = features.shape[1]
    z, x, y, c = (lax.axis_index(a).astype(jnp.int32) for a in ("z", X, Y, "c"))
    swap = [(0, 1), (1, 0)]

    features_t, quarters = vmem_call(
        spread_kernel, "spread", [], [features], [((NX, T, T), BF16), ((NZ, NX, T, T), BF16)],
        scratch=[pltpu.VMEM((NX, T, T), BF16), pltpu.SemaphoreType.DMA((NZ + 1,))], outside=2, bytes_accessed=1_500_000,
    )
    blocks = lax.all_to_all(quarters.reshape(OWNERS, T, T), ("z",) + X, 0, 0, tiled=True)

    codes_t = neighbours.T
    weights_t = edge_weights.T
    told = jnp.concatenate([send_count[0], send_list[0].reshape(1, GROUPS * CAP)], axis=1).astype(BF16)
    told = jnp.pad(told, ((0, 3), (0, T - GROUPS * (1 + CAP))))
    block, row = (codes_t // T).astype(BF16), (codes_t % T).astype(BF16)
    gap = jnp.zeros((16 - K_LOC, T), BF16)
    of_remote = jnp.concatenate([block[K_LOC:], row[K_LOC:], weights_t[K_LOC:], told], axis=0)
    of_local = jnp.concatenate([block[:K_LOC], gap, row[:K_LOC], gap, weights_t[:K_LOC], gap], axis=0)
    codes = jnp.concatenate([of_remote, of_local], axis=0)
    forward = [[(i, (i + k) % NX) for i in range(NX)] for k in range(NX)]
    codes = lax.all_gather(lax.all_gather(codes, "x1", axis=0), "x0", axis=0)
    remote_codes, local_codes = vmem_call(
        split_kernel, "split", [], [codes], [((NX, TOLD, T), BF16), ((2, 2, 48, T), BF16)],
        scratch=[pltpu.SemaphoreType.DMA((2,))], outside=1, bytes_accessed=100_000,
    )
    remote_codes = lax.all_gather(remote_codes, Y + ("c",), axis=0)
    blocks, remote_codes = lax.optimization_barrier((blocks, remote_codes))
    told = remote_codes[:, :, 12].astype(jnp.int32)
    sources = jnp.arange(GROUPS, dtype=jnp.int32)[:, None, None]

    def of_source(group):
        here = jnp.sum(jnp.where(sources == group, told, 0), axis=0)
        return here, jnp.sum(jnp.where(sources < group, told[:, :, :GROUPS], 0), axis=0)

    core = c[None]
    others = lax.ppermute(blocks, "c", swap)
    (part,) = vmem_call(
        first_kernel, "own_group", [core, *of_source(y * NC + c)], [blocks, remote_codes], [((NX, NY, T, T), F32)],
        flops=300_000_000, bytes_accessed=3_500_000,
    )
    (chip_sum,) = vmem_call(
        second_kernel, "other_group", [core, *of_source(y * NC + 1 - c)], [others, remote_codes, part], [((NY, NX, T, T), BF16)],
        scratch=[pltpu.VMEM((NY, NX, T, T), BF16), pltpu.SemaphoreType.DMA((NY,))], outside=1,
        flops=300_000_000, bytes_accessed=5_500_000,
    )
    arrived = lax.all_to_all(chip_sum.reshape(NX * NY, T, T), Y + X, 0, 0, tiled=True)

    features_later, _ = lax.optimization_barrier((features, chip_sum))
    near = []
    for k in (2, 1, 3, 0):
        (sums,) = vmem_call(
            functools.partial(local_kernel, k, k == 0), "local_sums", [jnp.stack([z, x])], [blocks, local_codes],
            [((T, T), F32)],
            scratch=[pltpu.VMEM((4 * T, T), BF16)] + ([] if k else [pltpu.VMEM((T, T), F32), pltpu.SemaphoreType.DMA]),
            outside=int(k == 0), flops=150_000_000, bytes_accessed=1_200_000,
        )
        near.append(lax.ppermute(sums, X, forward[NX - k]) if k else sums)
    two, three, one, near_0 = near

    share = width // OWNERS
    operands = ((2 * NX, T, T), BF16)
    (from_self,) = vmem_call(
        self_kernel, "from_self", [], [features_later, w_self], [((T, width), F32)],
        scratch=[pltpu.VMEM((T, width), F32), pltpu.SemaphoreType.DMA], outside=1, flops=67_000_000, bytes_accessed=900_000,
    )
    arrived, x, c = lax.optimization_barrier((arrived, x, c))
    outside = [near_0, weights_t, from_self, features_t]
    preact, send, keep = vmem_call(
        dense_kernel, "dense", [jnp.stack([x, c])], [arrived.reshape(NY, NX, T, T), one, two, three, w_agg, cotangent],
        [((T, width), F32), operands, operands],
        scratch=[pltpu.VMEM((width, T), F32)]
        + [pltpu.VMEM(of.shape, of.dtype) for of in outside]
        + [pltpu.SemaphoreType.DMA((len(outside),))],
        anywhere=[pltpu.with_memory_space_constraint(of, pltpu.HBM) for of in outside],
        flops=150_000_000, bytes_accessed=3_500_000, transcendentals=65536,
    )
    received = lax.ppermute(send, "c", swap)
    (hidden,) = vmem_call(hidden_kernel, "hidden", [], [preact], [((T, width), BF16)], flops=1_000_000, bytes_accessed=400_000, transcendentals=65536)
    received, hidden = lax.optimization_barrier((received, hidden))
    (chip_grad,) = vmem_call(
        grad_kernel, "gradient", [], [keep, received], [((OWNERS, share, width), BF16)], flops=300_000_000, bytes_accessed=1_000_000
    )
    planes = added(lax.all_to_all(chip_grad, X + ("z",), 0, 0, tiled=True), BF16, (NY,))
    planes = lax.all_to_all(planes, Y, 0, 0, tiled=True)
    grads = lax.all_gather(added(planes, F32), "c", axis=0)
    return hidden, grads[0], grads[1]


def solution(mesh):
    axes = ("z",) + X + Y + ("c",)
    fine = Mesh(mesh.devices.reshape(NZ, 2, 2, 2, 2, 2, NC), axes)
    row, rep = ("z",) + X, Y + ("c",)
    nodes = P(row + rep, None)
    in_specs = (nodes, nodes, nodes, P(row, rep, None, None), P(row, rep, None), P(), P(), nodes)
    out_specs = (nodes, P(row, None), P(row, None))
    return jax.shard_map(body, mesh=fine, in_specs=in_specs, out_specs=out_specs, check_vma=False)
```

```python
import functools

import jax
import jax.numpy as jnp
from jax import lax
from jax.experimental import pallas as pl
from jax.experimental.pallas import tpu as pltpu
from jax.sharding import Mesh, PartitionSpec as P

NZ, NX, NY, NC = 8, 4, 8, 2
OWNERS = NZ * NX
GROUPS = NY * NC
T = 128
K_LOC = 12
K_REM = 4
CAP = 2
TOLD = 16
X, Y = ("x1", "x0"), ("y2", "y1", "y0")
F32 = jnp.float32
BF16 = jnp.bfloat16
VMEM_LIMIT = 16 * 1024 * 1024


def vmem_call(
    kernel, name, scalar_inputs, array_inputs, outputs, scratch=(), anywhere=(), outside=0, flops=0, bytes_accessed=0, transcendentals=0
):
    vmem = pl.BlockSpec(memory_space=pltpu.VMEM)
    return pl.pallas_call(
        kernel,
        in_specs=[pl.BlockSpec(memory_space=pltpu.SMEM)] * len(scalar_inputs)
        + [pl.BlockSpec(memory_space=pltpu.HBM)] * len(anywhere)
        + [vmem] * len(array_inputs),
        out_specs=[vmem] * (len(outputs) - outside) + [pl.BlockSpec(memory_space=pltpu.HBM)] * outside,
        out_shape=[jax.ShapeDtypeStruct(*of) for of in outputs[: len(outputs) - outside]]
        + [pltpu.HBM(*of) for of in outputs[len(outputs) - outside :]],
        scratch_shapes=list(scratch),
        compiler_params=pltpu.CompilerParams(vmem_limit_bytes=VMEM_LIMIT),
        cost_estimate=pl.CostEstimate(flops=flops, bytes_accessed=bytes_accessed, transcendentals=transcendentals),
        name=name,
    )(*scalar_inputs, *anywhere, *array_inputs)


def spread_kernel(features_ref, features_out, quarters_ref, features_t, sems):
    features_t[...] = features_ref[...].astype(F32).T.astype(BF16).reshape(NX, T, T)
    copies = [pltpu.make_async_copy(features_t, quarters_ref.at[z], sems.at[z]) for z in range(NZ)]
    copies.append(pltpu.make_async_copy(features_t, features_out, sems.at[NZ]))
    for copy in copies:
        copy.start()
    for copy in copies:
        copy.wait()


def split_kernel(codes_ref, remote_ref, local_ref, sems):
    copies = [pltpu.make_async_copy(codes_ref.at[i, :, TOLD:], local_ref.at[i], sems.at[i]) for i in range(2)]
    for copy in copies:
        copy.start()
    for x in range(NX):
        remote_ref[x] = codes_ref[x % 2, x // 2, 0:TOLD]
    for copy in copies:
        copy.wait()


def remote_product(core, here, before, blocks_ref, told_ref, x, y):
    group = y * NC + core[0]
    first = jnp.clip(here[x, GROUPS + group * CAP], 0, OWNERS - 1)
    second = jnp.clip(here[x, GROUPS + group * CAP + 1], 0, OWNERS - 1)
    start, count = before[x, group].astype(F32), here[x, group].astype(F32)
    told = told_ref[group, x].astype(F32)
    entry = told[0:K_REM] - start
    row = jnp.where(entry < count, entry * T + told[K_REM : 2 * K_REM], -1.0).astype(jnp.int16)
    weight = told[2 * K_REM : 3 * K_REM].astype(BF16)
    rows = lax.broadcasted_iota(jnp.int16, (CAP * T, T), 0)
    hot = jnp.zeros((CAP * T, T), BF16)
    for slot in range(K_REM):
        hot = jnp.where(rows == row[slot : slot + 1], weight[slot : slot + 1], hot)
    pair = jnp.concatenate([blocks_ref[first], blocks_ref[second]], axis=1)
    return jnp.dot(pair, hot, preferred_element_type=F32)


def first_kernel(core, here, before, blocks_ref, told_ref, part_ref):
    for y in range(NY):
        for x in range(NX):
            part_ref[x, y] = remote_product(core, here, before, blocks_ref, told_ref, x, y)


def second_kernel(core, here, before, blocks_ref, told_ref, part_ref, sums_ref, sums, sems):
    copies = []
    for y in range(NY):
        for x in range(NX):
            sums[y, x] = (part_ref[x, y] + remote_product(core, here, before, blocks_ref, told_ref, x, y)).astype(BF16)
        copies.append(pltpu.make_async_copy(sums.at[y], sums_ref.at[y], sems.at[y]))
        copies[-1].start()
    for copy in copies:
        copy.wait()


def local_kernel(k, outside, scalars, blocks_ref, told_ref, out, hot_ref, total=None, sem=None):
    x = lax.rem(scalars[1] + (NX - k), NX)
    owner = scalars[0] * NX + x
    rows = lax.broadcasted_iota(jnp.int16, (T, T), 0)
    lanes = lax.broadcasted_iota(jnp.int32, (1, T), 1).astype(F32)
    ones, zeros = jnp.ones((T, T), BF16), jnp.zeros((T, T), BF16)
    block, row, weight = (told_ref[lax.rem(x, 2), lax.div(x, 2), n * 16 : n * 16 + 16, :].astype(F32) for n in range(3))
    weight = weight.astype(BF16)

    def of_four(i, summed):
        for j in range(4):
            p = 4 * i + j
            code = ((block - p.astype(F32)) * T + row).astype(jnp.int16)
            own = (lanes - jnp.where(p == owner, 0.0, 1024.0)).astype(jnp.int16)
            hot = jnp.where(rows == own, ones, zeros)
            for slot in range(K_LOC):
                hot = jnp.where(rows == code[slot : slot + 1], weight[slot : slot + 1], hot)
            hot_ref[j * T : (j + 1) * T, :] = hot
        four = jnp.concatenate([blocks_ref[4 * i + j] for j in range(4)], axis=1)
        return summed + jnp.dot(four, hot_ref[...], preferred_element_type=F32)

    summed = lax.fori_loop(0, OWNERS // 4, of_four, jnp.zeros((T, T), F32), unroll=2)
    if outside:
        total[...] = summed
        copy = pltpu.make_async_copy(total, out, sem)
        copy.start()
        copy.wait()
    else:
        out[...] = summed


def dense_kernel(
    scalars, near_0_in, weights_in, from_self_in, features_t_in, arrived, near_1, near_2, near_3, w_agg, cotangent,
    preact_ref, send_ref, keep_ref, agg_t, near_0, weights_t, from_self, features_t, sems,
):
    own_x, own_c = scalars[0], scalars[1]
    sources = (near_0_in, weights_in, from_self_in, features_t_in)
    targets = (near_0, weights_t, from_self, features_t)
    copies = [pltpu.make_async_copy(of, to, sems.at[i]) for i, (of, to) in enumerate(zip(sources, targets))]
    for copy in copies:
        copy.start()

    for x in range(NX):
        summed = arrived[0, x].astype(F32)
        for y in range(1, NY):
            summed = summed + arrived[y, x].astype(F32)
        agg_t[x * T : (x + 1) * T, :] = summed
    for k, near in ((1, near_1), (2, near_2), (3, near_3), (0, near_0)):
        if k == 0:
            copies[0].wait()
        quarter = lax.rem(own_x + (NX - k), NX)
        agg_t[pl.ds(pl.multiple_of(quarter * T, T), T), :] += near[...]
    copies[1].wait()
    degree = 1.0 + jnp.sum(weights_t[...].astype(F32), axis=0, keepdims=True)
    aggregate = (agg_t[...] / degree).astype(BF16)
    contract = (((0,), (0,)), ((), ()))
    preact = lax.dot_general(aggregate, w_agg[...], contract, preferred_element_type=F32)
    copies[2].wait()
    preact = preact + from_self[...]
    preact_ref[...] = preact
    sigma = jax.nn.sigmoid(preact)
    grad_pre = (cotangent[...].astype(F32) * sigma * (1.0 + preact * (1.0 - sigma))).astype(BF16)
    copies[3].wait()
    for j in range(NX):
        columns = grad_pre[:, j * T : (j + 1) * T]
        keep_ref[NX + j] = columns
        send_ref[NX + j] = columns
        of_agg, of_self = aggregate[j * T : (j + 1) * T, :], features_t[j]
        keep_ref[j] = jnp.where(own_c == 0, of_agg, of_self)
        send_ref[j] = jnp.where(own_c == 0, of_self, of_agg)


def self_kernel(features, w_self, out_ref, product, sem):
    product[...] = jnp.dot(features[...], w_self[...], preferred_element_type=F32)
    copy = pltpu.make_async_copy(product, out_ref, sem)
    copy.start()
    copy.wait()


def hidden_kernel(preact_ref, hidden_ref):
    preact = preact_ref[...]
    hidden_ref[...] = (preact * jax.nn.sigmoid(preact)).astype(BF16)


def grad_kernel(keep_ref, received_ref, grad_ref):
    both = (keep_ref, received_ref)
    left = jnp.concatenate([ref[0:NX].reshape(NX * T, T) for ref in both], axis=1)
    for j in range(NX):
        right = jnp.concatenate([ref[NX + j] for ref in both], axis=0)
        product = jnp.dot(left, right, preferred_element_type=F32)
        shares = product.astype(BF16).reshape(NZ, NX, grad_ref.shape[1], T)
        for x in range(NX):
            grad_ref[x * NZ : (x + 1) * NZ, :, j * T : (j + 1) * T] = shares[:, x]


def add_kernel(parts_ref, sum_ref):
    summed = parts_ref[0].astype(F32)
    for i in range(1, parts_ref.shape[0]):
        summed = summed + parts_ref[i].astype(F32)
    sum_ref[...] = jnp.broadcast_to(summed.astype(sum_ref.dtype), sum_ref.shape)


def added(parts, dtype, copies=()):
    (summed,) = vmem_call(
        add_kernel, "added", [], [parts], [(copies + parts.shape[1:], dtype)], flops=parts.size, bytes_accessed=3 * parts.size
    )
    return summed


def body(features, edge_weights, neighbours, send_list, send_count, w_agg, w_self, cotangent):
    width = features.shape[1]
    z, x, y, c = (lax.axis_index(a).astype(jnp.int32) for a in ("z", X, Y, "c"))
    swap = [(0, 1), (1, 0)]

    features_t, quarters = vmem_call(
        spread_kernel, "spread", [], [features], [((NX, T, T), BF16), ((NZ, NX, T, T), BF16)],
        scratch=[pltpu.VMEM((NX, T, T), BF16), pltpu.SemaphoreType.DMA((NZ + 1,))], outside=2, bytes_accessed=1_500_000,
    )
    blocks = lax.all_to_all(quarters.reshape(OWNERS, T, T), ("z",) + X, 0, 0, tiled=True)

    codes_t = neighbours.T
    weights_t = edge_weights.T
    told = jnp.concatenate([send_count[0], send_list[0].reshape(1, GROUPS * CAP)], axis=1).astype(BF16)
    told = jnp.pad(told, ((0, 3), (0, T - GROUPS * (1 + CAP))))
    block, row = (codes_t // T).astype(BF16), (codes_t % T).astype(BF16)
    gap = jnp.zeros((16 - K_LOC, T), BF16)
    of_remote = jnp.concatenate([block[K_LOC:], row[K_LOC:], weights_t[K_LOC:], told], axis=0)
    of_local = jnp.concatenate([block[:K_LOC], gap, row[:K_LOC], gap, weights_t[:K_LOC], gap], axis=0)
    codes = jnp.concatenate([of_remote, of_local], axis=0)
    forward = [[(i, (i + k) % NX) for i in range(NX)] for k in range(NX)]
    codes = lax.all_gather(lax.all_gather(codes, "x1", axis=0), "x0", axis=0)
    remote_codes, local_codes = vmem_call(
        split_kernel, "split", [], [codes], [((NX, TOLD, T), BF16), ((2, 2, 48, T), BF16)],
        scratch=[pltpu.SemaphoreType.DMA((2,))], outside=1, bytes_accessed=100_000,
    )
    remote_codes = lax.all_gather(remote_codes, Y + ("c",), axis=0)
    blocks, remote_codes = lax.optimization_barrier((blocks, remote_codes))
    told = remote_codes[:, :, 12].astype(jnp.int32)
    sources = jnp.arange(GROUPS, dtype=jnp.int32)[:, None, None]

    def of_source(group):
        here = jnp.sum(jnp.where(sources == group, told, 0), axis=0)
        return here, jnp.sum(jnp.where(sources < group, told[:, :, :GROUPS], 0), axis=0)

    core = c[None]
    others = lax.ppermute(blocks, "c", swap)
    (part,) = vmem_call(
        first_kernel, "own_group", [core, *of_source(y * NC + c)], [blocks, remote_codes], [((NX, NY, T, T), F32)],
        flops=300_000_000, bytes_accessed=3_500_000,
    )
    (chip_sum,) = vmem_call(
        second_kernel, "other_group", [core, *of_source(y * NC + 1 - c)], [others, remote_codes, part], [((NY, NX, T, T), BF16)],
        scratch=[pltpu.VMEM((NY, NX, T, T), BF16), pltpu.SemaphoreType.DMA((NY,))], outside=1,
        flops=300_000_000, bytes_accessed=5_500_000,
    )
    arrived = lax.all_to_all(chip_sum.reshape(NX * NY, T, T), Y + X, 0, 0, tiled=True)

    features_later, _ = lax.optimization_barrier((features, chip_sum))
    near = []
    for k in (2, 1, 3, 0):
        (sums,) = vmem_call(
            functools.partial(local_kernel, k, k == 0), "local_sums", [jnp.stack([z, x])], [blocks, local_codes],
            [((T, T), F32)],
            scratch=[pltpu.VMEM((4 * T, T), BF16)] + ([] if k else [pltpu.VMEM((T, T), F32), pltpu.SemaphoreType.DMA]),
            outside=int(k == 0), flops=150_000_000, bytes_accessed=1_200_000,
        )
        near.append(lax.ppermute(sums, X, forward[NX - k]) if k else sums)
    two, three, one, near_0 = near

    share = width // OWNERS
    operands = ((2 * NX, T, T), BF16)
    (from_self,) = vmem_call(
        self_kernel, "from_self", [], [features_later, w_self], [((T, width), F32)],
        scratch=[pltpu.VMEM((T, width), F32), pltpu.SemaphoreType.DMA], outside=1, flops=67_000_000, bytes_accessed=900_000,
    )
    arrived, x, c = lax.optimization_barrier((arrived, x, c))
    outside = [near_0, weights_t, from_self, features_t]
    preact, send, keep = vmem_call(
        dense_kernel, "dense", [jnp.stack([x, c])], [arrived.reshape(NY, NX, T, T), one, two, three, w_agg, cotangent],
        [((T, width), F32), operands, operands],
        scratch=[pltpu.VMEM((width, T), F32)]
        + [pltpu.VMEM(of.shape, of.dtype) for of in outside]
        + [pltpu.SemaphoreType.DMA((len(outside),))],
        anywhere=[pltpu.with_memory_space_constraint(of, pltpu.HBM) for of in outside],
        flops=150_000_000, bytes_accessed=3_500_000, transcendentals=65536,
    )
    received = lax.ppermute(send, "c", swap)
    (hidden,) = vmem_call(hidden_kernel, "hidden", [], [preact], [((T, width), BF16)], flops=1_000_000, bytes_accessed=400_000, transcendentals=65536)
    received, hidden = lax.optimization_barrier((received, hidden))
    (chip_grad,) = vmem_call(
        grad_kernel, "gradient", [], [keep, received], [((OWNERS, share, width), BF16)], flops=300_000_000, bytes_accessed=1_000_000
    )
    planes = added(lax.all_to_all(chip_grad, X + ("z",), 0, 0, tiled=True), BF16, (NY,))
    planes = lax.all_to_all(planes, Y[::-1], 0, 0, tiled=True)
    grads = lax.all_gather(added(planes, F32), "c", axis=0)
    return hidden, grads[0], grads[1]


def solution(mesh):
    axes = ("z",) + X + Y + ("c",)
    fine = Mesh(mesh.devices.reshape(NZ, 2, 2, 2, 2, 2, NC), axes)
    row, rep = ("z",) + X, Y + ("c",)
    nodes = P(row + rep, None)
    in_specs = (nodes, nodes, nodes, P(row, rep, None, None), P(row, rep, None), P(), P(), nodes)
    out_specs = (nodes, P(row, None), P(row, None))
    return jax.shard_map(body, mesh=fine, in_specs=in_specs, out_specs=out_specs, check_vma=False)
```
